512 devices in a mesh: patch: 128 (over y, z, core), pair: 4 (over x).
Axes of the slice: x: 4, y: 8, z: 8, core: 2. Of those that a mesh axis runs over, the one named last changes fastest.
Arguments:
- right_side: float32 [262144], P('patch'), may hold values from -8 to 8
- coords: float32 [3, 262144], P(None, 'patch'), as said below
- diagonal: float32 [262144], P('patch'), may hold values from 1 to 2
- near_pairs: int32 [2, 8192], P(None, ('patch', 'pair')), may hold values from 0 to 1023, as said below
- far_pairs: int32 [2, 16384], P(None, ('patch', 'pair')), may hold values from 0 to 1023, as said below
- far_rank: int32 [16384], P(('patch', 'pair')), may hold values from 1 to 32, as said below
- far_left: bfloat16 [16384, 32, 256], P(('patch', 'pair')), may hold values from -0.375 to 0.375
- far_right: bfloat16 [16384, 32, 256], P(('patch', 'pair')), may hold values from -0.375 to 0.375
- far_scale: float32 [16384, 32], P(('patch', 'pair')), may hold values from 0.02 to 0.3
Outputs:
- solution: float32 [262144], P('patch')
- residual_norm: float32 [], replicated
The draws below stay inside these ranges and needn't reach their ends.
Inputs may be any that keep to these rules, and one draw needn't show every extreme that they name: Column k of near_pairs belongs to patch group g = k // 64; its target block lies among blocks g*8 to (g+1)*8 - 1, its source differs from the target by 1 to 4 blocks, and 4 is reached on every device. Column k of far_pairs belongs to patch group g = k // 128; its target block lies among that group's blocks, its source lies more than 4 blocks from the target, anywhere else. `far_rank`: every device holds a far pair of rank 32. `coords`: panel centres of block b lie within distance 2 in each component of (b / 2, 0.3 sin(0.7 b), 0).
All inputs are finite; a program needn't handle non-finite values.
Results may differ from the reference program's by a relative error of at most 0.0003.
Values sent between devices are 32-bit elements; how exact they have to be, the bound alone decides.
A program may use at most 64 MiB of HBM per device.

```python
import math
import jax
import jax.numpy as jnp
from jax import lax

BS = 256
RMAX = 32
ITERS = 2
BLK_DEV = 8
NEAR_DEV = 16
FAR_DEV = 32
RIM = 4
NB = 1024
PANELS = 262144
NEAR = 8192
FAR = 16384
N_PAIR = 4


def draw_coords(key, part):
    key = jax.random.fold_in(key, 11)
    block = (jnp.arange(PANELS, dtype=jnp.int32) // BS).astype(jnp.float32)
    jitter = jax.random.uniform(key, (3, PANELS), jnp.float32, -1.0, 1.0)
    first = 0.5 * block + jitter[0]
    second = 0.3 * jnp.sin(0.7 * block) + jitter[1]
    third = jitter[2]
    return jnp.stack([first, second, third]).astype(jnp.float32)


def draw_near_pairs(key, part):
    key = jax.random.fold_in(key, 23)
    key_a, key_b, key_c = jax.random.split(key, 3)
    row = jnp.arange(NEAR, dtype=jnp.int32)
    group = row // (N_PAIR * NEAR_DEV)
    target = group * BLK_DEV + jax.random.randint(key_a, (NEAR,), 0, BLK_DEV)
    reach = jax.random.randint(key_b, (NEAR,), 1, RIM + 1)
    reach = jnp.where(row % NEAR_DEV == 0, RIM, reach)
    sign = 2 * jax.random.randint(key_c, (NEAR,), 0, 2) - 1
    source = target + sign * reach
    source = jnp.where((source < 0) | (source >= NB), target - sign * reach, source)
    return jnp.stack([source, target]).astype(jnp.int32)


def draw_far_pairs(key, part):
    key = jax.random.fold_in(key, 37)
    key_a, key_b = jax.random.split(key)
    row = jnp.arange(FAR, dtype=jnp.int32)
    group = row // (N_PAIR * FAR_DEV)
    target = group * BLK_DEV + jax.random.randint(key_a, (FAR,), 0, BLK_DEV)
    offset = jax.random.randint(key_b, (FAR,), 0, NB - 2 * RIM - 1)
    source = (target + RIM + 1 + offset) % NB
    return jnp.stack([source, target]).astype(jnp.int32)


def draw_far_rank(key, part):
    key = jax.random.fold_in(key, 41)
    row = jnp.arange(FAR, dtype=jnp.int32)
    ranks = jax.random.randint(key, (FAR,), 1, RMAX + 1)
    return jnp.where(row % FAR_DEV == 0, RMAX, ranks).astype(jnp.int32)


def block_levels(own_key, dims, shards, smallest, largest):
    gain, own = 1.0, jax.random.fold_in(own_key, 6)
    for axis_at, shards_of in shards:
        steps = jnp.exp(jax.random.uniform(jax.random.fold_in(own, axis_at), (shards_of,), jnp.float32, smallest / len(shards), largest / len(shards)))
        gain = gain * jnp.repeat(steps, dims[axis_at] // shards_of).reshape([-1 if axis == axis_at else 1 for axis in range(len(dims))])
    return gain


def gaussian(stream_key, dims, spread, limit, cuts=(), kind=jnp.bfloat16):
    level = block_levels(stream_key, dims, cuts, -0.22, 0.18) if cuts else 1.0
    entries = jax.random.normal(stream_key, dims, jnp.float32) * spread * level
    return jnp.minimum(jnp.maximum(entries, -limit), limit).astype(kind)


def setup_inputs(seed: int = 0) -> dict:
    arg_keys = jax.random.split(jax.random.key(seed), 10)
    right_side = gaussian(arg_keys[0], (PANELS,), 1.0, 8.0, ((0, 128),), jnp.float32)
    coords = draw_coords(jax.random.fold_in(arg_keys[9], 71), 0)
    diagonal = jnp.clip(1.0 + 1.0 * jax.random.uniform(arg_keys[2], (PANELS,), jnp.float32) ** block_levels(arg_keys[2], (PANELS,), ((0, 128),), -0.2, 0.2), 1.0, 2.0)
    near_pairs = draw_near_pairs(jax.random.fold_in(arg_keys[9], 71), 0)
    far_pairs = draw_far_pairs(jax.random.fold_in(arg_keys[9], 71), 0)
    far_rank = draw_far_rank(jax.random.fold_in(arg_keys[9], 71), 0)
    far_left = gaussian(arg_keys[6], (FAR, RMAX, BS), BS ** -0.5, 0.375, ((0, 512),))
    far_right = gaussian(arg_keys[7], (FAR, RMAX, BS), BS ** -0.5, 0.375, ((0, 512),))
    far_scale = jnp.clip(jnp.exp(math.log(0.3) - 2.7080503 * jax.random.uniform(arg_keys[8], (FAR, RMAX), jnp.float32) ** block_levels(arg_keys[8], (FAR, RMAX), ((0, 512),), -0.2, 0.2)), 0.02, 0.3)
    return {"right_side": right_side, "coords": coords, "diagonal": diagonal, "near_pairs": near_pairs, "far_pairs": far_pairs, "far_rank": far_rank, "far_left": far_left, "far_right": far_right, "far_scale": far_scale}


NEAR_GAIN = 2.0
SOFT_SQ = 0.25
HIGH = lax.Precision.HIGHEST

def tile_from(source_coords, target_coords):
    diff_a = target_coords[0][:, :, None] - source_coords[0][:, None, :]
    diff_b = target_coords[1][:, :, None] - source_coords[1][:, None, :]
    diff_c = target_coords[2][:, :, None] - source_coords[2][:, None, :]
    dist = diff_a * diff_a + diff_b * diff_b + diff_c * diff_c
    return NEAR_GAIN / (BS * jnp.sqrt(dist + SOFT_SQ))

def apply_operator(charges, coords, diagonal, near_pairs, far_pairs, far_rank, far_left, far_right, far_scale):
    blocks = charges.reshape(NB, BS)
    coord_blocks = coords.reshape(3, NB, BS)

    def near_step(total, pairs):
        source = pairs[0]
        target = pairs[1]
        tile = tile_from(coord_blocks[:, source], coord_blocks[:, target])
        to_target = jnp.einsum('pij,pj->pi', tile, blocks[source], precision=HIGH)
        to_source = jnp.einsum('pij,pi->pj', tile, blocks[target], precision=HIGH)
        total = total.at[target].add(to_target).at[source].add(to_source)
        return (total, None)
    near_groups = near_pairs.reshape(2, NEAR // 8, 8).transpose(1, 0, 2)
    total, _ = lax.scan(near_step, jnp.zeros((NB, BS), jnp.float32), near_groups)

    def far_step(total, items):
        pairs, ranks, left_bf, right_bf, scales = items
        source = pairs[0]
        target = pairs[1]
        columns = jnp.arange(RMAX, dtype=jnp.int32)
        weights = scales * (columns[None, :] < ranks[:, None]).astype(jnp.float32)
        left = left_bf.astype(jnp.float32)
        right = right_bf.astype(jnp.float32)
        coef_t = weights * jnp.einsum('prb,pb->pr', right, blocks[source], precision=HIGH)
        coef_s = weights * jnp.einsum('prb,pb->pr', left, blocks[target], precision=HIGH)
        to_target = jnp.einsum('prb,pr->pb', left, coef_t, precision=HIGH)
        to_source = jnp.einsum('prb,pr->pb', right, coef_s, precision=HIGH)
        total = total.at[target].add(to_target).at[source].add(to_source)
        return (total, None)
    groups = FAR // FAR_DEV
    items = (far_pairs.reshape(2, groups, FAR_DEV).transpose(1, 0, 2), far_rank.reshape(groups, FAR_DEV), far_left.reshape(groups, FAR_DEV, RMAX, BS), far_right.reshape(groups, FAR_DEV, RMAX, BS), far_scale.reshape(groups, FAR_DEV, RMAX))
    total, _ = lax.scan(far_step, total, items)
    return diagonal * charges + total.reshape(-1)

def reference(right_side, coords, diagonal, near_pairs, far_pairs, far_rank, far_left, far_right, far_scale):
    beta = jnp.sqrt(jnp.sum(right_side * right_side))
    basis = [right_side / beta]
    columns = []
    for j in range(ITERS):
        work = apply_operator(basis[j], coords, diagonal, near_pairs, far_pairs, far_rank, far_left, far_right, far_scale)
        heights = [jnp.sum(basis[i] * work) for i in range(j + 1)]
        for i in range(j + 1):
            work = work - heights[i] * basis[i]
        below = jnp.sqrt(jnp.sum(work * work))
        basis.append(work / below)
        columns.append(heights + [below])
    return finish(beta, basis, columns)

def finish(beta, basis, columns):
    rotations = []
    target = [beta] + [jnp.float32(0.0) for _ in range(ITERS)]
    upper = []
    for j in range(ITERS):
        column = list(columns[j])
        for i in range(j):
            cos_i, sin_i = rotations[i]
            first = cos_i * column[i] + sin_i * column[i + 1]
            second = -sin_i * column[i] + cos_i * column[i + 1]
            column[i] = first
            column[i + 1] = second
        radius = jnp.sqrt(column[j] * column[j] + column[j + 1] * column[j + 1])
        cos_j = column[j] / radius
        sin_j = column[j + 1] / radius
        column[j] = radius
        rotations.append((cos_j, sin_j))
        target[j + 1] = -sin_j * target[j]
        target[j] = cos_j * target[j]
        upper.append(column[:j + 1])
    coeffs = [jnp.float32(0.0) for _ in range(ITERS)]
    for j in range(ITERS - 1, -1, -1):
        value = target[j]
        for k in range(j + 1, ITERS):
            value = value - upper[k][j] * coeffs[k]
        coeffs[j] = value / upper[j][j]
    solution = coeffs[0] * basis[0]
    for j in range(1, ITERS):
        solution = solution + coeffs[j] * basis[j]
    return (solution, jnp.abs(target[ITERS]))
```

```python
import functools

import jax
import jax.numpy as jnp
from jax import lax
from jax.experimental import pallas as pl
from jax.experimental.pallas import tpu as pltpu
from jax.sharding import PartitionSpec as P

BS = 256
BLK_DEV = 8
RIM = 4
RMAX = 32
NEAR_DEV = 16
FAR_DEV = 32
NEAR_GAIN = 2.0
SOFT_SQ = 0.25

N_Y, N_Z, N_X = 8, 8, 4
N_YZ = N_Y * N_Z
ROWS = 4 * N_YZ
SLOTS = BLK_DEV + 2 * RIM
FACT = FAR_DEV * RMAX
KEY = 80

MESH = pl.DeviceIdType.MESH
HIGH = lax.Precision.HIGHEST
F32 = jnp.float32
BF16 = jnp.bfloat16


def place():
    patch = lax.axis_index("patch")
    return lax.axis_index("pair"), patch // (2 * N_Z), (patch // 2) % N_Z, patch % 2


def device(x, y, z, core):
    return {"patch": (y * N_Z + z) * 2 + core, "pair": x}


def send(src, dst, send_sem, recv_sem, to):
    return pltpu.make_async_remote_copy(
        src_ref=src, dst_ref=dst, send_sem=send_sem, recv_sem=recv_sem, device_id=to, device_id_type=MESH
    )


def plane_peer(i, x, y, z, core):
    return device(x, (y + i // N_Z) % N_Y, (z + i % N_Z) % N_Z, core)


def split(value):
    high = value.astype(BF16)
    low = (value - high.astype(F32)).astype(BF16)
    return jnp.concatenate([high, low], axis=0)


def dot(a, b):
    return jnp.dot(a, b, preferred_element_type=F32)


def dot_rows(a, b):
    return lax.dot_general(a, b, (((1,), (1,)), ((), ())), preferred_element_type=F32)


def total(value):
    return jnp.sum(jnp.sum(value, axis=0, keepdims=True), axis=1, keepdims=True)


def kernel(
    near_smem, far_smem, right_ref, coords_ref, diag_ref, near_ref, far_ref, rank_ref, scale_ref,
    left_hbm, right_hbm,
    out_ref, norm_ref,
    left, right, hc, hct, cbc, tiles, hot, weight_d, hit_t,
    gath_a, gath_b, spread_a, spread_b, core_a, core_b, xs_a, xs_b, yz_a, yz_b,
    rows_v, rows_t, rows_y, own, diag, sums_yz, sums_x, sums_c,
    local_sem, halo_sem, gather_sem, scatter_sem, sums_sem,
):
    x, y, z, core = place()
    patch = lax.axis_index("patch")
    n_patch = 2 * N_YZ
    first = patch * BLK_DEV
    yz = y * N_Z + z
    mine = pl.ds(pl.multiple_of(yz * 4, 4), 4)
    up = {"patch": (patch + 1) % n_patch}
    down = {"patch": (patch + n_patch - 1) % n_patch}
    x_peers = [device((x + i) % N_X, y, z, core) for i in range(1, N_X)]
    twin = device(x, y, z, 1 - core)

    barrier = pltpu.get_barrier_semaphore()

    def greet(i, _):
        pl.semaphore_signal(barrier, inc=1, device_id=plane_peer(i, x, y, z, core), device_id_type=MESH)
        return 0

    lax.fori_loop(1, N_YZ, greet, 0)
    for to in x_peers + [twin, up, down]:
        pl.semaphore_signal(barrier, inc=1, device_id=to, device_id_type=MESH)

    load_left = pltpu.make_async_copy(left_hbm, left, local_sem.at[0])
    load_right = pltpu.make_async_copy(right_hbm, right, local_sem.at[1])
    load_left.start()
    load_right.start()

    start = 8 * (x // 2) + x % 2
    for i in range(4):
        gath_a[core, x, pl.ds(yz * 4 + i, 1), :] = right_ref[pl.ds(start + 2 * i, 1), :]
        diag[pl.ds(i, 1), :] = diag_ref[pl.ds(start + 2 * i, 1), :]
    for d in range(3):
        for b in range(BLK_DEV):
            hc[d, RIM + b : RIM + b + 1, :] = coords_ref[d : d + 1, b * BS : (b + 1) * BS]

    pl.semaphore_wait(barrier, N_YZ - 1 + N_X - 1 + 1 + 2)

    halo_up = send(hc.at[:, pl.ds(BLK_DEV, RIM)], hc.at[:, pl.ds(0, RIM)], halo_sem.at[0], halo_sem.at[1], up)
    halo_down = send(
        hc.at[:, pl.ds(RIM, RIM)], hc.at[:, pl.ds(RIM + BLK_DEV, RIM)], halo_sem.at[2], halo_sem.at[3], down
    )
    halo_up.start()
    halo_down.start()

    def wait_rows(ref, sem, n, sent):
        view = ref.at[core, x, pl.ds(0, n)]
        copy = send(view, view, sem, sem, twin)
        if sent:
            copy.wait_send()
        else:
            copy.wait_recv()

    def gather_start(ref, sems):
        own_rows = ref.at[core, x, mine]

        def step(i, _):
            send(own_rows, own_rows, sems.at[0], sems.at[1], plane_peer(i, x, y, z, core)).start()
            return 0

        lax.fori_loop(1, N_YZ, step, 0)

    def gather_middle(ref, sems):
        wait_rows(ref, sems.at[1], ROWS - 4, False)
        for i in range(1, N_X):
            send(ref.at[core, x], ref.at[core, x], sems.at[2], sems.at[2 + i], x_peers[i - 1]).start()

    def gather_end(ref, sems):
        for i in range(1, N_X):
            view = ref.at[core, (x + N_X - i) % N_X]
            send(view, view, sems.at[2], sems.at[2 + i], twin).wait_recv()
        send(ref.at[core], ref.at[core], sems.at[6], sems.at[7], twin).start()
        theirs = ref.at[1 - core]
        copy = send(theirs, theirs, sems.at[6], sems.at[7], twin)
        copy.wait_recv()
        copy.wait_send()
        wait_rows(ref, sems.at[0], ROWS - 4, True)
        for _ in range(1, N_X):
            wait_rows(ref, sems.at[2], ROWS, True)

    gather_start(gath_a, gather_sem.at[0])

    near_f = near_ref[...].astype(F32)
    far_f = far_ref[...].astype(F32)
    lane = lax.broadcasted_iota(jnp.int32, (1, 2 * KEY), 1) % KEY

    def lay(row, count, at):
        pick = lax.broadcasted_iota(jnp.int32, (count, 2 * KEY), 1) % KEY == (
            lax.broadcasted_iota(jnp.int32, (count, 2 * KEY), 0) + at
        )
        return jnp.dot(row, pick.astype(F32), precision=HIGH, preferred_element_type=F32)

    key = lay(near_f, NEAR_DEV, 0)[1:2] + lay(near_f, NEAR_DEV, NEAR_DEV)[0:1]
    key = key + lay(far_f, FAR_DEV, 2 * NEAR_DEV)[0:1]
    key = (key + 0.5).astype(jnp.int32)
    at_own = 2 * NEAR_DEV + FAR_DEV
    key = jnp.where(lane >= at_own, jnp.where(lane < at_own + BLK_DEV, first + lane - at_own, -1), key)
    row = lax.broadcasted_iota(jnp.int32, (ROWS, 2 * KEY), 0)
    for c in range(2):
        for a in range(2):
            block = (row // 4) * 16 + c * 8 + a * 4 + row % 4
            hot[c, a] = (block == key).astype(F32).astype(BF16)

    pair_of = lax.broadcasted_iota(jnp.int32, (FAR_DEV, FACT), 1) // RMAX
    term_of = lax.broadcasted_iota(jnp.int32, (FAR_DEV, FACT), 1) % RMAX
    sub = lax.broadcasted_iota(jnp.int32, (FAR_DEV, FACT), 0)
    eye = lax.broadcasted_iota(jnp.int32, (FAR_DEV, FAR_DEV), 0) == lax.broadcasted_iota(
        jnp.int32, (FAR_DEV, FAR_DEV), 1
    )
    rank_col = jnp.sum(jnp.where(eye, rank_ref[...].astype(F32), 0.0), axis=1, keepdims=True)
    term = lax.broadcasted_iota(jnp.int32, (FAR_DEV, RMAX), 1).astype(F32)
    weights = jnp.where(term < rank_col, scale_ref[...], 0.0)
    spread_w = jnp.dot(weights, (sub == term_of).astype(F32), precision=HIGH, preferred_element_type=F32)
    weight_d[...] = jnp.where(sub == pair_of, spread_w, 0.0)
    target_row = far_ref[1:2, :] - first
    onto = (lax.broadcasted_iota(jnp.int32, (BLK_DEV, FAR_DEV), 0) == target_row).astype(F32)
    hit_t[...] = jnp.dot(onto, (sub == pair_of).astype(F32), preferred_element_type=F32)

    halo_up.wait_recv()
    halo_down.wait_recv()
    for d in range(3):
        hct[pl.ds(SLOTS * d, SLOTS), :] = hc[d]
    turned = hct[...].T
    for b in range(SLOTS):
        for d in range(3):
            at = SLOTS * d + b
            cbc[b, d] = jnp.broadcast_to(turned[:, at : at + 1], (BS, 128))

    def build(k, _):
        source = jnp.clip(near_smem[0, k] - first + RIM, 0, SLOTS - 1)
        target = jnp.clip(near_smem[1, k] - first + RIM, 0, SLOTS - 1)
        for way, (across, along) in enumerate(((source, target), (target, source))):
            line = [hc[d, pl.ds(along, 1), :] for d in range(3)]
            for r in range(0, BS, 64):
                col = [cbc[across, d, r : r + 64, :] for d in range(3)]
                for h in range(2):
                    dist = SOFT_SQ
                    for d in range(3):
                        diff = col[d] - line[d][:, 128 * h : 128 * h + 128]
                        dist = dist + diff * diff
                    tile = (NEAR_GAIN / BS) * lax.rsqrt(dist)
                    high = tile.astype(BF16)
                    tiles[k, way, 0, r : r + 64, 128 * h : 128 * h + 128] = high
                    tiles[k, way, 1, r : r + 64, 128 * h : 128 * h + 128] = (tile - high.astype(F32)).astype(BF16)
        return 0

    lax.fori_loop(0, NEAR_DEV // 2, build, 0)
    gather_middle(gath_a, gather_sem.at[0])
    lax.fori_loop(NEAR_DEV // 2, NEAR_DEV, build, 0)
    gather_end(gath_a, gather_sem.at[0])
    halo_up.wait_send()
    halo_down.wait_send()
    load_left.wait()
    load_right.wait()

    def fetch(ref, s):
        group = s // BLK_DEV
        b = s % BLK_DEV
        at = (group // 2) * 4 + b % 4
        return [ref[group % 2, 2 * (b // 4) + h, pl.ds(at, 1), :] for h in range(2)]

    def product(ref, spread):
        for k in range(NEAR_DEV):
            for h, part in enumerate(fetch(ref, near_smem[0, k])):
                rows_v[k : k + 1, 128 * h : 128 * h + 128] = part
            for h, part in enumerate(fetch(ref, near_smem[1, k])):
                rows_t[k : k + 1, 128 * h : 128 * h + 128] = part
        for k in range(FAR_DEV):
            for h, part in enumerate(fetch(ref, far_smem[0, k])):
                rows_v[NEAR_DEV + k : NEAR_DEV + k + 1, 128 * h : 128 * h + 128] = part
        for a in range(2):
            for h in range(2):
                own[4 * a : 4 * a + 4, 128 * h : 128 * h + 128] = ref[core, 2 * a + h, mine, :]

        far_v = split(rows_v[NEAR_DEV:, :])
        coef = dot_rows(far_v, right[...])
        coef = jnp.sum(weight_d[...] * (coef[:FAR_DEV] + coef[FAR_DEV:]), axis=0, keepdims=True)
        to_own = dot(split(hit_t[...] * coef), left[...])
        rows_y[at_own : at_own + BLK_DEV, :] = to_own[:BLK_DEV] + to_own[BLK_DEV:]
        rows_y[at_own + BLK_DEV :, :] = jnp.zeros((KEY - at_own - BLK_DEV, BS), F32)
        back = dot_rows(split(own[...]), left[...])
        back = jnp.sum(hit_t[...] * (back[:BLK_DEV] + back[BLK_DEV:]), axis=0, keepdims=True)
        to_far = dot(split(weight_d[...] * back), right[...])
        rows_y[2 * NEAR_DEV : at_own, :] = to_far[:FAR_DEV] + to_far[FAR_DEV:]

        near_v = split(rows_v[:NEAR_DEV, :])
        near_t = split(rows_t[...])
        for k in range(NEAR_DEV):
            for way, vectors in enumerate((near_v, near_t)):
                image = dot(vectors, tiles[k, way, 0]) + dot(vectors, tiles[k, way, 1])
                at = way * NEAR_DEV + k
                rows_y[at : at + 1, :] = image[k : k + 1] + image[NEAR_DEV + k : NEAR_DEV + k + 1]

        rows = split(rows_y[...])

        def lay_out(c):
            for a in range(2):
                image = dot(hot[c, a], rows)
                for h in range(2):
                    spread[c, 2 * a + h] = image[:, 128 * h : 128 * h + 128]

        return lay_out

    def scatter(lay_out, spread, core_buf, xs, yzs, sems):
        lay_out(1 - core)
        swap = send(spread.at[1 - core], core_buf, sems.at[0], sems.at[1], twin)
        swap.start()
        lay_out(core)
        swap.wait_recv()
        copies = []
        for i in range(1, N_X):
            q = (x + i) % N_X
            spread[core, q] = spread[core, q] + core_buf[q]
            copy = send(spread.at[core, q], xs.at[i - 1], sems.at[2], sems.at[2 + i], x_peers[i - 1])
            copy.start()
            copies.append(copy)
        spread[core, x] = spread[core, x] + core_buf[x]
        for copy in copies:
            copy.wait_recv()
        spread[core, x] = spread[core, x] + (xs[0] + (xs[1] + xs[2]))
        yzs[mine, :] = spread[core, x, mine, :]

        def step(i, _):
            there = ((y + i // N_Z) % N_Y) * N_Z + (z + i % N_Z) % N_Z
            rows = pl.ds(pl.multiple_of(there * 4, 4), 4)
            send(
                spread.at[core, x, rows], yzs.at[mine], sems.at[6], sems.at[7], plane_peer(i, x, y, z, core)
            ).start()
            return 0

        lax.fori_loop(1, N_YZ, step, 0)
        wait_rows(spread, sems.at[7], ROWS - 4, False)
        wait_rows(spread, sems.at[6], ROWS - 4, True)
        swap.wait_send()
        for copy in copies:
            copy.wait_send()
        image = jnp.sum(yzs[...].reshape(ROWS // 8, 8, 128), axis=0)
        return image[:4] + image[4:]

    def whole_dot(a_ref, b_ref):
        acc = jnp.zeros((8, 128), F32)
        for c in range(2):
            for q in range(4):
                acc = acc + jnp.sum((a_ref[c, q] * b_ref[c, q]).reshape(ROWS // 8, 8, 128), axis=0)
        return total(acc)

    lay_out = product(gath_a, spread_a)
    beta = jnp.sqrt(whole_dot(gath_a, gath_a))
    inv_beta = 1.0 / beta
    image = scatter(lay_out, spread_a, core_a, xs_a, yz_a, scatter_sem.at[0])
    b_mine = gath_a[core, x, mine, :]
    gath_b[core, x, mine, :] = (image + diag[...] * b_mine) * inv_beta

    gather_start(gath_b, gather_sem.at[1])
    gather_middle(gath_b, gather_sem.at[1])
    gather_end(gath_b, gather_sem.at[1])

    h00 = whole_dot(gath_a, gath_b) * inv_beta
    alpha = h00 * inv_beta
    for c in range(2):
        for q in range(4):
            gath_b[c, q] = gath_b[c, q] - alpha * gath_a[c, q]
    h10 = jnp.sqrt(whole_dot(gath_b, gath_b))
    inv_h10 = 1.0 / h10

    lay_out = product(gath_b, spread_b)
    image = scatter(lay_out, spread_b, core_b, xs_b, yz_b, scatter_sem.at[1])
    v0 = b_mine * inv_beta
    w_mine = gath_b[core, x, mine, :]
    v1 = w_mine * inv_h10
    rest = (image + diag[...] * w_mine) * inv_h10 - h10 * v0 - h00 * v1

    def fold(value):
        return jnp.sum(value, axis=0, keepdims=True)

    sums_yz[mine, :] = jnp.concatenate(
        [fold(rest * rest), fold(rest * v0), fold(rest * v1), jnp.zeros((1, 128), F32)], axis=0
    )

    def tell(i, _):
        send(
            sums_yz.at[mine], sums_yz.at[mine], sums_sem.at[0], sums_sem.at[1], plane_peer(i, x, y, z, core)
        ).start()
        return 0

    lax.fori_loop(1, N_YZ, tell, 0)
    most = sums_yz.at[pl.ds(0, ROWS - 4)]
    copy = send(most, most, sums_sem.at[0], sums_sem.at[1], twin)
    copy.wait_recv()
    copy.wait_send()
    acc = jnp.sum(sums_yz[...].reshape(ROWS // 8, 8, 128), axis=0)
    sums_x[x] = acc
    copies = []
    for i in range(1, N_X):
        copy = send(sums_x.at[x], sums_x.at[x], sums_sem.at[2], sums_sem.at[2 + i], x_peers[i - 1])
        copy.start()
        copies.append(copy)
    for i in range(1, N_X):
        view = sums_x.at[(x + N_X - i) % N_X]
        send(view, view, sums_sem.at[2], sums_sem.at[2 + i], twin).wait_recv()
    for copy in copies:
        copy.wait_send()
    sums_c[0] = (sums_x[0] + sums_x[1]) + (sums_x[2] + sums_x[3])
    copy = send(sums_c.at[0], sums_c.at[1], sums_sem.at[6], sums_sem.at[7], twin)
    copy.start()
    copy.wait()
    acc = sums_c[0] + sums_c[1]
    acc = jnp.sum(acc[:4] + acc[4:], axis=1, keepdims=True)
    sq, a0, a1 = acc[0:1], acc[1:2], acc[2:3]
    h01 = h10 + a0
    h11 = h00 + a1
    h21 = jnp.sqrt(jnp.maximum(sq - a0 * a0 - a1 * a1, 0.0))

    rho0 = jnp.sqrt(h00 * h00 + h10 * h10)
    c0 = h00 / rho0
    s0 = h10 / rho0
    r01 = c0 * h01 + s0 * h11
    r11 = c0 * h11 - s0 * h01
    rho1 = jnp.sqrt(r11 * r11 + h21 * h21)
    c1 = r11 / rho1
    s1 = h21 / rho1
    g0 = c0 * beta
    g1 = -s0 * beta
    y1 = c1 * g1 / rho1
    y0 = (g0 - r01 * y1) / rho0
    norm_ref[...] = jnp.broadcast_to(jnp.abs(s1 * g1), (8, 128))
    f0 = y0 * inv_beta
    f1 = y1 * inv_h10
    for a in range(2):
        for h in range(2):
            part = f0 * gath_a[core, 2 * a + h, mine, :] + f1 * gath_b[core, 2 * a + h, mine, :]
            for i in range(4):
                at = 8 * a + 2 * i + h
                out_ref[at : at + 1, :] = part[i : i + 1]


def body(
    right_side, coords, diagonal, near_pairs, far_pairs, far_rank, far_left, far_right, far_scale
):
    vmem = pl.BlockSpec(memory_space=pltpu.VMEM)
    smem = pl.BlockSpec(memory_space=pltpu.SMEM)
    hbm = pl.BlockSpec(memory_space=pl.ANY)
    scratch = [
        pltpu.VMEM((FACT, BS), BF16),
        pltpu.VMEM((FACT, BS), BF16),
        pltpu.VMEM((3, SLOTS, BS), F32),
        pltpu.VMEM((3 * SLOTS, BS), F32),
        pltpu.VMEM((SLOTS, 3, BS, 128), F32),
        pltpu.VMEM((NEAR_DEV, 2, 2, BS, BS), BF16),
        pltpu.VMEM((2, 2, ROWS, 2 * KEY), BF16),
        pltpu.VMEM((FAR_DEV, FACT), F32),
        pltpu.VMEM((BLK_DEV, FACT), F32),
        pltpu.VMEM((2, 4, ROWS, 128), F32),
        pltpu.VMEM((2, 4, ROWS, 128), F32),
        pltpu.VMEM((2, 4, ROWS, 128), F32),
        pltpu.VMEM((2, 4, ROWS, 128), F32),
        pltpu.VMEM((4, ROWS, 128), F32),
        pltpu.VMEM((4, ROWS, 128), F32),
        pltpu.VMEM((3, ROWS, 128), F32),
        pltpu.VMEM((3, ROWS, 128), F32),
        pltpu.VMEM((ROWS, 128), F32),
        pltpu.VMEM((ROWS, 128), F32),
        pltpu.VMEM((NEAR_DEV + FAR_DEV, BS), F32),
        pltpu.VMEM((NEAR_DEV, BS), F32),
        pltpu.VMEM((KEY, BS), F32),
        pltpu.VMEM((BLK_DEV, BS), F32),
        pltpu.VMEM((4, 128), F32),
        pltpu.VMEM((ROWS, 128), F32),
        pltpu.VMEM((4, 8, 128), F32),
        pltpu.VMEM((2, 8, 128), F32),
        pltpu.SemaphoreType.DMA((2,)),
        pltpu.SemaphoreType.DMA((4,)),
        pltpu.SemaphoreType.DMA((2, 8)),
        pltpu.SemaphoreType.DMA((2, 8)),
        pltpu.SemaphoreType.DMA((8,)),
    ]
    solution, norm = pl.pallas_call(
        kernel,
        out_shape=(
            jax.ShapeDtypeStruct((16, 128), F32),
            jax.ShapeDtypeStruct((8, 128), F32),
        ),
        in_specs=[smem, smem, vmem, vmem, vmem, vmem, vmem, vmem, vmem, hbm, hbm],
        out_specs=(vmem, vmem),
        scratch_shapes=scratch,
        compiler_params=pltpu.CompilerParams(
            collective_id=0, has_side_effects=True, vmem_limit_bytes=48 * 1024 * 1024
        ),
        cost_estimate=pl.CostEstimate(flops=100_000_000, bytes_accessed=2_000_000, transcendentals=2_000_000),
        name="gmres",
    )(
        near_pairs, far_pairs, right_side.reshape(16, 128), coords, diagonal.reshape(16, 128), near_pairs,
        far_pairs, far_rank.reshape(1, FAR_DEV), far_scale, far_left.reshape(FACT, BS),
        far_right.reshape(FACT, BS),
    )
    return solution.reshape(BLK_DEV * BS), norm[0, 0]


def solution(mesh):
    placed = (
        P("patch"),
        P(None, "patch"),
        P("patch"),
        P(None, ("patch", "pair")),
        P(None, ("patch", "pair")),
        P(("patch", "pair")),
        P(("patch", "pair"), None, None),
        P(("patch", "pair"), None, None),
        P(("patch", "pair"), None),
    )
    return jax.shard_map(
        body, mesh=mesh, in_specs=placed, out_specs=(P("patch"), P()), check_vma=False
    )
```

```python
import functools

import jax
import jax.numpy as jnp
from jax import lax
from jax.experimental import pallas as pl
from jax.experimental.pallas import tpu as pltpu
from jax.sharding import PartitionSpec as P

BS = 256
BLK_DEV = 8
RIM = 4
RMAX = 32
NEAR_DEV = 16
FAR_DEV = 32
NEAR_GAIN = 2.0
SOFT_SQ = 0.25

N_Y, N_Z, N_X = 8, 8, 4
N_YZ = N_Y * N_Z
ROWS = 4 * N_YZ
COLUMN = 2 * N_X
SLOTS = BLK_DEV + 2 * RIM
FACT = FAR_DEV * RMAX
EXTRA = 8

MESH = pl.DeviceIdType.MESH
HIGH = lax.Precision.HIGHEST
F32 = jnp.float32
BF16 = jnp.bfloat16


def place():
    patch = lax.axis_index("patch")
    return lax.axis_index("pair"), patch // (2 * N_Z), (patch // 2) % N_Z, patch % 2


def device(x, y, z, core):
    return {"patch": (y * N_Z + z) * 2 + core, "pair": x}


def send(src, dst, send_sem, recv_sem, to):
    return pltpu.make_async_remote_copy(
        src_ref=src, dst_ref=dst, send_sem=send_sem, recv_sem=recv_sem, device_id=to, device_id_type=MESH
    )


def plane_peer(i, x, y, z, core):
    return device(x, (y + i // N_Z) % N_Y, (z + i % N_Z) % N_Z, core)


def parts(value, count):
    found = []
    for _ in range(count):
        found.append(value.astype(BF16))
        value = value - found[-1].astype(F32)
    return found


def split(value):
    return jnp.concatenate(parts(value, 2), axis=0)


def dot(a, b):
    return jnp.dot(a, b, preferred_element_type=F32)


def dot_rows(a, b):
    return lax.dot_general(a, b, (((1,), (1,)), ((), ())), preferred_element_type=F32)


def fold(value):
    return jnp.sum(value, axis=0, keepdims=True)


def total(value):
    return jnp.sum(fold(value), axis=1, keepdims=True)


def kernel(
    near_smem, right_hbm, coords_hbm, diag_hbm, near_hbm, far_hbm, rank_hbm, scale_hbm, left_hbm, factor_hbm,
    out_ref, norm_ref,
    left, right, right_ref, coords_ref, diag_ref, near_ref, far_ref, rank_ref, scale_ref,
    hc, hct, cbc, tiles, keys, hot, hot_t, weight_d, hit_t,
    quarter, picked, got, given, taken, spread, landed, span, rim, joined,
    rows_n, sums_yz, sums_c,
    local_sem, once_sem, step_sem, sums_sem,
):
    x, y, z, core = place()
    patch = lax.axis_index("patch")
    n_patch = 2 * N_YZ
    first = patch * BLK_DEV
    yz = y * N_Z + z
    me = 2 * x + core
    mine = pl.ds(pl.multiple_of(yz * 4, 4), 4)
    up = {"patch": (patch + 1) % n_patch}
    down = {"patch": (patch + n_patch - 1) % n_patch}
    x_peers = [device((x + i) % N_X, y, z, core) for i in range(1, N_X)]
    twin = device(x, y, z, 1 - core)
    column = []
    for i in range(1, COLUMN):
        other_x, other_core = (x + i // 2) % N_X, (core + i) % 2
        column.append((2 * other_x + other_core, other_x % 2, device(other_x, y, z, other_core)))

    barrier = pltpu.get_barrier_semaphore()

    def greet(i, _):
        pl.semaphore_signal(barrier, inc=1, device_id=plane_peer(i, x, y, z, core), device_id_type=MESH)
        return 0

    loads = [
        pltpu.make_async_copy(src, dst, local_sem.at[i])
        for i, (src, dst) in enumerate(
            (
                (left_hbm, left), (factor_hbm, right), (right_hbm, right_ref), (coords_hbm, coords_ref),
                (diag_hbm, diag_ref), (near_hbm, near_ref), (far_hbm, far_ref), (rank_hbm, rank_ref),
                (scale_hbm, scale_ref),
            )
        )
    ]
    for load in loads:
        load.start()
    lax.fori_loop(1, N_YZ, greet, 0)
    for _, _, to in column:
        pl.semaphore_signal(barrier, inc=1, device_id=to, device_id_type=MESH)
    for to in (up, down):
        pl.semaphore_signal(barrier, inc=1, device_id=to, device_id_type=MESH)
    for load in loads:
        load.wait()

    def natural(ref):
        return jnp.concatenate([ref[pl.ds(h, BLK_DEV, stride=2), :] for h in range(2)], axis=1)

    def own_quarter(value):
        found = value[:4, :128]
        for q in range(1, N_X):
            a, h = q // 2, q % 2
            found = jnp.where(x == q, value[4 * a : 4 * a + 4, 128 * h : 128 * h + 128], found)
        return found

    b_own = natural(right_ref)
    diag = natural(diag_ref)
    span[0, RIM : RIM + BLK_DEV, :] = b_own
    quarter[0, mine, :] = own_quarter(b_own)
    for d in range(3):
        for b in range(BLK_DEV):
            hc[d, RIM + b : RIM + b + 1, :] = coords_ref[d : d + 1, b * BS : (b + 1) * BS]

    near_f = near_ref[...].astype(F32)
    far_f = far_ref[...].astype(F32)
    sub_key = lax.broadcasted_iota(jnp.int32, (FAR_DEV, COLUMN * FAR_DEV), 0)
    lane_key = lax.broadcasted_iota(jnp.int32, (FAR_DEV, COLUMN * FAR_DEV), 1)
    pick = (lane_key == sub_key + me * FAR_DEV).astype(F32)
    laid = jnp.dot(far_f, pick, precision=HIGH, preferred_element_type=F32)
    keys[me] = jnp.broadcast_to(laid[0:1], (8, COLUMN * FAR_DEV))

    pair_of = lax.broadcasted_iota(jnp.int32, (FAR_DEV, FACT), 1) // RMAX
    term_of = lax.broadcasted_iota(jnp.int32, (FAR_DEV, FACT), 1) % RMAX
    sub = lax.broadcasted_iota(jnp.int32, (FAR_DEV, FACT), 0)
    eye = lax.broadcasted_iota(jnp.int32, (FAR_DEV, FAR_DEV), 0) == lax.broadcasted_iota(
        jnp.int32, (FAR_DEV, FAR_DEV), 1
    )
    rank_col = jnp.sum(jnp.where(eye, rank_ref[...].astype(F32), 0.0), axis=1, keepdims=True)
    term = lax.broadcasted_iota(jnp.int32, (FAR_DEV, RMAX), 1).astype(F32)
    weights = jnp.where(term < rank_col, scale_ref[...], 0.0)
    spread_w = jnp.dot(weights, (sub == term_of).astype(F32), precision=HIGH, preferred_element_type=F32)
    weight_d[...] = jnp.where(sub == pair_of, spread_w, 0.0)
    target_row = far_ref[1:2, :] - first
    onto = (lax.broadcasted_iota(jnp.int32, (BLK_DEV, FAR_DEV), 0) == target_row).astype(F32)
    hit_t[...] = jnp.dot(onto, (sub == pair_of).astype(F32), preferred_element_type=F32)

    def wait_for(view, sem, sent):
        copy = send(view, view, sem, sem, twin)
        if sent:
            copy.wait_send()
        else:
            copy.wait_recv()

    def plane(step, sems):
        def each(i, _):
            src, dst = step(((y + i // N_Z) % N_Y) * N_Z + (z + i % N_Z) % N_Z)
            send(src, dst, sems[0], sems[1], plane_peer(i, x, y, z, core)).start()
            return 0

        lax.fori_loop(1, N_YZ, each, 0)

    def give(it, own_value):
        back = dot_rows(split(own_value), left[...])
        back = fold(hit_t[...] * (back[:BLK_DEV] + back[BLK_DEV:]))
        to_far = dot(split(weight_d[...] * back), right[...])
        to_far = to_far[:FAR_DEV] + to_far[FAR_DEV:]
        for h in range(2):
            given[it, h] = to_far[:, 128 * h : 128 * h + 128]
        taken[it, me] = given[it, x % 2]

    def give_start(it):
        for number, half, to in column:
            send(given.at[it, half], taken.at[it, me], step_sem.at[it, 0], step_sem.at[it, 1], to).start()

    def gather_start(it):
        own_rows = quarter.at[it, mine]
        plane(lambda there: (own_rows, own_rows), (step_sem.at[it, 2], step_sem.at[it, 3]))

    def span_start(it):
        send(
            span.at[it, pl.ds(BLK_DEV, RIM)], span.at[it, pl.ds(0, RIM)],
            step_sem.at[it, 4], step_sem.at[it, 5], up,
        ).start()
        send(
            span.at[it, pl.ds(RIM, RIM)], span.at[it, pl.ds(RIM + BLK_DEV, RIM)],
            step_sem.at[it, 6], step_sem.at[it, 7], down,
        ).start()

    def scatter_plane(it):
        wait_for(taken.at[it, pl.ds(0, COLUMN - 1)], step_sem.at[it, 1], False)
        value = 0.0
        for part in parts(taken[it].reshape(COLUMN * FAR_DEV, 128), 3):
            value = value + dot(hot[...], part)
        spread[it] = value
        landed[it, mine, :] = spread[it, mine, :]
        plane(
            lambda there: (spread.at[it, pl.ds(pl.multiple_of(there * 4, 4), 4)], landed.at[it, mine]),
            (step_sem.at[it, 8], step_sem.at[it, 9]),
        )

    def gather_column(it, extras):
        wait_for(quarter.at[it, pl.ds(0, ROWS - 4)], step_sem.at[it, 3], False)
        value = 0.0
        for part in parts(quarter[it], 3):
            value = value + dot(hot_t[...], part)
        picked[it, :, pl.ds(0, FAR_DEV), :] = value.reshape(COLUMN, FAR_DEV, 128)
        sums = [fold(quarter[i] * quarter[j]) for i, j in extras]
        sums = jnp.concatenate(sums + [jnp.zeros((EXTRA - len(sums), 128), F32)], axis=0)
        for g in range(COLUMN):
            picked[it, g, pl.ds(FAR_DEV, EXTRA), :] = sums
        got[it, me] = picked[it, me]
        for number, half, to in column:
            send(picked.at[it, number], got.at[it, me], step_sem.at[it, 10], step_sem.at[it, 11], to).start()

    def gather_end(it):
        wait_for(got.at[it, pl.ds(0, COLUMN - 1)], step_sem.at[it, 11], False)
        halves = []
        for h in range(2):
            at = 2 * h
            halves.append((got[it, at] + got[it, at + 1]) + (got[it, at + 4] + got[it, at + 5]))
        sums = jnp.sum(halves[0][FAR_DEV:] + halves[1][FAR_DEV:], axis=1, keepdims=True)
        far_v = split(jnp.concatenate([half[:FAR_DEV] for half in halves], axis=1))
        coef = dot_rows(far_v, right[...])
        coef = fold(weight_d[...] * (coef[:FAR_DEV] + coef[FAR_DEV:]))
        to_own = dot(split(hit_t[...] * coef), left[...])
        return to_own[:BLK_DEV] + to_own[BLK_DEV:], sums

    def near(it):
        wait_for(span.at[it, pl.ds(0, RIM)], step_sem.at[it, 5], False)
        wait_for(span.at[it, pl.ds(0, RIM)], step_sem.at[it, 7], False)
        vectors = []
        for way in range(2):
            rows = [
                span[it, pl.ds(jnp.clip(near_smem[way, k] - first + RIM, 0, SLOTS - 1), 1), :]
                for k in range(NEAR_DEV)
            ]
            vectors.append(split(jnp.concatenate(rows, axis=0)))
        for k in range(NEAR_DEV):
            for way in range(2):
                image = dot(vectors[way], tiles[k, way, 0]) + dot(vectors[way], tiles[k, way, 1])
                at = way * NEAR_DEV + k
                rows_n[at : at + 1, :] = image[k : k + 1] + image[NEAR_DEV + k : NEAR_DEV + k + 1]
        slot = lax.broadcasted_iota(jnp.int32, (SLOTS, NEAR_DEV), 0)
        hits = [(slot == near_ref[way : way + 1, :] - first + RIM).astype(F32) for way in (1, 0)]
        hits = jnp.concatenate(hits, axis=1).astype(BF16)
        value = 0.0
        for part in parts(rows_n[...], 3):
            value = value + dot(hits, part)
        rim[it, 0] = value
        send(
            rim.at[it, 0, pl.ds(0, RIM)], rim.at[it, 1, pl.ds(RIM, RIM)],
            step_sem.at[it, 12], step_sem.at[it, 13], down,
        ).start()
        send(
            rim.at[it, 0, pl.ds(RIM + BLK_DEV, RIM)], rim.at[it, 1, pl.ds(0, RIM)],
            step_sem.at[it, 14], step_sem.at[it, 15], up,
        ).start()

    def join(it, far_own):
        wait_for(rim.at[it, 1, pl.ds(0, RIM)], step_sem.at[it, 13], False)
        wait_for(rim.at[it, 1, pl.ds(0, RIM)], step_sem.at[it, 15], False)
        local = far_own + rim[it, 0, RIM : RIM + BLK_DEV, :] + rim[it, 1, 0:BLK_DEV, :]
        wait_for(landed.at[it, pl.ds(0, ROWS - 4)], step_sem.at[it, 9], False)
        image = jnp.sum(landed[it].reshape(ROWS // 8, 8, 128), axis=0)
        image = image[:4] + image[4:]
        image = jnp.concatenate([image, image], axis=0)
        image = jnp.concatenate([image, image], axis=1)
        at_row = lax.broadcasted_iota(jnp.int32, (BLK_DEV, BS), 0) // 4
        at_half = lax.broadcasted_iota(jnp.int32, (BLK_DEV, BS), 1) // 128
        joined[it, x] = local + jnp.where(2 * at_row + at_half == x, image, 0.0)
        for i in (2, 1, 3):
            send(
                joined.at[it, x], joined.at[it, x], step_sem.at[it, 16], step_sem.at[it, 16 + i], x_peers[i - 1]
            ).start()
        for i in range(1, N_X):
            wait_for(joined.at[it, (x + N_X - i) % N_X], step_sem.at[it, 16 + i], False)
        return (joined[it, 0] + joined[it, 1]) + (joined[it, 2] + joined[it, 3])

    def sent(it):
        wait_for(taken.at[it, pl.ds(0, COLUMN - 1)], step_sem.at[it, 0], True)
        wait_for(quarter.at[it, pl.ds(0, ROWS - 4)], step_sem.at[it, 2], True)
        wait_for(span.at[it, pl.ds(0, RIM)], step_sem.at[it, 4], True)
        wait_for(span.at[it, pl.ds(0, RIM)], step_sem.at[it, 6], True)
        wait_for(landed.at[it, pl.ds(0, ROWS - 4)], step_sem.at[it, 8], True)
        wait_for(got.at[it, pl.ds(0, COLUMN - 1)], step_sem.at[it, 10], True)
        wait_for(rim.at[it, 1, pl.ds(0, RIM)], step_sem.at[it, 12], True)
        wait_for(rim.at[it, 1, pl.ds(0, RIM)], step_sem.at[it, 14], True)
        wait_for(joined.at[it, pl.ds(0, N_X - 1)], step_sem.at[it, 16], True)

    def build(k, _):
        source = jnp.clip(near_smem[0, k] - first + RIM, 0, SLOTS - 1)
        target = jnp.clip(near_smem[1, k] - first + RIM, 0, SLOTS - 1)
        for way, (across, along) in enumerate(((source, target), (target, source))):
            line = [hc[d, pl.ds(along, 1), :] for d in range(3)]
            for r in range(0, BS, 64):
                col = [cbc[across, d, r : r + 64, :] for d in range(3)]
                for h in range(2):
                    dist = SOFT_SQ
                    for d in range(3):
                        diff = col[d] - line[d][:, 128 * h : 128 * h + 128]
                        dist = dist + diff * diff
                    tile = (NEAR_GAIN / BS) * lax.rsqrt(dist)
                    high = tile.astype(BF16)
                    tiles[k, way, 0, r : r + 64, 128 * h : 128 * h + 128] = high
                    tiles[k, way, 1, r : r + 64, 128 * h : 128 * h + 128] = (tile - high.astype(F32)).astype(BF16)
        return 0

    give(0, b_own)
    pl.semaphore_wait(barrier, N_YZ - 1 + COLUMN - 1 + 2)

    for number, half, to in column:
        send(keys.at[me], keys.at[me], once_sem.at[0], once_sem.at[1], to).start()
    give_start(0)
    halo_up = send(hc.at[:, pl.ds(BLK_DEV, RIM)], hc.at[:, pl.ds(0, RIM)], once_sem.at[2], once_sem.at[3], up)
    halo_down = send(
        hc.at[:, pl.ds(RIM, RIM)], hc.at[:, pl.ds(RIM + BLK_DEV, RIM)], once_sem.at[4], once_sem.at[5], down
    )
    halo_up.start()
    halo_down.start()
    gather_start(0)
    span_start(0)
    wait_for(keys.at[pl.ds(0, COLUMN - 1)], once_sem.at[1], False)
    key = keys[0]
    for g in range(1, COLUMN):
        key = key + keys[g]
    key = (key[0:1] + 0.5).astype(jnp.int32)
    row = lax.broadcasted_iota(jnp.int32, (ROWS, COLUMN * FAR_DEV), 0)
    block = (row // 4) * 16 + core * 8 + (x // 2) * 4 + row % 4
    hits = (block == key).astype(F32)
    hot[...] = hits.astype(BF16)
    hot_t[...] = hits.T.astype(BF16)
    scatter_plane(0)

    halo_up.wait_recv()
    halo_down.wait_recv()
    for d in range(3):
        hct[pl.ds(SLOTS * d, SLOTS), :] = hc[d]
    turned = hct[...].T
    for b in range(SLOTS):
        for d in range(3):
            at = SLOTS * d + b
            cbc[b, d] = jnp.broadcast_to(turned[:, at : at + 1], (BS, 128))
    lax.fori_loop(0, NEAR_DEV // 4, build, 0)
    gather_column(0, ((0, 0),))
    lax.fori_loop(NEAR_DEV // 4, NEAR_DEV, build, 0)
    near(0)
    far_own, sums = gather_end(0)
    beta = jnp.sqrt(sums[0:1])
    inv_beta = 1.0 / beta
    w_own = (join(0, far_own) + diag * b_own) * inv_beta

    span[1, RIM : RIM + BLK_DEV, :] = w_own
    quarter[1, mine, :] = own_quarter(w_own)
    give(1, w_own)
    give_start(1)
    span_start(1)
    gather_start(1)
    wait_for(keys.at[pl.ds(0, COLUMN - 1)], once_sem.at[0], True)
    halo_up.wait_send()
    halo_down.wait_send()
    sent(0)
    scatter_plane(1)
    near(1)
    gather_column(1, ((0, 1), (1, 1)))
    far_own, sums = gather_end(1)
    h00 = sums[0:1] * inv_beta
    shift = sums[1:2] - h00 * h00
    v0 = b_own * inv_beta
    u = w_own - h00 * v0
    rest = join(1, far_own) + diag * w_own - h00 * w_own - shift * v0 - h00 * u

    def lanes(value):
        value = fold(value)
        return value[:, :128] + value[:, 128:]

    sums_yz[mine, :] = jnp.concatenate(
        [lanes(rest * rest), lanes(rest * v0), lanes(rest * u), lanes(u * u)], axis=0
    )
    own_sums = sums_yz.at[mine]
    plane(lambda there: (own_sums, own_sums), (sums_sem.at[0], sums_sem.at[1]))
    sent(1)
    wait_for(sums_yz.at[pl.ds(0, ROWS - 4)], sums_sem.at[1], False)
    wait_for(sums_yz.at[pl.ds(0, ROWS - 4)], sums_sem.at[0], True)
    sums_c[0] = jnp.sum(sums_yz[...].reshape(ROWS // 8, 8, 128), axis=0)
    copy = send(sums_c.at[0], sums_c.at[1], sums_sem.at[2], sums_sem.at[3], twin)
    copy.start()
    copy.wait()
    acc = sums_c[0] + sums_c[1]
    acc = jnp.sum(acc[:4] + acc[4:], axis=1, keepdims=True)
    sq, a0, a1, uu = acc[0:1], acc[1:2], acc[2:3], acc[3:4]
    h10 = jnp.sqrt(uu)
    inv_h10 = 1.0 / h10
    a1 = a1 * inv_h10
    h01 = (shift + a0) * inv_h10
    h11 = h00 + a1 * inv_h10
    h21 = jnp.sqrt(jnp.maximum(sq - a0 * a0 - a1 * a1, 0.0)) * inv_h10

    rho0 = jnp.sqrt(h00 * h00 + h10 * h10)
    c0 = h00 / rho0
    s0 = h10 / rho0
    r01 = c0 * h01 + s0 * h11
    r11 = c0 * h11 - s0 * h01
    rho1 = jnp.sqrt(r11 * r11 + h21 * h21)
    c1 = r11 / rho1
    s1 = h21 / rho1
    g0 = c0 * beta
    g1 = -s0 * beta
    y1 = c1 * g1 / rho1
    y0 = (g0 - r01 * y1) / rho0
    norm_ref[...] = jnp.abs(s1 * g1)
    answer = y0 * v0 + (y1 * inv_h10) * u
    for h in range(2):
        out_ref[pl.ds(h, BLK_DEV, stride=2), :] = answer[:, 128 * h : 128 * h + 128]


def body(
    right_side, coords, diagonal, near_pairs, far_pairs, far_rank, far_left, far_right, far_scale
):
    vmem = pl.BlockSpec(memory_space=pltpu.VMEM)
    smem = pl.BlockSpec(memory_space=pltpu.SMEM)
    hbm = pl.BlockSpec(memory_space=pltpu.HBM)
    width = COLUMN * FAR_DEV
    scratch = [
        pltpu.VMEM((FACT, BS), BF16),
        pltpu.VMEM((FACT, BS), BF16),
        pltpu.VMEM((16, 128), F32),
        pltpu.VMEM((3, BLK_DEV * BS), F32),
        pltpu.VMEM((16, 128), F32),
        pltpu.VMEM((2, NEAR_DEV), jnp.int32),
        pltpu.VMEM((2, FAR_DEV), jnp.int32),
        pltpu.VMEM((1, FAR_DEV), jnp.int32),
        pltpu.VMEM((FAR_DEV, RMAX), F32),
        pltpu.VMEM((3, SLOTS, BS), F32),
        pltpu.VMEM((3 * SLOTS, BS), F32),
        pltpu.VMEM((SLOTS, 3, BS, 128), F32),
        pltpu.VMEM((NEAR_DEV, 2, 2, BS, BS), BF16),
        pltpu.VMEM((COLUMN, 8, width), F32),
        pltpu.VMEM((ROWS, width), BF16),
        pltpu.VMEM((width, ROWS), BF16),
        pltpu.VMEM((FAR_DEV, FACT), F32),
        pltpu.VMEM((BLK_DEV, FACT), F32),
        pltpu.VMEM((2, ROWS, 128), F32),
        pltpu.VMEM((2, COLUMN, FAR_DEV + EXTRA, 128), F32),
        pltpu.VMEM((2, COLUMN, FAR_DEV + EXTRA, 128), F32),
        pltpu.VMEM((2, 2, FAR_DEV, 128), F32),
        pltpu.VMEM((2, COLUMN, FAR_DEV, 128), F32),
        pltpu.VMEM((2, ROWS, 128), F32),
        pltpu.VMEM((2, ROWS, 128), F32),
        pltpu.VMEM((2, SLOTS, BS), F32),
        pltpu.VMEM((2, 2, SLOTS, BS), F32),
        pltpu.VMEM((2, N_X, BLK_DEV, BS), F32),
        pltpu.VMEM((2 * NEAR_DEV, BS), F32),
        pltpu.VMEM((ROWS, 128), F32),
        pltpu.VMEM((2, 8, 128), F32),
        pltpu.SemaphoreType.DMA((9,)),
        pltpu.SemaphoreType.DMA((6,)),
        pltpu.SemaphoreType.DMA((2, 20)),
        pltpu.SemaphoreType.DMA((4,)),
    ]
    solution, norm = pl.pallas_call(
        kernel,
        out_shape=(
            jax.ShapeDtypeStruct((16, 128), F32),
            jax.ShapeDtypeStruct((1, 1), F32),
        ),
        in_specs=[smem] + [hbm] * 9,
        out_specs=(vmem, vmem),
        scratch_shapes=scratch,
        compiler_params=pltpu.CompilerParams(
            collective_id=0, has_side_effects=True, vmem_limit_bytes=60 * 1024 * 1024
        ),
        cost_estimate=pl.CostEstimate(flops=100_000_000, bytes_accessed=2_000_000, transcendentals=2_000_000),
        name="gmres",
    )(
        near_pairs, right_side.reshape(16, 128), coords, diagonal.reshape(16, 128), near_pairs,
        far_pairs, far_rank.reshape(1, FAR_DEV), far_scale, far_left.reshape(FACT, BS),
        far_right.reshape(FACT, BS),
    )
    return solution.reshape(BLK_DEV * BS), norm.reshape(())


def solution(mesh):
    placed = (
        P("patch"),
        P(None, "patch"),
        P("patch"),
        P(None, ("patch", "pair")),
        P(None, ("patch", "pair")),
        P(("patch", "pair")),
        P(("patch", "pair"), None, None),
        P(("patch", "pair"), None, None),
        P(("patch", "pair"), None),
    )
    return jax.shard_map(
        body, mesh=mesh, in_specs=placed, out_specs=(P("patch"), P()), check_vma=False
    )
```

```python
import functools

import jax
import jax.numpy as jnp
from jax import lax
from jax.experimental import pallas as pl
from jax.experimental.pallas import tpu as pltpu
from jax.sharding import PartitionSpec as P

BS = 256
BLK_DEV = 8
RIM = 4
RMAX = 32
NEAR_DEV = 16
FAR_DEV = 32
NEAR_GAIN = 2.0
SOFT_SQ = 0.25

N_Y, N_Z, N_X = 8, 8, 4
N_YZ = N_Y * N_Z
ROWS = 4 * N_YZ
COLUMN = 2 * N_X
SLOTS = BLK_DEV + 2 * RIM
FACT = FAR_DEV * RMAX
EXTRA = 8

MESH = pl.DeviceIdType.MESH
HIGH = lax.Precision.HIGHEST
F32 = jnp.float32
BF16 = jnp.bfloat16


def place():
    patch = lax.axis_index("patch")
    return lax.axis_index("pair"), patch // (2 * N_Z), (patch // 2) % N_Z, patch % 2


def device(x, y, z, core):
    return {"patch": (y * N_Z + z) * 2 + core, "pair": x}


def send(src, dst, send_sem, recv_sem, to):
    return pltpu.make_async_remote_copy(
        src_ref=src, dst_ref=dst, send_sem=send_sem, recv_sem=recv_sem, device_id=to, device_id_type=MESH
    )


def far_first(n):
    return sorted(range(n), key=lambda d: -min(d, n - d))


def parts(value, count):
    found = []
    for _ in range(count):
        found.append(value.astype(BF16))
        value = value - found[-1].astype(F32)
    return found


def split(value):
    return jnp.concatenate(parts(value, 2), axis=0)


def dot(a, b):
    return jnp.dot(a, b, preferred_element_type=F32)


def dot_rows(a, b):
    return lax.dot_general(a, b, (((1,), (1,)), ((), ())), preferred_element_type=F32)


def fold(value):
    return jnp.sum(value, axis=0, keepdims=True)


def total(value):
    return jnp.sum(fold(value), axis=1, keepdims=True)


def kernel(
    near_smem, right_hbm, coords_hbm, diag_hbm, near_hbm, far_hbm, rank_hbm, scale_hbm, left_hbm, factor_hbm,
    out_ref, norm_ref,
    left, right, right_ref, coords_ref, diag_ref, near_ref, far_ref, rank_ref, scale_ref,
    hc, hct, cbc, tiles, keys, hot, hot_t, weight_d, hit_t,
    quarter, picked, got, given, taken, spread, landed, span, rim, joined,
    rows_n, sums_yz, sums_c,
    local_sem, once_sem, step_sem, sums_sem,
):
    x, y, z, core = place()
    patch = lax.axis_index("patch")
    n_patch = 2 * N_YZ
    first = patch * BLK_DEV
    yz = y * N_Z + z
    me = 2 * x + core
    mine = pl.ds(pl.multiple_of(yz * 4, 4), 4)
    up = {"patch": (patch + 1) % n_patch}
    down = {"patch": (patch + n_patch - 1) % n_patch}
    x_peers = [device((x + i) % N_X, y, z, core) for i in range(1, N_X)]
    twin = device(x, y, z, 1 - core)
    column = []
    for i in (4, 5, 2, 3, 6, 7, 1):
        other_x, other_core = (x + i // 2) % N_X, (core + i) % 2
        column.append((2 * other_x + other_core, other_x % 2, device(other_x, y, z, other_core)))

    barrier = pltpu.get_barrier_semaphore()

    z_peers = [((z + d) % N_Z, d) for d in far_first(N_Z)]

    def over_plane(act):
        def rows(k, _):
            other_y = (y + N_Y // 2 + ((k + 1) // 2) * (1 - 2 * (k % 2))) % N_Y
            for other_z, _ in z_peers:
                act(other_y, other_z)
            return 0

        lax.fori_loop(0, N_Y - 1, rows, 0)
        for other_z, d in z_peers:
            if d:
                act(y, other_z)

    def greet(other_y, other_z):
        pl.semaphore_signal(
            barrier, inc=1, device_id=device(x, other_y, other_z, core), device_id_type=MESH
        )

    over_plane(greet)
    for _, _, to in column:
        pl.semaphore_signal(barrier, inc=1, device_id=to, device_id_type=MESH)
    for to in (up, down):
        pl.semaphore_signal(barrier, inc=1, device_id=to, device_id_type=MESH)
    loads = [
        pltpu.make_async_copy(src, dst, local_sem.at[i])
        for i, (src, dst) in enumerate(
            (
                (left_hbm, left), (factor_hbm, right), (right_hbm, right_ref), (coords_hbm, coords_ref),
                (diag_hbm, diag_ref), (near_hbm, near_ref), (far_hbm, far_ref), (rank_hbm, rank_ref),
                (scale_hbm, scale_ref),
            )
        )
    ]
    for load in loads:
        load.start()
    for load in loads:
        load.wait()

    def natural(ref):
        return jnp.concatenate([ref[pl.ds(h, BLK_DEV, stride=2), :] for h in range(2)], axis=1)

    def own_quarter(value):
        found = value[:4, :128]
        for q in range(1, N_X):
            a, h = q // 2, q % 2
            found = jnp.where(x == q, value[4 * a : 4 * a + 4, 128 * h : 128 * h + 128], found)
        return found

    b_own = natural(right_ref)
    diag = natural(diag_ref)
    span[0, RIM : RIM + BLK_DEV, :] = b_own
    quarter[0, mine, :] = own_quarter(b_own)
    for d in range(3):
        for b in range(BLK_DEV):
            hc[d, RIM + b : RIM + b + 1, :] = coords_ref[d : d + 1, b * BS : (b + 1) * BS]

    near_f = near_ref[...].astype(F32)
    far_f = far_ref[...].astype(F32)
    sub_key = lax.broadcasted_iota(jnp.int32, (FAR_DEV, COLUMN * FAR_DEV), 0)
    lane_key = lax.broadcasted_iota(jnp.int32, (FAR_DEV, COLUMN * FAR_DEV), 1)
    pick = (lane_key == sub_key + me * FAR_DEV).astype(F32)
    laid = jnp.dot(far_f, pick, precision=HIGH, preferred_element_type=F32)
    keys[me] = jnp.broadcast_to(laid[0:1], (8, COLUMN * FAR_DEV))

    pair_of = lax.broadcasted_iota(jnp.int32, (FAR_DEV, FACT), 1) // RMAX
    term_of = lax.broadcasted_iota(jnp.int32, (FAR_DEV, FACT), 1) % RMAX
    sub = lax.broadcasted_iota(jnp.int32, (FAR_DEV, FACT), 0)
    eye = lax.broadcasted_iota(jnp.int32, (FAR_DEV, FAR_DEV), 0) == lax.broadcasted_iota(
        jnp.int32, (FAR_DEV, FAR_DEV), 1
    )
    rank_col = jnp.sum(jnp.where(eye, rank_ref[...].astype(F32), 0.0), axis=1, keepdims=True)
    term = lax.broadcasted_iota(jnp.int32, (FAR_DEV, RMAX), 1).astype(F32)
    weights = jnp.where(term < rank_col, scale_ref[...], 0.0)
    spread_w = jnp.dot(weights, (sub == term_of).astype(F32), precision=HIGH, preferred_element_type=F32)
    weight_d[...] = jnp.where(sub == pair_of, spread_w, 0.0)
    target_row = far_ref[1:2, :] - first
    onto = (lax.broadcasted_iota(jnp.int32, (BLK_DEV, FAR_DEV), 0) == target_row).astype(F32)
    hit_t[...] = jnp.dot(onto, (sub == pair_of).astype(F32), preferred_element_type=F32)

    def wait_for(view, sem, sent):
        copy = send(view, view, sem, sem, twin)
        if sent:
            copy.wait_send()
        else:
            copy.wait_recv()

    def plane(step, sems):
        def each(other_y, other_z):
            src, dst = step(other_y * N_Z + other_z)
            send(src, dst, sems[0], sems[1], device(x, other_y, other_z, core)).start()

        over_plane(each)

    def give(it, own_value):
        back = dot_rows(split(own_value), left[...])
        back = fold(hit_t[...] * (back[:BLK_DEV] + back[BLK_DEV:]))
        to_far = dot(split(weight_d[...] * back), right[...])
        to_far = to_far[:FAR_DEV] + to_far[FAR_DEV:]
        for h in range(2):
            given[it, h] = to_far[:, 128 * h : 128 * h + 128]
        taken[it, me] = given[it, x % 2]

    def give_start(it):
        for number, half, to in column:
            send(given.at[it, half], taken.at[it, me], step_sem.at[it, 0], step_sem.at[it, 1], to).start()

    def gather_start(it):
        own_rows = quarter.at[it, mine]
        plane(lambda there: (own_rows, own_rows), (step_sem.at[it, 2], step_sem.at[it, 3]))

    def span_start(it):
        send(
            span.at[it, pl.ds(BLK_DEV, RIM)], span.at[it, pl.ds(0, RIM)],
            step_sem.at[it, 4], step_sem.at[it, 5], up,
        ).start()
        send(
            span.at[it, pl.ds(RIM, RIM)], span.at[it, pl.ds(RIM + BLK_DEV, RIM)],
            step_sem.at[it, 6], step_sem.at[it, 7], down,
        ).start()

    def scatter_plane(it):
        wait_for(taken.at[it, pl.ds(0, COLUMN - 1)], step_sem.at[it, 1], False)
        value = 0.0
        for part in parts(taken[it].reshape(COLUMN * FAR_DEV, 128), 3):
            value = value + dot(hot[...], part)
        spread[it] = value
        landed[it, mine, :] = spread[it, mine, :]
        plane(
            lambda there: (spread.at[it, pl.ds(pl.multiple_of(there * 4, 4), 4)], landed.at[it, mine]),
            (step_sem.at[it, 8], step_sem.at[it, 9]),
        )

    def gather_column(it, extras):
        wait_for(quarter.at[it, pl.ds(0, ROWS - 4)], step_sem.at[it, 3], False)
        value = 0.0
        for part in parts(quarter[it], 3):
            value = value + dot(hot_t[...], part)
        picked[it, :, pl.ds(0, FAR_DEV), :] = value.reshape(COLUMN, FAR_DEV, 128)
        sums = [fold(quarter[i] * quarter[j]) for i, j in extras]
        sums = jnp.concatenate(sums + [jnp.zeros((EXTRA - len(sums), 128), F32)], axis=0)
        for g in range(COLUMN):
            picked[it, g, pl.ds(FAR_DEV, EXTRA), :] = sums
        got[it, me] = picked[it, me]
        for number, half, to in column:
            send(picked.at[it, number], got.at[it, me], step_sem.at[it, 10], step_sem.at[it, 11], to).start()

    def gather_end(it):
        wait_for(got.at[it, pl.ds(0, COLUMN - 1)], step_sem.at[it, 11], False)
        halves = []
        for h in range(2):
            at = 2 * h
            halves.append((got[it, at] + got[it, at + 1]) + (got[it, at + 4] + got[it, at + 5]))
        sums = jnp.sum(halves[0][FAR_DEV:] + halves[1][FAR_DEV:], axis=1, keepdims=True)
        far_v = split(jnp.concatenate([half[:FAR_DEV] for half in halves], axis=1))
        coef = dot_rows(far_v, right[...])
        coef = fold(weight_d[...] * (coef[:FAR_DEV] + coef[FAR_DEV:]))
        to_own = dot(split(hit_t[...] * coef), left[...])
        return to_own[:BLK_DEV] + to_own[BLK_DEV:], sums

    def near(it):
        wait_for(span.at[it, pl.ds(0, RIM)], step_sem.at[it, 5], False)
        wait_for(span.at[it, pl.ds(0, RIM)], step_sem.at[it, 7], False)
        vectors = []
        for way in range(2):
            rows = [
                span[it, pl.ds(jnp.clip(near_smem[way, k] - first + RIM, 0, SLOTS - 1), 1), :]
                for k in range(NEAR_DEV)
            ]
            vectors.append(split(jnp.concatenate(rows, axis=0)))
        for k in range(NEAR_DEV):
            for way in range(2):
                image = dot(vectors[way], tiles[k, way, 0]) + dot(vectors[way], tiles[k, way, 1])
                at = way * NEAR_DEV + k
                rows_n[at : at + 1, :] = image[k : k + 1] + image[NEAR_DEV + k : NEAR_DEV + k + 1]
        slot = lax.broadcasted_iota(jnp.int32, (SLOTS, NEAR_DEV), 0)
        hits = [(slot == near_ref[way : way + 1, :] - first + RIM).astype(F32) for way in (1, 0)]
        hits = jnp.concatenate(hits, axis=1).astype(BF16)
        value = 0.0
        for part in parts(rows_n[...], 3):
            value = value + dot(hits, part)
        rim[it, 0] = value
        send(
            rim.at[it, 0, pl.ds(0, RIM)], rim.at[it, 1, pl.ds(RIM, RIM)],
            step_sem.at[it, 12], step_sem.at[it, 13], down,
        ).start()
        send(
            rim.at[it, 0, pl.ds(RIM + BLK_DEV, RIM)], rim.at[it, 1, pl.ds(0, RIM)],
            step_sem.at[it, 14], step_sem.at[it, 15], up,
        ).start()

    def join(it, far_own):
        wait_for(rim.at[it, 1, pl.ds(0, RIM)], step_sem.at[it, 13], False)
        wait_for(rim.at[it, 1, pl.ds(0, RIM)], step_sem.at[it, 15], False)
        local = far_own + rim[it, 0, RIM : RIM + BLK_DEV, :] + rim[it, 1, 0:BLK_DEV, :]
        wait_for(landed.at[it, pl.ds(0, ROWS - 4)], step_sem.at[it, 9], False)
        image = jnp.sum(landed[it].reshape(ROWS // 8, 8, 128), axis=0)
        image = image[:4] + image[4:]
        image = jnp.concatenate([image, image], axis=0)
        image = jnp.concatenate([image, image], axis=1)
        at_row = lax.broadcasted_iota(jnp.int32, (BLK_DEV, BS), 0) // 4
        at_half = lax.broadcasted_iota(jnp.int32, (BLK_DEV, BS), 1) // 128
        joined[it, x] = local + jnp.where(2 * at_row + at_half == x, image, 0.0)
        for i in (2, 1, 3):
            send(
                joined.at[it, x], joined.at[it, x], step_sem.at[it, 16], step_sem.at[it, 16 + i], x_peers[i - 1]
            ).start()
        for i in range(1, N_X):
            wait_for(joined.at[it, (x + N_X - i) % N_X], step_sem.at[it, 16 + i], False)
        return (joined[it, 0] + joined[it, 1]) + (joined[it, 2] + joined[it, 3])

    def sent(it):
        wait_for(taken.at[it, pl.ds(0, COLUMN - 1)], step_sem.at[it, 0], True)
        wait_for(quarter.at[it, pl.ds(0, ROWS - 4)], step_sem.at[it, 2], True)
        wait_for(span.at[it, pl.ds(0, RIM)], step_sem.at[it, 4], True)
        wait_for(span.at[it, pl.ds(0, RIM)], step_sem.at[it, 6], True)
        wait_for(landed.at[it, pl.ds(0, ROWS - 4)], step_sem.at[it, 8], True)
        wait_for(got.at[it, pl.ds(0, COLUMN - 1)], step_sem.at[it, 10], True)
        wait_for(rim.at[it, 1, pl.ds(0, RIM)], step_sem.at[it, 12], True)
        wait_for(rim.at[it, 1, pl.ds(0, RIM)], step_sem.at[it, 14], True)
        wait_for(joined.at[it, pl.ds(0, N_X - 1)], step_sem.at[it, 16], True)

    def build(k, _):
        source = jnp.clip(near_smem[0, k] - first + RIM, 0, SLOTS - 1)
        target = jnp.clip(near_smem[1, k] - first + RIM, 0, SLOTS - 1)
        for way, (across, along) in enumerate(((source, target), (target, source))):
            line = [hc[d, pl.ds(along, 1), :] for d in range(3)]
            for r in range(0, BS, 64):
                col = [cbc[across, d, r : r + 64, :] for d in range(3)]
                for h in range(2):
                    dist = SOFT_SQ
                    for d in range(3):
                        diff = col[d] - line[d][:, 128 * h : 128 * h + 128]
                        dist = dist + diff * diff
                    tile = (NEAR_GAIN / BS) * lax.rsqrt(dist)
                    high = tile.astype(BF16)
                    tiles[k, way, 0, r : r + 64, 128 * h : 128 * h + 128] = high
                    tiles[k, way, 1, r : r + 64, 128 * h : 128 * h + 128] = (tile - high.astype(F32)).astype(BF16)
        return 0

    give(0, b_own)
    pl.semaphore_wait(barrier, N_YZ - 1 + COLUMN - 1 + 2)

    for number, half, to in column:
        send(keys.at[me], keys.at[me], once_sem.at[0], once_sem.at[1], to).start()
    give_start(0)
    halo_up = send(hc.at[:, pl.ds(BLK_DEV, RIM)], hc.at[:, pl.ds(0, RIM)], once_sem.at[2], once_sem.at[3], up)
    halo_down = send(
        hc.at[:, pl.ds(RIM, RIM)], hc.at[:, pl.ds(RIM + BLK_DEV, RIM)], once_sem.at[4], once_sem.at[5], down
    )
    halo_up.start()
    halo_down.start()
    gather_start(0)
    span_start(0)
    wait_for(keys.at[pl.ds(0, COLUMN - 1)], once_sem.at[1], False)
    key = keys[0]
    for g in range(1, COLUMN):
        key = key + keys[g]
    key = (key[0:1] + 0.5).astype(jnp.int32)
    row = lax.broadcasted_iota(jnp.int32, (ROWS, COLUMN * FAR_DEV), 0)
    block = (row // 4) * 16 + core * 8 + (x // 2) * 4 + row % 4
    hits = (block == key).astype(F32)
    hot[...] = hits.astype(BF16)
    hot_t[...] = hits.T.astype(BF16)
    scatter_plane(0)

    halo_up.wait_recv()
    halo_down.wait_recv()
    for d in range(3):
        hct[pl.ds(SLOTS * d, SLOTS), :] = hc[d]
    turned = hct[...].T
    for b in range(SLOTS):
        for d in range(3):
            at = SLOTS * d + b
            cbc[b, d] = jnp.broadcast_to(turned[:, at : at + 1], (BS, 128))
    lax.fori_loop(0, NEAR_DEV // 4, build, 0)
    gather_column(0, ((0, 0),))
    lax.fori_loop(NEAR_DEV // 4, NEAR_DEV, build, 0)
    near(0)
    far_own, sums = gather_end(0)
    beta = jnp.sqrt(sums[0:1])
    inv_beta = 1.0 / beta
    w_own = (join(0, far_own) + diag * b_own) * inv_beta

    span[1, RIM : RIM + BLK_DEV, :] = w_own
    quarter[1, mine, :] = own_quarter(w_own)
    give(1, w_own)
    give_start(1)
    span_start(1)
    gather_start(1)
    wait_for(keys.at[pl.ds(0, COLUMN - 1)], once_sem.at[0], True)
    halo_up.wait_send()
    halo_down.wait_send()
    sent(0)
    scatter_plane(1)
    near(1)
    gather_column(1, ((0, 1), (1, 1)))
    far_own, sums = gather_end(1)
    h00 = sums[0:1] * inv_beta
    shift = sums[1:2] - h00 * h00
    v0 = b_own * inv_beta
    u = w_own - h00 * v0
    rest = join(1, far_own) + diag * w_own - h00 * w_own - shift * v0 - h00 * u

    def lanes(value):
        value = fold(value)
        return value[:, :128] + value[:, 128:]

    sums_yz[mine, :] = jnp.concatenate(
        [lanes(rest * rest), lanes(rest * v0), lanes(rest * u), lanes(u * u)], axis=0
    )
    own_sums = sums_yz.at[mine]
    plane(lambda there: (own_sums, own_sums), (sums_sem.at[0], sums_sem.at[1]))
    sent(1)
    wait_for(sums_yz.at[pl.ds(0, ROWS - 4)], sums_sem.at[1], False)
    wait_for(sums_yz.at[pl.ds(0, ROWS - 4)], sums_sem.at[0], True)
    sums_c[0] = jnp.sum(sums_yz[...].reshape(ROWS // 8, 8, 128), axis=0)
    copy = send(sums_c.at[0], sums_c.at[1], sums_sem.at[2], sums_sem.at[3], twin)
    copy.start()
    copy.wait()
    acc = sums_c[0] + sums_c[1]
    acc = jnp.sum(acc[:4] + acc[4:], axis=1, keepdims=True)
    sq, a0, a1, uu = acc[0:1], acc[1:2], acc[2:3], acc[3:4]
    h10 = jnp.sqrt(uu)
    inv_h10 = 1.0 / h10
    a1 = a1 * inv_h10
    h01 = (shift + a0) * inv_h10
    h11 = h00 + a1 * inv_h10
    h21 = jnp.sqrt(jnp.maximum(sq - a0 * a0 - a1 * a1, 0.0)) * inv_h10

    rho0 = jnp.sqrt(h00 * h00 + h10 * h10)
    c0 = h00 / rho0
    s0 = h10 / rho0
    r01 = c0 * h01 + s0 * h11
    r11 = c0 * h11 - s0 * h01
    rho1 = jnp.sqrt(r11 * r11 + h21 * h21)
    c1 = r11 / rho1
    s1 = h21 / rho1
    g0 = c0 * beta
    g1 = -s0 * beta
    y1 = c1 * g1 / rho1
    y0 = (g0 - r01 * y1) / rho0
    norm_ref[...] = jnp.abs(s1 * g1)
    answer = y0 * v0 + (y1 * inv_h10) * u
    for h in range(2):
        out_ref[pl.ds(h, BLK_DEV, stride=2), :] = answer[:, 128 * h : 128 * h + 128]


def body(
    right_side, coords, diagonal, near_pairs, far_pairs, far_rank, far_left, far_right, far_scale
):
    vmem = pl.BlockSpec(memory_space=pltpu.VMEM)
    smem = pl.BlockSpec(memory_space=pltpu.SMEM)
    hbm = pl.BlockSpec(memory_space=pltpu.HBM)
    width = COLUMN * FAR_DEV
    scratch = [
        pltpu.VMEM((FACT, BS), BF16),
        pltpu.VMEM((FACT, BS), BF16),
        pltpu.VMEM((16, 128), F32),
        pltpu.VMEM((3, BLK_DEV * BS), F32),
        pltpu.VMEM((16, 128), F32),
        pltpu.VMEM((2, NEAR_DEV), jnp.int32),
        pltpu.VMEM((2, FAR_DEV), jnp.int32),
        pltpu.VMEM((1, FAR_DEV), jnp.int32),
        pltpu.VMEM((FAR_DEV, RMAX), F32),
        pltpu.VMEM((3, SLOTS, BS), F32),
        pltpu.VMEM((3 * SLOTS, BS), F32),
        pltpu.VMEM((SLOTS, 3, BS, 128), F32),
        pltpu.VMEM((NEAR_DEV, 2, 2, BS, BS), BF16),
        pltpu.VMEM((COLUMN, 8, width), F32),
        pltpu.VMEM((ROWS, width), BF16),
        pltpu.VMEM((width, ROWS), BF16),
        pltpu.VMEM((FAR_DEV, FACT), F32),
        pltpu.VMEM((BLK_DEV, FACT), F32),
        pltpu.VMEM((2, ROWS, 128), F32),
        pltpu.VMEM((2, COLUMN, FAR_DEV + EXTRA, 128), F32),
        pltpu.VMEM((2, COLUMN, FAR_DEV + EXTRA, 128), F32),
        pltpu.VMEM((2, 2, FAR_DEV, 128), F32),
        pltpu.VMEM((2, COLUMN, FAR_DEV, 128), F32),
        pltpu.VMEM((2, ROWS, 128), F32),
        pltpu.VMEM((2, ROWS, 128), F32),
        pltpu.VMEM((2, SLOTS, BS), F32),
        pltpu.VMEM((2, 2, SLOTS, BS), F32),
        pltpu.VMEM((2, N_X, BLK_DEV, BS), F32),
        pltpu.VMEM((2 * NEAR_DEV, BS), F32),
        pltpu.VMEM((ROWS, 128), F32),
        pltpu.VMEM((2, 8, 128), F32),
        pltpu.SemaphoreType.DMA((9,)),
        pltpu.SemaphoreType.DMA((6,)),
        pltpu.SemaphoreType.DMA((2, 20)),
        pltpu.SemaphoreType.DMA((4,)),
    ]
    solution, norm = pl.pallas_call(
        kernel,
        out_shape=(
            jax.ShapeDtypeStruct((16, 128), F32),
            jax.ShapeDtypeStruct((1, 1), F32),
        ),
        in_specs=[smem] + [hbm] * 9,
        out_specs=(vmem, vmem),
        scratch_shapes=scratch,
        compiler_params=pltpu.CompilerParams(
            collective_id=0, has_side_effects=True, vmem_limit_bytes=60 * 1024 * 1024
        ),
        cost_estimate=pl.CostEstimate(flops=100_000_000, bytes_accessed=2_000_000, transcendentals=2_000_000),
        name="gmres",
    )(
        near_pairs, right_side.reshape(16, 128), coords, diagonal.reshape(16, 128), near_pairs,
        far_pairs, far_rank.reshape(1, FAR_DEV), far_scale, far_left.reshape(FACT, BS),
        far_right.reshape(FACT, BS),
    )
    return solution.reshape(BLK_DEV * BS), norm.reshape(())


def solution(mesh):
    placed = (
        P("patch"),
        P(None, "patch"),
        P("patch"),
        P(None, ("patch", "pair")),
        P(None, ("patch", "pair")),
        P(("patch", "pair")),
        P(("patch", "pair"), None, None),
        P(("patch", "pair"), None, None),
        P(("patch", "pair"), None),
    )
    return jax.shard_map(
        body, mesh=mesh, in_specs=placed, out_specs=(P("patch"), P()), check_vma=False
    )
```

```python
import functools

import jax
import jax.numpy as jnp
from jax import lax
from jax.experimental import pallas as pl
from jax.experimental.pallas import tpu as pltpu
from jax.sharding import PartitionSpec as P

BS = 256
BLK_DEV = 8
RIM = 4
RMAX = 32
NEAR_DEV = 16
FAR_DEV = 32
NEAR_GAIN = 2.0
SOFT_SQ = 0.25

N_Y, N_Z, N_X = 8, 8, 4
N_YZ = N_Y * N_Z
ROWS = 4 * N_YZ
COLUMN = 2 * N_X
SLOTS = BLK_DEV + 2 * RIM
FACT = FAR_DEV * RMAX
EXTRA = 8

MESH = pl.DeviceIdType.MESH
HIGH = lax.Precision.HIGHEST
F32 = jnp.float32
BF16 = jnp.bfloat16


def place():
    patch = lax.axis_index("patch")
    return lax.axis_index("pair"), patch // (2 * N_Z), (patch // 2) % N_Z, patch % 2


def device(x, y, z, core):
    return {"patch": (y * N_Z + z) * 2 + core, "pair": x}


def send(src, dst, send_sem, recv_sem, to):
    return pltpu.make_async_remote_copy(
        src_ref=src, dst_ref=dst, send_sem=send_sem, recv_sem=recv_sem, device_id=to, device_id_type=MESH
    )


def far_first(n):
    return sorted(range(n), key=lambda d: -min(d, n - d))


def parts(value, count):
    found = []
    for _ in range(count):
        found.append(value.astype(BF16))
        value = value - found[-1].astype(F32)
    return found


def split(value):
    return jnp.concatenate(parts(value, 2), axis=0)


def dot(a, b):
    return jnp.dot(a, b, preferred_element_type=F32)


def dot_rows(a, b):
    return lax.dot_general(a, b, (((1,), (1,)), ((), ())), preferred_element_type=F32)


def fold(value):
    return jnp.sum(value, axis=0, keepdims=True)


def total(value):
    return jnp.sum(fold(value), axis=1, keepdims=True)


def kernel(
    near_smem, right_hbm, coords_hbm, diag_hbm, near_hbm, far_hbm, rank_hbm, scale_hbm, left_hbm, factor_hbm,
    out_ref, norm_ref,
    left, right, right_ref, coords_ref, diag_ref, near_ref, far_ref, rank_ref, scale_ref,
    hc, hct, cbc, tiles, keys, hot, hot_t, weight_d, hit_t,
    quarter, picked, got, given, taken, spread, landed, span, rim, joined,
    rows_n, sums_yz, sums_c,
    local_sem, once_sem, step_sem, sums_sem,
):
    x, y, z, core = place()
    patch = lax.axis_index("patch")
    n_patch = 2 * N_YZ
    first = patch * BLK_DEV
    yz = y * N_Z + z
    me = 2 * x + core
    mine = pl.ds(pl.multiple_of(yz * 4, 4), 4)
    up = {"patch": (patch + 1) % n_patch}
    down = {"patch": (patch + n_patch - 1) % n_patch}
    x_peers = [device((x + i) % N_X, y, z, core) for i in range(1, N_X)]
    twin = device(x, y, z, 1 - core)
    column = []
    for i in (4, 5, 2, 3, 6, 7, 1):
        other_x, other_core = (x + i // 2) % N_X, (core + i) % 2
        column.append((2 * other_x + other_core, other_x % 2, device(other_x, y, z, other_core)))

    barrier = pltpu.get_barrier_semaphore()

    z_peers = [((z + d) % N_Z, d) for d in far_first(N_Z)]

    def over_plane(act):
        def rows(k, _):
            other_y = (y + N_Y // 2 + ((k + 1) // 2) * (1 - 2 * (k % 2))) % N_Y
            for other_z, _ in z_peers:
                act(other_y, other_z)
            return 0

        lax.fori_loop(0, N_Y - 1, rows, 0)
        for other_z, d in z_peers:
            if d:
                act(y, other_z)

    def greet(other_y, other_z):
        pl.semaphore_signal(
            barrier, inc=1, device_id=device(x, other_y, other_z, core), device_id_type=MESH
        )

    over_plane(greet)
    for _, _, to in column:
        pl.semaphore_signal(barrier, inc=1, device_id=to, device_id_type=MESH)
    for to in (up, down):
        pl.semaphore_signal(barrier, inc=1, device_id=to, device_id_type=MESH)
    loads = [
        pltpu.make_async_copy(src, dst, local_sem.at[i])
        for i, (src, dst) in enumerate(
            (
                (left_hbm, left), (factor_hbm, right), (right_hbm, right_ref), (coords_hbm, coords_ref),
                (diag_hbm, diag_ref), (near_hbm, near_ref), (far_hbm, far_ref), (rank_hbm, rank_ref),
                (scale_hbm, scale_ref),
            )
        )
    ]
    for load in loads:
        load.start()
    for load in loads:
        load.wait()

    def natural(ref):
        return jnp.concatenate([ref[pl.ds(h, BLK_DEV, stride=2), :] for h in range(2)], axis=1)

    def own_quarter(value):
        found = value[:4, :128]
        for q in range(1, N_X):
            a, h = q // 2, q % 2
            found = jnp.where(x == q, value[4 * a : 4 * a + 4, 128 * h : 128 * h + 128], found)
        return found

    b_own = natural(right_ref)
    diag = natural(diag_ref)
    span[0, RIM : RIM + BLK_DEV, :] = b_own
    quarter[0, mine, :] = own_quarter(b_own)
    for d in range(3):
        for b in range(BLK_DEV):
            hc[d, RIM + b : RIM + b + 1, :] = coords_ref[d : d + 1, b * BS : (b + 1) * BS]

    near_f = near_ref[...].astype(F32)
    far_f = far_ref[...].astype(F32)
    sub_key = lax.broadcasted_iota(jnp.int32, (FAR_DEV, COLUMN * FAR_DEV), 0)
    lane_key = lax.broadcasted_iota(jnp.int32, (FAR_DEV, COLUMN * FAR_DEV), 1)
    pick = (lane_key == sub_key + me * FAR_DEV).astype(F32)
    laid = jnp.dot(far_f, pick, precision=HIGH, preferred_element_type=F32)
    keys[me] = jnp.broadcast_to(laid[0:1], (8, COLUMN * FAR_DEV))

    pair_of = lax.broadcasted_iota(jnp.int32, (FAR_DEV, FACT), 1) // RMAX
    term_of = lax.broadcasted_iota(jnp.int32, (FAR_DEV, FACT), 1) % RMAX
    sub = lax.broadcasted_iota(jnp.int32, (FAR_DEV, FACT), 0)
    eye = lax.broadcasted_iota(jnp.int32, (FAR_DEV, FAR_DEV), 0) == lax.broadcasted_iota(
        jnp.int32, (FAR_DEV, FAR_DEV), 1
    )
    rank_col = jnp.sum(jnp.where(eye, rank_ref[...].astype(F32), 0.0), axis=1, keepdims=True)
    term = lax.broadcasted_iota(jnp.int32, (FAR_DEV, RMAX), 1).astype(F32)
    weights = jnp.where(term < rank_col, scale_ref[...], 0.0)
    spread_w = jnp.dot(weights, (sub == term_of).astype(F32), precision=HIGH, preferred_element_type=F32)
    weight_d[...] = jnp.where(sub == pair_of, spread_w, 0.0)
    target_row = far_ref[1:2, :] - first
    onto = (lax.broadcasted_iota(jnp.int32, (BLK_DEV, FAR_DEV), 0) == target_row).astype(F32)
    hit_t[...] = jnp.dot(onto, (sub == pair_of).astype(F32), preferred_element_type=F32)

    def wait_for(view, sem, sent):
        copy = send(view, view, sem, sem, twin)
        if sent:
            copy.wait_send()
        else:
            copy.wait_recv()

    def plane(step, sems):
        def each(other_y, other_z):
            src, dst = step(other_y * N_Z + other_z)
            send(src, dst, sems[0], sems[1], device(x, other_y, other_z, core)).start()

        over_plane(each)

    def give(it, own_value):
        back = dot_rows(split(own_value), left[...])
        back = fold(hit_t[...] * (back[:BLK_DEV] + back[BLK_DEV:]))
        to_far = dot(split(weight_d[...] * back), right[...])
        to_far = to_far[:FAR_DEV] + to_far[FAR_DEV:]
        for h in range(2):
            given[it, h] = to_far[:, 128 * h : 128 * h + 128]
        taken[it, me] = given[it, x % 2]

    def give_start(it):
        for number, half, to in column:
            send(given.at[it, half], taken.at[it, me], step_sem.at[it, 0], step_sem.at[it, 1], to).start()

    def gather_start(it):
        own_rows = quarter.at[it, mine]
        plane(lambda there: (own_rows, own_rows), (step_sem.at[it, 2], step_sem.at[it, 3]))

    def span_start(it):
        send(
            span.at[it, pl.ds(BLK_DEV, RIM)], span.at[it, pl.ds(0, RIM)],
            step_sem.at[it, 4], step_sem.at[it, 5], up,
        ).start()
        send(
            span.at[it, pl.ds(RIM, RIM)], span.at[it, pl.ds(RIM + BLK_DEV, RIM)],
            step_sem.at[it, 6], step_sem.at[it, 7], down,
        ).start()

    def scatter_plane(it):
        wait_for(taken.at[it, pl.ds(0, COLUMN - 1)], step_sem.at[it, 1], False)
        value = 0.0
        for part in parts(taken[it].reshape(COLUMN * FAR_DEV, 128), 3):
            value = value + dot(hot[...], part)
        spread[it] = value
        landed[it, mine, :] = spread[it, mine, :]
        plane(
            lambda there: (spread.at[it, pl.ds(pl.multiple_of(there * 4, 4), 4)], landed.at[it, mine]),
            (step_sem.at[it, 8], step_sem.at[it, 9]),
        )

    def gather_column(it, extras):
        wait_for(quarter.at[it, pl.ds(0, ROWS - 4)], step_sem.at[it, 3], False)
        value = 0.0
        for part in parts(quarter[it], 3):
            value = value + dot(hot_t[...], part)
        picked[it, :, pl.ds(0, FAR_DEV), :] = value.reshape(COLUMN, FAR_DEV, 128)
        sums = [fold(quarter[i] * quarter[j]) for i, j in extras]
        sums = jnp.concatenate(sums + [jnp.zeros((EXTRA - len(sums), 128), F32)], axis=0)
        for g in range(COLUMN):
            picked[it, g, pl.ds(FAR_DEV, EXTRA), :] = sums
        got[it, me] = picked[it, me]
        for number, half, to in column:
            send(picked.at[it, number], got.at[it, me], step_sem.at[it, 10], step_sem.at[it, 11], to).start()

    def gather_end(it):
        wait_for(got.at[it, pl.ds(0, COLUMN - 1)], step_sem.at[it, 11], False)
        halves = []
        for h in range(2):
            at = 2 * h
            halves.append((got[it, at] + got[it, at + 1]) + (got[it, at + 4] + got[it, at + 5]))
        sums = jnp.sum(halves[0][FAR_DEV:] + halves[1][FAR_DEV:], axis=1, keepdims=True)
        far_v = split(jnp.concatenate([half[:FAR_DEV] for half in halves], axis=1))
        coef = dot_rows(far_v, right[...])
        coef = fold(weight_d[...] * (coef[:FAR_DEV] + coef[FAR_DEV:]))
        to_own = dot(split(hit_t[...] * coef), left[...])
        return to_own[:BLK_DEV] + to_own[BLK_DEV:], sums

    def near(it):
        wait_for(span.at[it, pl.ds(0, RIM)], step_sem.at[it, 5], False)
        wait_for(span.at[it, pl.ds(0, RIM)], step_sem.at[it, 7], False)
        vectors = []
        for way in range(2):
            rows = [
                span[it, pl.ds(jnp.clip(near_smem[way, k] - first + RIM, 0, SLOTS - 1), 1), :]
                for k in range(NEAR_DEV)
            ]
            vectors.append(split(jnp.concatenate(rows, axis=0)))
        for k in range(NEAR_DEV):
            for way, multiply in enumerate((dot_rows, dot)):
                image = multiply(vectors[way], tiles[k, 0]) + multiply(vectors[way], tiles[k, 1])
                at = way * NEAR_DEV + k
                rows_n[at : at + 1, :] = image[k : k + 1] + image[NEAR_DEV + k : NEAR_DEV + k + 1]
        slot = lax.broadcasted_iota(jnp.int32, (SLOTS, NEAR_DEV), 0)
        hits = [(slot == near_ref[way : way + 1, :] - first + RIM).astype(F32) for way in (1, 0)]
        hits = jnp.concatenate(hits, axis=1).astype(BF16)
        value = 0.0
        for part in parts(rows_n[...], 3):
            value = value + dot(hits, part)
        rim[it, 0] = value
        send(
            rim.at[it, 0, pl.ds(0, RIM)], rim.at[it, 1, pl.ds(RIM, RIM)],
            step_sem.at[it, 12], step_sem.at[it, 13], down,
        ).start()
        send(
            rim.at[it, 0, pl.ds(RIM + BLK_DEV, RIM)], rim.at[it, 1, pl.ds(0, RIM)],
            step_sem.at[it, 14], step_sem.at[it, 15], up,
        ).start()

    def join(it, far_own):
        wait_for(rim.at[it, 1, pl.ds(0, RIM)], step_sem.at[it, 13], False)
        wait_for(rim.at[it, 1, pl.ds(0, RIM)], step_sem.at[it, 15], False)
        local = far_own + rim[it, 0, RIM : RIM + BLK_DEV, :] + rim[it, 1, 0:BLK_DEV, :]
        wait_for(landed.at[it, pl.ds(0, ROWS - 4)], step_sem.at[it, 9], False)
        image = jnp.sum(landed[it].reshape(ROWS // 8, 8, 128), axis=0)
        image = image[:4] + image[4:]
        image = jnp.concatenate([image, image], axis=0)
        image = jnp.concatenate([image, image], axis=1)
        at_row = lax.broadcasted_iota(jnp.int32, (BLK_DEV, BS), 0) // 4
        at_half = lax.broadcasted_iota(jnp.int32, (BLK_DEV, BS), 1) // 128
        joined[it, x] = local + jnp.where(2 * at_row + at_half == x, image, 0.0)
        for i in (2, 1, 3):
            send(
                joined.at[it, x], joined.at[it, x], step_sem.at[it, 16], step_sem.at[it, 16 + i], x_peers[i - 1]
            ).start()
        for i in range(1, N_X):
            wait_for(joined.at[it, (x + N_X - i) % N_X], step_sem.at[it, 16 + i], False)
        return (joined[it, 0] + joined[it, 1]) + (joined[it, 2] + joined[it, 3])

    def sent(it):
        wait_for(taken.at[it, pl.ds(0, COLUMN - 1)], step_sem.at[it, 0], True)
        wait_for(quarter.at[it, pl.ds(0, ROWS - 4)], step_sem.at[it, 2], True)
        wait_for(span.at[it, pl.ds(0, RIM)], step_sem.at[it, 4], True)
        wait_for(span.at[it, pl.ds(0, RIM)], step_sem.at[it, 6], True)
        wait_for(landed.at[it, pl.ds(0, ROWS - 4)], step_sem.at[it, 8], True)
        wait_for(got.at[it, pl.ds(0, COLUMN - 1)], step_sem.at[it, 10], True)
        wait_for(rim.at[it, 1, pl.ds(0, RIM)], step_sem.at[it, 12], True)
        wait_for(rim.at[it, 1, pl.ds(0, RIM)], step_sem.at[it, 14], True)
        wait_for(joined.at[it, pl.ds(0, N_X - 1)], step_sem.at[it, 16], True)

    def build(k, _):
        source = jnp.clip(near_smem[0, k] - first + RIM, 0, SLOTS - 1)
        target = jnp.clip(near_smem[1, k] - first, 0, BLK_DEV - 1)
        line = [hc[d, pl.ds(source, 1), :] for d in range(3)]
        for r in range(0, BS, 64):
            col = [cbc[target, d, r : r + 64, :] for d in range(3)]
            for h in range(2):
                dist = SOFT_SQ
                for d in range(3):
                    diff = col[d] - line[d][:, 128 * h : 128 * h + 128]
                    dist = dist + diff * diff
                tile = (NEAR_GAIN / BS) * lax.rsqrt(dist)
                high = tile.astype(BF16)
                tiles[k, 0, r : r + 64, 128 * h : 128 * h + 128] = high
                tiles[k, 1, r : r + 64, 128 * h : 128 * h + 128] = (tile - high.astype(F32)).astype(BF16)
        return 0

    give(0, b_own)
    for d in range(3):
        hct[pl.ds(BLK_DEV * d, BLK_DEV), :] = hc[d, RIM : RIM + BLK_DEV, :]
    turned = hct[...].T
    for b in range(BLK_DEV):
        for d in range(3):
            at = BLK_DEV * d + b
            cbc[b, d] = jnp.broadcast_to(turned[:, at : at + 1], (BS, 128))
    pl.semaphore_wait(barrier, N_YZ - 1 + COLUMN - 1 + 2)

    for number, half, to in column:
        send(keys.at[me], keys.at[me], once_sem.at[0], once_sem.at[1], to).start()
    give_start(0)
    halo_up = send(hc.at[:, pl.ds(BLK_DEV, RIM)], hc.at[:, pl.ds(0, RIM)], once_sem.at[2], once_sem.at[3], up)
    halo_down = send(
        hc.at[:, pl.ds(RIM, RIM)], hc.at[:, pl.ds(RIM + BLK_DEV, RIM)], once_sem.at[4], once_sem.at[5], down
    )
    gather_start(0)
    halo_up.start()
    halo_down.start()
    span_start(0)
    wait_for(keys.at[pl.ds(0, COLUMN - 1)], once_sem.at[1], False)
    key = keys[0]
    for g in range(1, COLUMN):
        key = key + keys[g]
    key = (key[0:1] + 0.5).astype(jnp.int32)
    row = lax.broadcasted_iota(jnp.int32, (ROWS, COLUMN * FAR_DEV), 0)
    block = (row // 4) * 16 + core * 8 + (x // 2) * 4 + row % 4
    hits = (block == key).astype(F32)
    hot[...] = hits.astype(BF16)
    hot_t[...] = hits.T.astype(BF16)
    scatter_plane(0)

    halo_up.wait_recv()
    halo_down.wait_recv()
    lax.fori_loop(0, NEAR_DEV // 2, build, 0)
    gather_column(0, ((0, 0),))
    lax.fori_loop(NEAR_DEV // 2, NEAR_DEV, build, 0)
    near(0)
    far_own, sums = gather_end(0)
    beta = jnp.sqrt(sums[0:1])
    inv_beta = 1.0 / beta
    w_own = (join(0, far_own) + diag * b_own) * inv_beta

    span[1, RIM : RIM + BLK_DEV, :] = w_own
    quarter[1, mine, :] = own_quarter(w_own)
    give(1, w_own)
    give_start(1)
    span_start(1)
    gather_start(1)
    wait_for(keys.at[pl.ds(0, COLUMN - 1)], once_sem.at[0], True)
    halo_up.wait_send()
    halo_down.wait_send()
    sent(0)
    scatter_plane(1)
    near(1)
    gather_column(1, ((0, 1), (1, 1)))
    far_own, sums = gather_end(1)
    h00 = sums[0:1] * inv_beta
    shift = sums[1:2] - h00 * h00
    v0 = b_own * inv_beta
    u = w_own - h00 * v0
    rest = join(1, far_own) + diag * w_own - h00 * w_own - shift * v0 - h00 * u

    def lanes(value):
        value = fold(value)
        return value[:, :128] + value[:, 128:]

    sums_yz[mine, :] = jnp.concatenate(
        [lanes(rest * rest), lanes(rest * v0), lanes(rest * u), lanes(u * u)], axis=0
    )
    own_sums = sums_yz.at[mine]
    plane(lambda there: (own_sums, own_sums), (sums_sem.at[0], sums_sem.at[1]))
    sent(1)
    wait_for(sums_yz.at[pl.ds(0, ROWS - 4)], sums_sem.at[1], False)
    wait_for(sums_yz.at[pl.ds(0, ROWS - 4)], sums_sem.at[0], True)
    sums_c[0] = jnp.sum(sums_yz[...].reshape(ROWS // 8, 8, 128), axis=0)
    copy = send(sums_c.at[0], sums_c.at[1], sums_sem.at[2], sums_sem.at[3], twin)
    copy.start()
    copy.wait()
    acc = sums_c[0] + sums_c[1]
    acc = jnp.sum(acc[:4] + acc[4:], axis=1, keepdims=True)
    sq, a0, a1, uu = acc[0:1], acc[1:2], acc[2:3], acc[3:4]
    h10 = jnp.sqrt(uu)
    inv_h10 = 1.0 / h10
    a1 = a1 * inv_h10
    h01 = (shift + a0) * inv_h10
    h11 = h00 + a1 * inv_h10
    h21 = jnp.sqrt(jnp.maximum(sq - a0 * a0 - a1 * a1, 0.0)) * inv_h10

    rho0 = jnp.sqrt(h00 * h00 + h10 * h10)
    c0 = h00 / rho0
    s0 = h10 / rho0
    r01 = c0 * h01 + s0 * h11
    r11 = c0 * h11 - s0 * h01
    rho1 = jnp.sqrt(r11 * r11 + h21 * h21)
    c1 = r11 / rho1
    s1 = h21 / rho1
    g0 = c0 * beta
    g1 = -s0 * beta
    y1 = c1 * g1 / rho1
    y0 = (g0 - r01 * y1) / rho0
    norm_ref[...] = jnp.abs(s1 * g1)
    answer = y0 * v0 + (y1 * inv_h10) * u
    for h in range(2):
        out_ref[pl.ds(h, BLK_DEV, stride=2), :] = answer[:, 128 * h : 128 * h + 128]


def body(
    right_side, coords, diagonal, near_pairs, far_pairs, far_rank, far_left, far_right, far_scale
):
    vmem = pl.BlockSpec(memory_space=pltpu.VMEM)
    smem = pl.BlockSpec(memory_space=pltpu.SMEM)
    hbm = pl.BlockSpec(memory_space=pltpu.HBM)
    width = COLUMN * FAR_DEV
    scratch = [
        pltpu.VMEM((FACT, BS), BF16),
        pltpu.VMEM((FACT, BS), BF16),
        pltpu.VMEM((16, 128), F32),
        pltpu.VMEM((3, BLK_DEV * BS), F32),
        pltpu.VMEM((16, 128), F32),
        pltpu.VMEM((2, NEAR_DEV), jnp.int32),
        pltpu.VMEM((2, FAR_DEV), jnp.int32),
        pltpu.VMEM((1, FAR_DEV), jnp.int32),
        pltpu.VMEM((FAR_DEV, RMAX), F32),
        pltpu.VMEM((3, SLOTS, BS), F32),
        pltpu.VMEM((3 * BLK_DEV, BS), F32),
        pltpu.VMEM((BLK_DEV, 3, BS, 128), F32),
        pltpu.VMEM((NEAR_DEV, 2, BS, BS), BF16),
        pltpu.VMEM((COLUMN, 8, width), F32),
        pltpu.VMEM((ROWS, width), BF16),
        pltpu.VMEM((width, ROWS), BF16),
        pltpu.VMEM((FAR_DEV, FACT), F32),
        pltpu.VMEM((BLK_DEV, FACT), F32),
        pltpu.VMEM((2, ROWS, 128), F32),
        pltpu.VMEM((2, COLUMN, FAR_DEV + EXTRA, 128), F32),
        pltpu.VMEM((2, COLUMN, FAR_DEV + EXTRA, 128), F32),
        pltpu.VMEM((2, 2, FAR_DEV, 128), F32),
        pltpu.VMEM((2, COLUMN, FAR_DEV, 128), F32),
        pltpu.VMEM((2, ROWS, 128), F32),
        pltpu.VMEM((2, ROWS, 128), F32),
        pltpu.VMEM((2, SLOTS, BS), F32),
        pltpu.VMEM((2, 2, SLOTS, BS), F32),
        pltpu.VMEM((2, N_X, BLK_DEV, BS), F32),
        pltpu.VMEM((2 * NEAR_DEV, BS), F32),
        pltpu.VMEM((ROWS, 128), F32),
        pltpu.VMEM((2, 8, 128), F32),
        pltpu.SemaphoreType.DMA((9,)),
        pltpu.SemaphoreType.DMA((6,)),
        pltpu.SemaphoreType.DMA((2, 20)),
        pltpu.SemaphoreType.DMA((4,)),
    ]
    solution, norm = pl.pallas_call(
        kernel,
        out_shape=(
            jax.ShapeDtypeStruct((16, 128), F32),
            jax.ShapeDtypeStruct((1, 1), F32),
        ),
        in_specs=[smem] + [hbm] * 9,
        out_specs=(vmem, vmem),
        scratch_shapes=scratch,
        compiler_params=pltpu.CompilerParams(
            collective_id=0, has_side_effects=True, vmem_limit_bytes=60 * 1024 * 1024
        ),
        cost_estimate=pl.CostEstimate(flops=100_000_000, bytes_accessed=2_000_000, transcendentals=2_000_000),
        name="gmres",
    )(
        near_pairs, right_side.reshape(16, 128), coords, diagonal.reshape(16, 128), near_pairs,
        far_pairs, far_rank.reshape(1, FAR_DEV), far_scale, far_left.reshape(FACT, BS),
        far_right.reshape(FACT, BS),
    )
    return solution.reshape(BLK_DEV * BS), norm.reshape(())


def solution(mesh):
    placed = (
        P("patch"),
        P(None, "patch"),
        P("patch"),
        P(None, ("patch", "pair")),
        P(None, ("patch", "pair")),
        P(("patch", "pair")),
        P(("patch", "pair"), None, None),
        P(("patch", "pair"), None, None),
        P(("patch", "pair"), None),
    )
    return jax.shard_map(
        body, mesh=mesh, in_specs=placed, out_specs=(P("patch"), P()), check_vma=False
    )
```

```python
import functools

import jax
import jax.numpy as jnp
from jax import lax
from jax.experimental import pallas as pl
from jax.experimental.pallas import tpu as pltpu
from jax.sharding import PartitionSpec as P

BS = 256
BLK_DEV = 8
RIM = 4
RMAX = 32
NEAR_DEV = 16
FAR_DEV = 32
NEAR_GAIN = 2.0
SOFT_SQ = 0.25

N_Y, N_Z, N_X = 8, 8, 4
N_YZ = N_Y * N_Z
ROWS = 4 * N_YZ
COLUMN = 2 * N_X
SLOTS = BLK_DEV + 2 * RIM
FACT = FAR_DEV * RMAX
EXTRA = 8

MESH = pl.DeviceIdType.MESH
HIGH = lax.Precision.HIGHEST
F32 = jnp.float32
BF16 = jnp.bfloat16


def place():
    patch = lax.axis_index("patch")
    return lax.axis_index("pair"), patch // (2 * N_Z), (patch // 2) % N_Z, patch % 2


def device(x, y, z, core):
    return {"patch": (y * N_Z + z) * 2 + core, "pair": x}


def send(src, dst, send_sem, recv_sem, to):
    return pltpu.make_async_remote_copy(
        src_ref=src, dst_ref=dst, send_sem=send_sem, recv_sem=recv_sem, device_id=to, device_id_type=MESH
    )


def far_first(n):
    return sorted(range(n), key=lambda d: -min(d, n - d))


def parts(value, count):
    found = []
    for _ in range(count):
        found.append(value.astype(BF16))
        value = value - found[-1].astype(F32)
    return found


def split(value):
    return jnp.concatenate(parts(value, 2), axis=0)


def dot(a, b):
    return jnp.dot(a, b, preferred_element_type=F32)


def dot_rows(a, b):
    return lax.dot_general(a, b, (((1,), (1,)), ((), ())), preferred_element_type=F32)


def fold(value):
    return jnp.sum(value, axis=0, keepdims=True)


def total(value):
    return jnp.sum(fold(value), axis=1, keepdims=True)


def kernel(
    near_smem, right_hbm, coords_hbm, diag_hbm, near_hbm, far_hbm, rank_hbm, scale_hbm, left_hbm, factor_hbm,
    out_ref, norm_ref,
    left, right, right_ref, coords_ref, diag_ref, near_ref, far_ref, rank_ref, scale_ref,
    hc, hct, cbc, tiles, keys, hot, hot_t, weight_d, hit_t,
    quarter, picked, got, given, taken, spread, landed, span, rim, joined,
    rows_n, shared, sums_yz,
    local_sem, once_sem, step_sem, sums_sem,
):
    x, y, z, core = place()
    patch = lax.axis_index("patch")
    n_patch = 2 * N_YZ
    first = patch * BLK_DEV
    yz = y * N_Z + z
    me = 2 * x + core
    mine = pl.ds(pl.multiple_of(yz * 4, 4), 4)
    up = {"patch": (patch + 1) % n_patch}
    down = {"patch": (patch + n_patch - 1) % n_patch}
    twin = device(x, y, z, 1 - core)
    column = []
    for i in (4, 5, 2, 3, 6, 7, 1):
        other_x, other_core = (x + i // 2) % N_X, (core + i) % 2
        column.append((2 * other_x + other_core, other_x % 2, device(other_x, y, z, other_core)))

    joins = ([device((x + i) % N_X, y, z, core) for i in (2, 1, 3)], [to for _, _, to in column])

    barrier = pltpu.get_barrier_semaphore()

    z_peers = [((z + d) % N_Z, d) for d in far_first(N_Z)]

    def over_plane(act):
        def rows(k, _):
            other_y = (y + N_Y // 2 + ((k + 1) // 2) * (1 - 2 * (k % 2))) % N_Y
            for other_z, _ in z_peers:
                act(other_y, other_z)
            return 0

        lax.fori_loop(0, N_Y - 1, rows, 0)
        for other_z, d in z_peers:
            if d:
                act(y, other_z)

    def greet(other_y, other_z):
        pl.semaphore_signal(
            barrier, inc=1, device_id=device(x, other_y, other_z, core), device_id_type=MESH
        )

    over_plane(greet)
    for _, _, to in column:
        pl.semaphore_signal(barrier, inc=1, device_id=to, device_id_type=MESH)
    for to in (up, down):
        pl.semaphore_signal(barrier, inc=1, device_id=to, device_id_type=MESH)
    loads = [
        pltpu.make_async_copy(src, dst, local_sem.at[i])
        for i, (src, dst) in enumerate(
            (
                (left_hbm, left), (factor_hbm, right), (right_hbm, right_ref), (coords_hbm, coords_ref),
                (diag_hbm, diag_ref), (near_hbm, near_ref), (far_hbm, far_ref), (rank_hbm, rank_ref),
                (scale_hbm, scale_ref),
            )
        )
    ]
    for load in loads:
        load.start()
    for load in loads:
        load.wait()

    def natural(ref):
        return jnp.concatenate([ref[pl.ds(h, BLK_DEV, stride=2), :] for h in range(2)], axis=1)

    def own_quarter(value):
        found = value[:4, :128]
        for q in range(1, N_X):
            a, h = q // 2, q % 2
            found = jnp.where(x == q, value[4 * a : 4 * a + 4, 128 * h : 128 * h + 128], found)
        return found

    b_own = natural(right_ref)
    diag = natural(diag_ref)
    span[0, RIM : RIM + BLK_DEV, :] = b_own
    shared[core, 0] = b_own
    shared[core, 1] = diag
    quarter[0, mine, :] = own_quarter(b_own)
    for d in range(3):
        for b in range(BLK_DEV):
            hc[d, RIM + b : RIM + b + 1, :] = coords_ref[d : d + 1, b * BS : (b + 1) * BS]

    near_f = near_ref[...].astype(F32)
    far_f = far_ref[...].astype(F32)
    sub_key = lax.broadcasted_iota(jnp.int32, (FAR_DEV, COLUMN * FAR_DEV), 0)
    lane_key = lax.broadcasted_iota(jnp.int32, (FAR_DEV, COLUMN * FAR_DEV), 1)
    pick = (lane_key == sub_key + me * FAR_DEV).astype(F32)
    laid = jnp.dot(far_f, pick, precision=HIGH, preferred_element_type=F32)
    keys[me] = jnp.broadcast_to(laid[0:1], (8, COLUMN * FAR_DEV))

    pair_of = lax.broadcasted_iota(jnp.int32, (FAR_DEV, FACT), 1) // RMAX
    term_of = lax.broadcasted_iota(jnp.int32, (FAR_DEV, FACT), 1) % RMAX
    sub = lax.broadcasted_iota(jnp.int32, (FAR_DEV, FACT), 0)
    eye = lax.broadcasted_iota(jnp.int32, (FAR_DEV, FAR_DEV), 0) == lax.broadcasted_iota(
        jnp.int32, (FAR_DEV, FAR_DEV), 1
    )
    rank_col = jnp.sum(jnp.where(eye, rank_ref[...].astype(F32), 0.0), axis=1, keepdims=True)
    term = lax.broadcasted_iota(jnp.int32, (FAR_DEV, RMAX), 1).astype(F32)
    weights = jnp.where(term < rank_col, scale_ref[...], 0.0)
    spread_w = jnp.dot(weights, (sub == term_of).astype(F32), precision=HIGH, preferred_element_type=F32)
    weight_d[...] = jnp.where(sub == pair_of, spread_w, 0.0)
    target_row = far_ref[1:2, :] - first
    onto = (lax.broadcasted_iota(jnp.int32, (BLK_DEV, FAR_DEV), 0) == target_row).astype(F32)
    hit_t[...] = jnp.dot(onto, (sub == pair_of).astype(F32), preferred_element_type=F32)

    def wait_for(view, sem, sent):
        copy = send(view, view, sem, sem, twin)
        if sent:
            copy.wait_send()
        else:
            copy.wait_recv()

    def plane(step, sems):
        def each(other_y, other_z):
            src, dst = step(other_y * N_Z + other_z)
            send(src, dst, sems[0], sems[1], device(x, other_y, other_z, core)).start()

        over_plane(each)

    def give(it, own_value):
        back = dot_rows(split(own_value), left[...])
        back = fold(hit_t[...] * (back[:BLK_DEV] + back[BLK_DEV:]))
        to_far = dot(split(weight_d[...] * back), right[...])
        to_far = to_far[:FAR_DEV] + to_far[FAR_DEV:]
        for h in range(2):
            given[it, h] = to_far[:, 128 * h : 128 * h + 128]
        taken[it, me] = given[it, x % 2]

    def give_start(it):
        for number, half, to in column:
            send(given.at[it, half], taken.at[it, me], step_sem.at[it, 0], step_sem.at[it, 1], to).start()

    def gather_start(it):
        own_rows = quarter.at[it, mine]
        plane(lambda there: (own_rows, own_rows), (step_sem.at[it, 2], step_sem.at[it, 3]))

    def span_start(it):
        send(
            span.at[it, pl.ds(BLK_DEV, RIM)], span.at[it, pl.ds(0, RIM)],
            step_sem.at[it, 4], step_sem.at[it, 5], up,
        ).start()
        send(
            span.at[it, pl.ds(RIM, RIM)], span.at[it, pl.ds(RIM + BLK_DEV, RIM)],
            step_sem.at[it, 6], step_sem.at[it, 7], down,
        ).start()

    def scatter_plane(it):
        wait_for(taken.at[it, pl.ds(0, COLUMN - 1)], step_sem.at[it, 1], False)
        value = 0.0
        for part in parts(taken[it].reshape(COLUMN * FAR_DEV, 128), 3):
            value = value + dot(hot[...], part)
        spread[it] = value
        landed[it, mine, :] = spread[it, mine, :]
        plane(
            lambda there: (spread.at[it, pl.ds(pl.multiple_of(there * 4, 4), 4)], landed.at[it, mine]),
            (step_sem.at[it, 8], step_sem.at[it, 9]),
        )

    def gather_column(it, extras):
        wait_for(quarter.at[it, pl.ds(0, ROWS - 4)], step_sem.at[it, 3], False)
        value = 0.0
        for part in parts(quarter[it], 3):
            value = value + dot(hot_t[...], part)
        picked[it, :, pl.ds(0, FAR_DEV), :] = value.reshape(COLUMN, FAR_DEV, 128)
        sums = [fold(quarter[i] * quarter[j]) for i, j in extras]
        sums = jnp.concatenate(sums + [jnp.zeros((EXTRA - len(sums), 128), F32)], axis=0)
        for g in range(COLUMN):
            picked[it, g, pl.ds(FAR_DEV, EXTRA), :] = sums
        got[it, me] = picked[it, me]
        for number, half, to in column:
            send(picked.at[it, number], got.at[it, me], step_sem.at[it, 10], step_sem.at[it, 11], to).start()

    def gather_end(it):
        wait_for(got.at[it, pl.ds(0, COLUMN - 1)], step_sem.at[it, 11], False)
        halves = []
        for h in range(2):
            at = 2 * h
            halves.append((got[it, at] + got[it, at + 1]) + (got[it, at + 4] + got[it, at + 5]))
        sums = jnp.sum(halves[0][FAR_DEV:] + halves[1][FAR_DEV:], axis=1, keepdims=True)
        far_v = split(jnp.concatenate([half[:FAR_DEV] for half in halves], axis=1))
        coef = dot_rows(far_v, right[...])
        coef = fold(weight_d[...] * (coef[:FAR_DEV] + coef[FAR_DEV:]))
        to_own = dot(split(hit_t[...] * coef), left[...])
        return to_own[:BLK_DEV] + to_own[BLK_DEV:], sums

    def near(it):
        wait_for(span.at[it, pl.ds(0, RIM)], step_sem.at[it, 5], False)
        wait_for(span.at[it, pl.ds(0, RIM)], step_sem.at[it, 7], False)
        vectors = []
        for way in range(2):
            rows = [
                span[it, pl.ds(jnp.clip(near_smem[way, k] - first + RIM, 0, SLOTS - 1), 1), :]
                for k in range(NEAR_DEV)
            ]
            vectors.append(split(jnp.concatenate(rows, axis=0)))
        for k in range(NEAR_DEV):
            for way, multiply in enumerate((dot_rows, dot)):
                image = multiply(vectors[way], tiles[k, 0]) + multiply(vectors[way], tiles[k, 1])
                at = way * NEAR_DEV + k
                rows_n[at : at + 1, :] = image[k : k + 1] + image[NEAR_DEV + k : NEAR_DEV + k + 1]
        slot = lax.broadcasted_iota(jnp.int32, (SLOTS, NEAR_DEV), 0)
        hits = [(slot == near_ref[way : way + 1, :] - first + RIM).astype(F32) for way in (1, 0)]
        hits = jnp.concatenate(hits, axis=1).astype(BF16)
        value = 0.0
        for part in parts(rows_n[...], 3):
            value = value + dot(hits, part)
        rim[it, 0] = value
        send(
            rim.at[it, 0, pl.ds(0, RIM)], rim.at[it, 1, pl.ds(RIM, RIM)],
            step_sem.at[it, 12], step_sem.at[it, 13], down,
        ).start()
        send(
            rim.at[it, 0, pl.ds(RIM + BLK_DEV, RIM)], rim.at[it, 1, pl.ds(0, RIM)],
            step_sem.at[it, 14], step_sem.at[it, 15], up,
        ).start()

    def join(it, far_own):
        wait_for(rim.at[it, 1, pl.ds(0, RIM)], step_sem.at[it, 13], False)
        wait_for(rim.at[it, 1, pl.ds(0, RIM)], step_sem.at[it, 15], False)
        local = far_own + rim[it, 0, RIM : RIM + BLK_DEV, :] + rim[it, 1, 0:BLK_DEV, :]
        wait_for(landed.at[it, pl.ds(0, ROWS - 4)], step_sem.at[it, 9], False)
        image = jnp.sum(landed[it].reshape(ROWS // 8, 8, 128), axis=0)
        image = image[:4] + image[4:]
        image = jnp.concatenate([image, image], axis=0)
        image = jnp.concatenate([image, image], axis=1)
        at_row = lax.broadcasted_iota(jnp.int32, (BLK_DEV, BS), 0) // 4
        at_half = lax.broadcasted_iota(jnp.int32, (BLK_DEV, BS), 1) // 128
        joined[it, me] = local + jnp.where(2 * at_row + at_half == x, image, 0.0)
        for to in joins[it]:
            send(joined.at[it, me], joined.at[it, me], step_sem.at[it, 16], step_sem.at[it, 17], to).start()
        wait_for(joined.at[it, pl.ds(0, len(joins[it]))], step_sem.at[it, 17], False)

    def pair_sum(it, c):
        return (joined[it, c] + joined[it, 2 + c]) + (joined[it, 4 + c] + joined[it, 6 + c])

    def sent(it):
        wait_for(taken.at[it, pl.ds(0, COLUMN - 1)], step_sem.at[it, 0], True)
        wait_for(quarter.at[it, pl.ds(0, ROWS - 4)], step_sem.at[it, 2], True)
        wait_for(span.at[it, pl.ds(0, RIM)], step_sem.at[it, 4], True)
        wait_for(span.at[it, pl.ds(0, RIM)], step_sem.at[it, 6], True)
        wait_for(landed.at[it, pl.ds(0, ROWS - 4)], step_sem.at[it, 8], True)
        wait_for(got.at[it, pl.ds(0, COLUMN - 1)], step_sem.at[it, 10], True)
        wait_for(rim.at[it, 1, pl.ds(0, RIM)], step_sem.at[it, 12], True)
        wait_for(rim.at[it, 1, pl.ds(0, RIM)], step_sem.at[it, 14], True)
        wait_for(joined.at[it, pl.ds(0, len(joins[it]))], step_sem.at[it, 16], True)

    def build(k, _):
        source = jnp.clip(near_smem[0, k] - first + RIM, 0, SLOTS - 1)
        target = jnp.clip(near_smem[1, k] - first, 0, BLK_DEV - 1)
        line = [hc[d, pl.ds(source, 1), :] for d in range(3)]
        for r in range(0, BS, 64):
            col = [cbc[target, d, r : r + 64, :] for d in range(3)]
            for h in range(2):
                dist = SOFT_SQ
                for d in range(3):
                    diff = col[d] - line[d][:, 128 * h : 128 * h + 128]
                    dist = dist + diff * diff
                tile = (NEAR_GAIN / BS) * lax.rsqrt(dist)
                high = tile.astype(BF16)
                tiles[k, 0, r : r + 64, 128 * h : 128 * h + 128] = high
                tiles[k, 1, r : r + 64, 128 * h : 128 * h + 128] = (tile - high.astype(F32)).astype(BF16)
        return 0

    give(0, b_own)
    for d in range(3):
        hct[pl.ds(BLK_DEV * d, BLK_DEV), :] = hc[d, RIM : RIM + BLK_DEV, :]
    turned = hct[...].T
    for b in range(BLK_DEV):
        for d in range(3):
            at = BLK_DEV * d + b
            cbc[b, d] = jnp.broadcast_to(turned[:, at : at + 1], (BS, 128))
    pl.semaphore_wait(barrier, N_YZ - 1 + COLUMN - 1 + 2)

    for number, half, to in column:
        send(keys.at[me], keys.at[me], once_sem.at[0], once_sem.at[1], to).start()
    give_start(0)
    halo_up = send(hc.at[:, pl.ds(BLK_DEV, RIM)], hc.at[:, pl.ds(0, RIM)], once_sem.at[2], once_sem.at[3], up)
    halo_down = send(
        hc.at[:, pl.ds(RIM, RIM)], hc.at[:, pl.ds(RIM + BLK_DEV, RIM)], once_sem.at[4], once_sem.at[5], down
    )
    gather_start(0)
    halo_up.start()
    halo_down.start()
    span_start(0)
    constants = shared.at[core, pl.ds(0, 2)]
    send(constants, constants, once_sem.at[6], once_sem.at[7], twin).start()
    wait_for(keys.at[pl.ds(0, COLUMN - 1)], once_sem.at[1], False)
    key = keys[0]
    for g in range(1, COLUMN):
        key = key + keys[g]
    key = (key[0:1] + 0.5).astype(jnp.int32)
    row = lax.broadcasted_iota(jnp.int32, (ROWS, COLUMN * FAR_DEV), 0)
    block = (row // 4) * 16 + core * 8 + (x // 2) * 4 + row % 4
    hits = (block == key).astype(F32)
    hot[...] = hits.astype(BF16)
    hot_t[...] = hits.T.astype(BF16)
    scatter_plane(0)

    halo_up.wait_recv()
    halo_down.wait_recv()
    lax.fori_loop(0, NEAR_DEV // 2, build, 0)
    gather_column(0, ((0, 0),))
    lax.fori_loop(NEAR_DEV // 2, NEAR_DEV, build, 0)
    near(0)
    far_own, sums = gather_end(0)
    beta = jnp.sqrt(sums[0:1])
    inv_beta = 1.0 / beta
    join(0, far_own)
    w_own = (pair_sum(0, core) + diag * b_own) * inv_beta

    span[1, RIM : RIM + BLK_DEV, :] = w_own
    quarter[1, mine, :] = own_quarter(w_own)
    give(1, w_own)
    give_start(1)
    span_start(1)
    gather_start(1)
    shared[core, 2] = w_own
    krylov = shared.at[core, pl.ds(2, 1)]
    send(krylov, krylov, once_sem.at[8], once_sem.at[9], twin).start()
    wait_for(constants, once_sem.at[6], True)
    wait_for(keys.at[pl.ds(0, COLUMN - 1)], once_sem.at[0], True)
    halo_up.wait_send()
    halo_down.wait_send()
    sent(0)
    scatter_plane(1)
    near(1)
    gather_column(1, ((0, 1), (1, 1)))
    far_own, sums = gather_end(1)
    h00 = sums[0:1] * inv_beta
    shift = sums[1:2] - h00 * h00
    alpha = h00 * inv_beta
    wait_for(constants, once_sem.at[7], False)
    wait_for(krylov, once_sem.at[9], False)
    wait_for(krylov, once_sem.at[8], True)
    v0 = shared[:, 0] * inv_beta
    w = shared[:, 2]
    u = w - h00 * v0
    known = shared[:, 1] * w - h00 * w - shift * v0 - h00 * u
    join(1, far_own)
    rest = jnp.stack([pair_sum(1, c) for c in range(2)]) + known

    def lanes(value):
        value = fold(value.reshape(2 * BLK_DEV, BS))
        return value[:, :128] + value[:, 128:]

    sums_yz[mine, :] = jnp.concatenate(
        [lanes(rest * rest), lanes(rest * v0), lanes(rest * u), lanes(u * u)], axis=0
    )
    own_sums = sums_yz.at[mine]
    plane(lambda there: (own_sums, own_sums), (sums_sem.at[0], sums_sem.at[1]))
    sent(1)
    wait_for(sums_yz.at[pl.ds(0, ROWS - 4)], sums_sem.at[1], False)
    wait_for(sums_yz.at[pl.ds(0, ROWS - 4)], sums_sem.at[0], True)
    acc = jnp.sum(sums_yz[...].reshape(ROWS // 8, 8, 128), axis=0)
    acc = jnp.sum(acc[:4] + acc[4:], axis=1, keepdims=True)
    sq, a0, a1, uu = acc[0:1], acc[1:2], acc[2:3], acc[3:4]
    h10 = jnp.sqrt(uu)
    inv_h10 = 1.0 / h10
    a1 = a1 * inv_h10
    h01 = (shift + a0) * inv_h10
    h11 = h00 + a1 * inv_h10
    h21 = jnp.sqrt(jnp.maximum(sq - a0 * a0 - a1 * a1, 0.0)) * inv_h10

    rho0 = jnp.sqrt(h00 * h00 + h10 * h10)
    c0 = h00 / rho0
    s0 = h10 / rho0
    r01 = c0 * h01 + s0 * h11
    r11 = c0 * h11 - s0 * h01
    rho1 = jnp.sqrt(r11 * r11 + h21 * h21)
    c1 = r11 / rho1
    s1 = h21 / rho1
    g0 = c0 * beta
    g1 = -s0 * beta
    y1 = c1 * g1 / rho1
    y0 = (g0 - r01 * y1) / rho0
    norm_ref[...] = jnp.abs(s1 * g1)
    u_own = w_own - alpha * b_own
    answer = (y0 * inv_beta) * b_own + (y1 * inv_h10) * u_own
    for h in range(2):
        out_ref[pl.ds(h, BLK_DEV, stride=2), :] = answer[:, 128 * h : 128 * h + 128]


def body(
    right_side, coords, diagonal, near_pairs, far_pairs, far_rank, far_left, far_right, far_scale
):
    vmem = pl.BlockSpec(memory_space=pltpu.VMEM)
    smem = pl.BlockSpec(memory_space=pltpu.SMEM)
    hbm = pl.BlockSpec(memory_space=pltpu.HBM)
    width = COLUMN * FAR_DEV
    scratch = [
        pltpu.VMEM((FACT, BS), BF16),
        pltpu.VMEM((FACT, BS), BF16),
        pltpu.VMEM((16, 128), F32),
        pltpu.VMEM((3, BLK_DEV * BS), F32),
        pltpu.VMEM((16, 128), F32),
        pltpu.VMEM((2, NEAR_DEV), jnp.int32),
        pltpu.VMEM((2, FAR_DEV), jnp.int32),
        pltpu.VMEM((1, FAR_DEV), jnp.int32),
        pltpu.VMEM((FAR_DEV, RMAX), F32),
        pltpu.VMEM((3, SLOTS, BS), F32),
        pltpu.VMEM((3 * BLK_DEV, BS), F32),
        pltpu.VMEM((BLK_DEV, 3, BS, 128), F32),
        pltpu.VMEM((NEAR_DEV, 2, BS, BS), BF16),
        pltpu.VMEM((COLUMN, 8, width), F32),
        pltpu.VMEM((ROWS, width), BF16),
        pltpu.VMEM((width, ROWS), BF16),
        pltpu.VMEM((FAR_DEV, FACT), F32),
        pltpu.VMEM((BLK_DEV, FACT), F32),
        pltpu.VMEM((2, ROWS, 128), F32),
        pltpu.VMEM((2, COLUMN, FAR_DEV + EXTRA, 128), F32),
        pltpu.VMEM((2, COLUMN, FAR_DEV + EXTRA, 128), F32),
        pltpu.VMEM((2, 2, FAR_DEV, 128), F32),
        pltpu.VMEM((2, COLUMN, FAR_DEV, 128), F32),
        pltpu.VMEM((2, ROWS, 128), F32),
        pltpu.VMEM((2, ROWS, 128), F32),
        pltpu.VMEM((2, SLOTS, BS), F32),
        pltpu.VMEM((2, 2, SLOTS, BS), F32),
        pltpu.VMEM((2, COLUMN, BLK_DEV, BS), F32),
        pltpu.VMEM((2 * NEAR_DEV, BS), F32),
        pltpu.VMEM((2, 3, BLK_DEV, BS), F32),
        pltpu.VMEM((ROWS, 128), F32),
        pltpu.SemaphoreType.DMA((9,)),
        pltpu.SemaphoreType.DMA((10,)),
        pltpu.SemaphoreType.DMA((2, 18)),
        pltpu.SemaphoreType.DMA((2,)),
    ]
    solution, norm = pl.pallas_call(
        kernel,
        out_shape=(
            jax.ShapeDtypeStruct((16, 128), F32),
            jax.ShapeDtypeStruct((1, 1), F32),
        ),
        in_specs=[smem] + [hbm] * 9,
        out_specs=(vmem, vmem),
        scratch_shapes=scratch,
        compiler_params=pltpu.CompilerParams(
            collective_id=0, has_side_effects=True, vmem_limit_bytes=60 * 1024 * 1024
        ),
        cost_estimate=pl.CostEstimate(flops=100_000_000, bytes_accessed=2_000_000, transcendentals=2_000_000),
        name="gmres",
    )(
        near_pairs, right_side.reshape(16, 128), coords, diagonal.reshape(16, 128), near_pairs,
        far_pairs, far_rank.reshape(1, FAR_DEV), far_scale, far_left.reshape(FACT, BS),
        far_right.reshape(FACT, BS),
    )
    return solution.reshape(BLK_DEV * BS), norm.reshape(())


def solution(mesh):
    placed = (
        P("patch"),
        P(None, "patch"),
        P("patch"),
        P(None, ("patch", "pair")),
        P(None, ("patch", "pair")),
        P(("patch", "pair")),
        P(("patch", "pair"), None, None),
        P(("patch", "pair"), None, None),
        P(("patch", "pair"), None),
    )
    return jax.shard_map(
        body, mesh=mesh, in_specs=placed, out_specs=(P("patch"), P()), check_vma=False
    )
```

```python
import functools

import jax
import jax.numpy as jnp
from jax import lax
from jax.experimental import pallas as pl
from jax.experimental.pallas import tpu as pltpu
from jax.sharding import PartitionSpec as P

BS = 256
BLK_DEV = 8
RIM = 4
RMAX = 32
NEAR_DEV = 16
FAR_DEV = 32
NEAR_GAIN = 2.0
SOFT_SQ = 0.25

N_Y, N_Z, N_X = 8, 8, 4
N_YZ = N_Y * N_Z
ROWS = 4 * N_YZ
COLUMN = 2 * N_X
SLOTS = BLK_DEV + 2 * RIM
FACT = FAR_DEV * RMAX
EXTRA = 8

MESH = pl.DeviceIdType.MESH
HIGH = lax.Precision.HIGHEST
F32 = jnp.float32
BF16 = jnp.bfloat16


def place():
    patch = lax.axis_index("patch")
    return lax.axis_index("pair"), patch // (2 * N_Z), (patch // 2) % N_Z, patch % 2


def device(x, y, z, core):
    return {"patch": (y * N_Z + z) * 2 + core, "pair": x}


def send(src, dst, send_sem, recv_sem, to):
    return pltpu.make_async_remote_copy(
        src_ref=src, dst_ref=dst, send_sem=send_sem, recv_sem=recv_sem, device_id=to, device_id_type=MESH
    )


def far_first(n):
    return sorted(range(n), key=lambda d: -min(d, n - d))


def parts(value, count):
    found = []
    for _ in range(count):
        found.append(value.astype(BF16))
        value = value - found[-1].astype(F32)
    return found


def split(value):
    return jnp.concatenate(parts(value, 2), axis=0)


def dot(a, b):
    return jnp.dot(a, b, preferred_element_type=F32)


def dot_rows(a, b):
    return lax.dot_general(a, b, (((1,), (1,)), ((), ())), preferred_element_type=F32)


def fold(value):
    return jnp.sum(value, axis=0, keepdims=True)


def total(value):
    return jnp.sum(fold(value), axis=1, keepdims=True)


def kernel(
    near_smem, right_hbm, coords_hbm, diag_hbm, near_hbm, far_hbm, rank_hbm, scale_hbm, left_hbm, factor_hbm,
    out_ref, norm_ref,
    left, right, right_ref, coords_ref, diag_ref, near_ref, far_ref, rank_ref, scale_ref,
    hc, hct, cbc, tiles, keys, hot, hot_t, weight_d, hit_t,
    quarter, picked, got, given, taken, spread, landed, span, rim, rim_in, joined,
    rows_n, shared, sums_yz,
    local_sem, once_sem, step_sem, sums_sem,
):
    x, y, z, core = place()
    patch = lax.axis_index("patch")
    n_patch = 2 * N_YZ
    first = patch * BLK_DEV
    yz = y * N_Z + z
    me = 2 * x + core
    mine = pl.ds(pl.multiple_of(yz * 4, 4), 4)
    up = {"patch": (patch + 1) % n_patch, "pair": x}
    down = {"patch": (patch + n_patch - 1) % n_patch, "pair": x}
    rims = ([(x + i) % N_X for i in range(N_X)], [x])
    twin = device(x, y, z, 1 - core)
    column = []
    for i in (4, 5, 2, 3, 6, 7, 1):
        other_x, other_core = (x + i // 2) % N_X, (core + i) % 2
        column.append((2 * other_x + other_core, other_x % 2, device(other_x, y, z, other_core)))

    joins = ([device((x + i) % N_X, y, z, core) for i in (2, 1, 3)], [to for _, _, to in column])

    barrier = pltpu.get_barrier_semaphore()

    z_peers = [((z + d) % N_Z, d) for d in far_first(N_Z)]

    def over_plane(act, begin=0, end=N_Y):
        def rows(k, _):
            other_y = (y + N_Y // 2 + ((k + 1) // 2) * (1 - 2 * (k % 2))) % N_Y
            for other_z, _ in z_peers:
                act(other_y, other_z)
            return 0

        lax.fori_loop(begin, min(end, N_Y - 1), rows, 0)
        if end == N_Y:
            for other_z, d in z_peers:
                if d:
                    act(y, other_z)

    def greet(other_y, other_z):
        pl.semaphore_signal(
            barrier, inc=1, device_id=device(x, other_y, other_z, core), device_id_type=MESH
        )

    over_plane(greet)
    for _, _, to in column:
        pl.semaphore_signal(barrier, inc=1, device_id=to, device_id_type=MESH)
    for other in rims[0]:
        for to in (up, down):
            pl.semaphore_signal(
                barrier, inc=1, device_id={"patch": to["patch"], "pair": other}, device_id_type=MESH
            )
    loads = [
        pltpu.make_async_copy(src, dst, local_sem.at[i])
        for i, (src, dst) in enumerate(
            (
                (left_hbm, left), (factor_hbm, right), (right_hbm, right_ref), (coords_hbm, coords_ref),
                (diag_hbm, diag_ref), (near_hbm, near_ref), (far_hbm, far_ref), (rank_hbm, rank_ref),
                (scale_hbm, scale_ref),
            )
        )
    ]
    for load in loads:
        load.start()
    for load in loads:
        load.wait()

    def natural(ref):
        return jnp.concatenate([ref[pl.ds(h, BLK_DEV, stride=2), :] for h in range(2)], axis=1)

    def own_quarter(value):
        found = value[:4, :128]
        for q in range(1, N_X):
            a, h = q // 2, q % 2
            found = jnp.where(x == q, value[4 * a : 4 * a + 4, 128 * h : 128 * h + 128], found)
        return found

    b_own = natural(right_ref)
    diag = natural(diag_ref)
    span[0, RIM : RIM + BLK_DEV, :] = b_own
    shared[core, 0] = b_own
    shared[core, 1] = diag
    quarter[0, mine, :] = own_quarter(b_own)
    for d in range(3):
        for b in range(BLK_DEV):
            hc[d, RIM + b : RIM + b + 1, :] = coords_ref[d : d + 1, b * BS : (b + 1) * BS]

    near_f = near_ref[...].astype(F32)
    far_f = far_ref[...].astype(F32)
    sub_key = lax.broadcasted_iota(jnp.int32, (FAR_DEV, COLUMN * FAR_DEV), 0)
    lane_key = lax.broadcasted_iota(jnp.int32, (FAR_DEV, COLUMN * FAR_DEV), 1)
    pick = (lane_key == sub_key + me * FAR_DEV).astype(F32)
    laid = jnp.dot(far_f, pick, precision=HIGH, preferred_element_type=F32)
    keys[me] = jnp.broadcast_to(laid[0:1], (8, COLUMN * FAR_DEV))

    pair_of = lax.broadcasted_iota(jnp.int32, (FAR_DEV, FACT), 1) // RMAX
    term_of = lax.broadcasted_iota(jnp.int32, (FAR_DEV, FACT), 1) % RMAX
    sub = lax.broadcasted_iota(jnp.int32, (FAR_DEV, FACT), 0)
    eye = lax.broadcasted_iota(jnp.int32, (FAR_DEV, FAR_DEV), 0) == lax.broadcasted_iota(
        jnp.int32, (FAR_DEV, FAR_DEV), 1
    )
    rank_col = jnp.sum(jnp.where(eye, rank_ref[...].astype(F32), 0.0), axis=1, keepdims=True)
    term = lax.broadcasted_iota(jnp.int32, (FAR_DEV, RMAX), 1).astype(F32)
    weights = jnp.where(term < rank_col, scale_ref[...], 0.0)
    spread_w = jnp.dot(weights, (sub == term_of).astype(F32), precision=HIGH, preferred_element_type=F32)
    weight_d[...] = jnp.where(sub == pair_of, spread_w, 0.0)
    target_row = far_ref[1:2, :] - first
    onto = (lax.broadcasted_iota(jnp.int32, (BLK_DEV, FAR_DEV), 0) == target_row).astype(F32)
    hit_t[...] = jnp.dot(onto, (sub == pair_of).astype(F32), preferred_element_type=F32)

    def wait_for(view, sem, sent):
        copy = send(view, view, sem, sem, twin)
        if sent:
            copy.wait_send()
        else:
            copy.wait_recv()

    def plane(step, sems, begin=0, end=N_Y):
        def each(other_y, other_z):
            src, dst = step(other_y * N_Z + other_z)
            send(src, dst, sems[0], sems[1], device(x, other_y, other_z, core)).start()

        over_plane(each, begin, end)

    def give(it, own_value):
        back = dot_rows(split(own_value), left[...])
        back = fold(hit_t[...] * (back[:BLK_DEV] + back[BLK_DEV:]))
        to_far = dot(split(weight_d[...] * back), right[...])
        to_far = to_far[:FAR_DEV] + to_far[FAR_DEV:]
        for h in range(2):
            given[it, h] = to_far[:, 128 * h : 128 * h + 128]
        taken[it, me] = given[it, x % 2]

    def give_start(it):
        for number, half, to in column:
            send(given.at[it, half], taken.at[it, me], step_sem.at[it, 0], step_sem.at[it, 1], to).start()

    def gather_start(it, begin, end):
        own_rows = quarter.at[it, mine]
        plane(lambda there: (own_rows, own_rows), (step_sem.at[it, 2], step_sem.at[it, 3]), begin, end)

    def span_start(it):
        send(
            span.at[it, pl.ds(BLK_DEV, RIM)], span.at[it, pl.ds(0, RIM)],
            step_sem.at[it, 4], step_sem.at[it, 5], up,
        ).start()
        send(
            span.at[it, pl.ds(RIM, RIM)], span.at[it, pl.ds(RIM + BLK_DEV, RIM)],
            step_sem.at[it, 6], step_sem.at[it, 7], down,
        ).start()

    def scatter_plane(it):
        wait_for(taken.at[it, pl.ds(0, COLUMN - 1)], step_sem.at[it, 1], False)
        value = 0.0
        for part in parts(taken[it].reshape(COLUMN * FAR_DEV, 128), 2):
            value = value + dot(hot[...], part)
        spread[it] = value
        landed[it, mine, :] = spread[it, mine, :]
        plane(
            lambda there: (spread.at[it, pl.ds(pl.multiple_of(there * 4, 4), 4)], landed.at[it, mine]),
            (step_sem.at[it, 8], step_sem.at[it, 9]),
        )

    def gather_column(it, extras):
        wait_for(quarter.at[it, pl.ds(0, ROWS - 4)], step_sem.at[it, 3], False)
        value = 0.0
        for part in parts(quarter[it], 2):
            value = value + dot(hot_t[...], part)
        picked[it, :, pl.ds(0, FAR_DEV), :] = value.reshape(COLUMN, FAR_DEV, 128)
        sums = [fold(quarter[i] * quarter[j]) for i, j in extras]
        sums = jnp.concatenate(sums + [jnp.zeros((EXTRA - len(sums), 128), F32)], axis=0)
        for g in range(COLUMN):
            picked[it, g, pl.ds(FAR_DEV, EXTRA), :] = sums
        got[it, me] = picked[it, me]
        for number, half, to in column:
            send(picked.at[it, number], got.at[it, me], step_sem.at[it, 10], step_sem.at[it, 11], to).start()

    def gather_end(it):
        wait_for(got.at[it, pl.ds(0, COLUMN - 1)], step_sem.at[it, 11], False)
        halves = []
        for h in range(2):
            at = 2 * h
            halves.append((got[it, at] + got[it, at + 1]) + (got[it, at + 4] + got[it, at + 5]))
        sums = jnp.sum(halves[0][FAR_DEV:] + halves[1][FAR_DEV:], axis=1, keepdims=True)
        far_v = split(jnp.concatenate([half[:FAR_DEV] for half in halves], axis=1))
        coef = dot_rows(far_v, right[...])
        coef = fold(weight_d[...] * (coef[:FAR_DEV] + coef[FAR_DEV:]))
        to_own = dot(split(hit_t[...] * coef), left[...])
        return to_own[:BLK_DEV] + to_own[BLK_DEV:], sums

    def near(it):
        wait_for(span.at[it, pl.ds(0, RIM)], step_sem.at[it, 5], False)
        wait_for(span.at[it, pl.ds(0, RIM)], step_sem.at[it, 7], False)
        vectors = []
        for way in range(2):
            rows = [
                span[it, pl.ds(jnp.clip(near_smem[way, k] - first + RIM, 0, SLOTS - 1), 1), :]
                for k in range(NEAR_DEV)
            ]
            vectors.append(split(jnp.concatenate(rows, axis=0)))
        for k in range(NEAR_DEV):
            for way, multiply in enumerate((dot_rows, dot)):
                image = multiply(vectors[way], tiles[k, 0]) + multiply(vectors[way], tiles[k, 1])
                at = way * NEAR_DEV + k
                rows_n[at : at + 1, :] = image[k : k + 1] + image[NEAR_DEV + k : NEAR_DEV + k + 1]
        slot = lax.broadcasted_iota(jnp.int32, (SLOTS, NEAR_DEV), 0)
        hits = [(slot == near_ref[way : way + 1, :] - first + RIM).astype(F32) for way in (1, 0)]
        hits = jnp.concatenate(hits, axis=1).astype(BF16)
        value = 0.0
        for part in parts(rows_n[...], 3):
            value = value + dot(hits, part)
        rim[it] = value
        for other in rims[it]:
            send(
                rim.at[it, pl.ds(0, RIM)], rim_in.at[it, x, pl.ds(RIM, RIM)],
                step_sem.at[it, 12], step_sem.at[it, 13], {"patch": down["patch"], "pair": other},
            ).start()
            send(
                rim.at[it, pl.ds(RIM + BLK_DEV, RIM)], rim_in.at[it, x, pl.ds(0, RIM)],
                step_sem.at[it, 14], step_sem.at[it, 15], {"patch": up["patch"], "pair": other},
            ).start()

    def rim_wait(it, at, sent):
        wait_for(rim.at[it, pl.ds(0, RIM * len(rims[it]))], step_sem.at[it, at], sent)

    def join(it, far_own):
        local = far_own + rim[it, RIM : RIM + BLK_DEV, :]
        if len(rims[it]) == 1:
            rim_wait(it, 13, False)
            rim_wait(it, 15, False)
            local = local + rim_in[it, x]
        wait_for(landed.at[it, pl.ds(0, ROWS - 4)], step_sem.at[it, 9], False)
        image = jnp.sum(landed[it].reshape(ROWS // 8, 8, 128), axis=0)
        image = image[:4] + image[4:]
        image = jnp.concatenate([image, image], axis=0)
        image = jnp.concatenate([image, image], axis=1)
        at_row = lax.broadcasted_iota(jnp.int32, (BLK_DEV, BS), 0) // 4
        at_half = lax.broadcasted_iota(jnp.int32, (BLK_DEV, BS), 1) // 128
        joined[it, me] = local + jnp.where(2 * at_row + at_half == x, image, 0.0)
        for to in joins[it]:
            send(joined.at[it, me], joined.at[it, me], step_sem.at[it, 16], step_sem.at[it, 17], to).start()
        wait_for(joined.at[it, pl.ds(0, len(joins[it]))], step_sem.at[it, 17], False)

    def pair_sum(it, c):
        return (joined[it, c] + joined[it, 2 + c]) + (joined[it, 4 + c] + joined[it, 6 + c])

    def sent(it):
        wait_for(taken.at[it, pl.ds(0, COLUMN - 1)], step_sem.at[it, 0], True)
        wait_for(quarter.at[it, pl.ds(0, ROWS - 4)], step_sem.at[it, 2], True)
        wait_for(span.at[it, pl.ds(0, RIM)], step_sem.at[it, 4], True)
        wait_for(span.at[it, pl.ds(0, RIM)], step_sem.at[it, 6], True)
        wait_for(landed.at[it, pl.ds(0, ROWS - 4)], step_sem.at[it, 8], True)
        wait_for(got.at[it, pl.ds(0, COLUMN - 1)], step_sem.at[it, 10], True)
        rim_wait(it, 12, True)
        rim_wait(it, 14, True)
        wait_for(joined.at[it, pl.ds(0, len(joins[it]))], step_sem.at[it, 16], True)

    def build(k, _):
        source = jnp.clip(near_smem[0, k] - first + RIM, 0, SLOTS - 1)
        target = jnp.clip(near_smem[1, k] - first, 0, BLK_DEV - 1)
        line = [hc[d, pl.ds(source, 1), :] for d in range(3)]
        for r in range(0, BS, 64):
            col = [cbc[target, d, r : r + 64, :] for d in range(3)]
            for h in range(2):
                dist = SOFT_SQ
                for d in range(3):
                    diff = col[d] - line[d][:, 128 * h : 128 * h + 128]
                    dist = dist + diff * diff
                tile = (NEAR_GAIN / BS) * lax.rsqrt(dist)
                high = tile.astype(BF16)
                tiles[k, 0, r : r + 64, 128 * h : 128 * h + 128] = high
                tiles[k, 1, r : r + 64, 128 * h : 128 * h + 128] = (tile - high.astype(F32)).astype(BF16)
        return 0

    give(0, b_own)
    for d in range(3):
        hct[pl.ds(BLK_DEV * d, BLK_DEV), :] = hc[d, RIM : RIM + BLK_DEV, :]
    turned = hct[...].T
    for b in range(BLK_DEV):
        for d in range(3):
            at = BLK_DEV * d + b
            cbc[b, d] = jnp.broadcast_to(turned[:, at : at + 1], (BS, 128))
    pl.semaphore_wait(barrier, N_YZ - 1 + COLUMN - 1 + 2 * N_X)

    gather_start(0, 0, 2)
    for number, half, to in column:
        send(keys.at[me], keys.at[me], once_sem.at[0], once_sem.at[1], to).start()
    give_start(0)
    halo_up = send(hc.at[:, pl.ds(BLK_DEV, RIM)], hc.at[:, pl.ds(0, RIM)], once_sem.at[2], once_sem.at[3], up)
    halo_down = send(
        hc.at[:, pl.ds(RIM, RIM)], hc.at[:, pl.ds(RIM + BLK_DEV, RIM)], once_sem.at[4], once_sem.at[5], down
    )
    halo_up.start()
    halo_down.start()
    gather_start(0, 2, N_Y)
    span_start(0)
    constants = shared.at[core, pl.ds(0, 2)]
    send(constants, constants, once_sem.at[6], once_sem.at[7], twin).start()
    halo_up.wait_recv()
    halo_down.wait_recv()
    lax.fori_loop(0, 8, build, 0)
    wait_for(keys.at[pl.ds(0, COLUMN - 1)], once_sem.at[1], False)
    key = keys[0]
    for g in range(1, COLUMN):
        key = key + keys[g]
    key = (key[0:1] + 0.5).astype(jnp.int32)
    row = lax.broadcasted_iota(jnp.int32, (ROWS, COLUMN * FAR_DEV), 0)
    block = (row // 4) * 16 + core * 8 + (x // 2) * 4 + row % 4
    hits = (block == key).astype(F32)
    hot[...] = hits.astype(BF16)
    hot_t[...] = hits.T.astype(BF16)
    scatter_plane(0)

    lax.fori_loop(8, 14, build, 0)
    gather_column(0, ((0, 0),))
    lax.fori_loop(14, NEAR_DEV, build, 0)
    near(0)
    far_own, sums = gather_end(0)
    beta = jnp.sqrt(sums[0:1])
    inv_beta = 1.0 / beta
    join(0, far_own)
    rim_wait(0, 13, False)
    rim_wait(0, 15, False)
    from_rims = (rim_in[0, 0] + rim_in[0, 1]) + (rim_in[0, 2] + rim_in[0, 3])
    w_own = (pair_sum(0, core) + from_rims + diag * b_own) * inv_beta

    span[1, RIM : RIM + BLK_DEV, :] = w_own
    quarter[1, mine, :] = own_quarter(w_own)
    gather_start(1, 0, 2)
    give(1, w_own)
    give_start(1)
    gather_start(1, 2, N_Y)
    span_start(1)
    shared[core, 2] = w_own
    krylov = shared.at[core, pl.ds(2, 1)]
    send(krylov, krylov, once_sem.at[8], once_sem.at[9], twin).start()
    wait_for(constants, once_sem.at[6], True)
    wait_for(keys.at[pl.ds(0, COLUMN - 1)], once_sem.at[0], True)
    halo_up.wait_send()
    halo_down.wait_send()
    sent(0)
    scatter_plane(1)
    near(1)
    gather_column(1, ((0, 1), (1, 1)))
    far_own, sums = gather_end(1)
    h00 = sums[0:1] * inv_beta
    shift = sums[1:2] - h00 * h00
    alpha = h00 * inv_beta
    wait_for(constants, once_sem.at[7], False)
    wait_for(krylov, once_sem.at[9], False)
    wait_for(krylov, once_sem.at[8], True)
    v0 = shared[:, 0] * inv_beta
    w = shared[:, 2]
    u = w - h00 * v0
    known = shared[:, 1] * w - h00 * w - shift * v0 - h00 * u
    join(1, far_own)
    rest = jnp.stack([pair_sum(1, c) for c in range(2)]) + known

    def lanes(value):
        value = fold(value.reshape(2 * BLK_DEV, BS))
        return value[:, :128] + value[:, 128:]

    sums_yz[mine, :] = jnp.concatenate(
        [lanes(rest * rest), lanes(rest * v0), lanes(rest * u), lanes(u * u)], axis=0
    )
    own_sums = sums_yz.at[mine]
    plane(lambda there: (own_sums, own_sums), (sums_sem.at[0], sums_sem.at[1]))
    sent(1)
    wait_for(sums_yz.at[pl.ds(0, ROWS - 4)], sums_sem.at[1], False)
    wait_for(sums_yz.at[pl.ds(0, ROWS - 4)], sums_sem.at[0], True)
    acc = jnp.sum(sums_yz[...].reshape(ROWS // 8, 8, 128), axis=0)
    acc = jnp.sum(acc[:4] + acc[4:], axis=1, keepdims=True)
    sq, a0, a1, uu = acc[0:1], acc[1:2], acc[2:3], acc[3:4]
    h10 = jnp.sqrt(uu)
    inv_h10 = 1.0 / h10
    a1 = a1 * inv_h10
    h01 = (shift + a0) * inv_h10
    h11 = h00 + a1 * inv_h10
    h21 = jnp.sqrt(jnp.maximum(sq - a0 * a0 - a1 * a1, 0.0)) * inv_h10

    rho0 = jnp.sqrt(h00 * h00 + h10 * h10)
    c0 = h00 / rho0
    s0 = h10 / rho0
    r01 = c0 * h01 + s0 * h11
    r11 = c0 * h11 - s0 * h01
    rho1 = jnp.sqrt(r11 * r11 + h21 * h21)
    c1 = r11 / rho1
    s1 = h21 / rho1
    g0 = c0 * beta
    g1 = -s0 * beta
    y1 = c1 * g1 / rho1
    y0 = (g0 - r01 * y1) / rho0
    norm_ref[...] = jnp.abs(s1 * g1)
    u_own = w_own - alpha * b_own
    answer = (y0 * inv_beta) * b_own + (y1 * inv_h10) * u_own
    for h in range(2):
        out_ref[pl.ds(h, BLK_DEV, stride=2), :] = answer[:, 128 * h : 128 * h + 128]


def body(
    right_side, coords, diagonal, near_pairs, far_pairs, far_rank, far_left, far_right, far_scale
):
    vmem = pl.BlockSpec(memory_space=pltpu.VMEM)
    smem = pl.BlockSpec(memory_space=pltpu.SMEM)
    hbm = pl.BlockSpec(memory_space=pltpu.HBM)
    width = COLUMN * FAR_DEV
    scratch = [
        pltpu.VMEM((FACT, BS), BF16),
        pltpu.VMEM((FACT, BS), BF16),
        pltpu.VMEM((16, 128), F32),
        pltpu.VMEM((3, BLK_DEV * BS), F32),
        pltpu.VMEM((16, 128), F32),
        pltpu.VMEM((2, NEAR_DEV), jnp.int32),
        pltpu.VMEM((2, FAR_DEV), jnp.int32),
        pltpu.VMEM((1, FAR_DEV), jnp.int32),
        pltpu.VMEM((FAR_DEV, RMAX), F32),
        pltpu.VMEM((3, SLOTS, BS), F32),
        pltpu.VMEM((3 * BLK_DEV, BS), F32),
        pltpu.VMEM((BLK_DEV, 3, BS, 128), F32),
        pltpu.VMEM((NEAR_DEV, 2, BS, BS), BF16),
        pltpu.VMEM((COLUMN, 8, width), F32),
        pltpu.VMEM((ROWS, width), BF16),
        pltpu.VMEM((width, ROWS), BF16),
        pltpu.VMEM((FAR_DEV, FACT), F32),
        pltpu.VMEM((BLK_DEV, FACT), F32),
        pltpu.VMEM((2, ROWS, 128), F32),
        pltpu.VMEM((2, COLUMN, FAR_DEV + EXTRA, 128), F32),
        pltpu.VMEM((2, COLUMN, FAR_DEV + EXTRA, 128), F32),
        pltpu.VMEM((2, 2, FAR_DEV, 128), F32),
        pltpu.VMEM((2, COLUMN, FAR_DEV, 128), F32),
        pltpu.VMEM((2, ROWS, 128), F32),
        pltpu.VMEM((2, ROWS, 128), F32),
        pltpu.VMEM((2, SLOTS, BS), F32),
        pltpu.VMEM((2, SLOTS, BS), F32),
        pltpu.VMEM((2, N_X, BLK_DEV, BS), F32),
        pltpu.VMEM((2, COLUMN, BLK_DEV, BS), F32),
        pltpu.VMEM((2 * NEAR_DEV, BS), F32),
        pltpu.VMEM((2, 3, BLK_DEV, BS), F32),
        pltpu.VMEM((ROWS, 128), F32),
        pltpu.SemaphoreType.DMA((9,)),
        pltpu.SemaphoreType.DMA((10,)),
        pltpu.SemaphoreType.DMA((2, 18)),
        pltpu.SemaphoreType.DMA((2,)),
    ]
    solution, norm = pl.pallas_call(
        kernel,
        out_shape=(
            jax.ShapeDtypeStruct((16, 128), F32),
            jax.ShapeDtypeStruct((1, 1), F32),
        ),
        in_specs=[smem] + [hbm] * 9,
        out_specs=(vmem, vmem),
        scratch_shapes=scratch,
        compiler_params=pltpu.CompilerParams(
            collective_id=0, has_side_effects=True, vmem_limit_bytes=60 * 1024 * 1024
        ),
        cost_estimate=pl.CostEstimate(flops=100_000_000, bytes_accessed=2_000_000, transcendentals=2_000_000),
        name="gmres",
    )(
        near_pairs, right_side.reshape(16, 128), coords, diagonal.reshape(16, 128), near_pairs,
        far_pairs, far_rank.reshape(1, FAR_DEV), far_scale, far_left.reshape(FACT, BS),
        far_right.reshape(FACT, BS),
    )
    return solution.reshape(BLK_DEV * BS), norm.reshape(())


def solution(mesh):
    placed = (
        P("patch"),
        P(None, "patch"),
        P("patch"),
        P(None, ("patch", "pair")),
        P(None, ("patch", "pair")),
        P(("patch", "pair")),
        P(("patch", "pair"), None, None),
        P(("patch", "pair"), None, None),
        P(("patch", "pair"), None),
    )
    return jax.shard_map(
        body, mesh=mesh, in_specs=placed, out_specs=(P("patch"), P()), check_vma=False
    )
```

```python
import functools

import jax
import jax.numpy as jnp
from jax import lax
from jax.experimental import pallas as pl
from jax.experimental.pallas import tpu as pltpu
from jax.sharding import PartitionSpec as P

BS = 256
BLK_DEV = 8
RIM = 4
RMAX = 32
NEAR_DEV = 16
FAR_DEV = 32
NEAR_GAIN = 2.0
SOFT_SQ = 0.25

N_Y, N_Z, N_X = 8, 8, 4
N_YZ = N_Y * N_Z
ROWS = 4 * N_YZ
COLUMN = 2 * N_X
SLOTS = BLK_DEV + 2 * RIM
FACT = FAR_DEV * RMAX
EXTRA = 8

MESH = pl.DeviceIdType.MESH
HIGH = lax.Precision.HIGHEST
F32 = jnp.float32
BF16 = jnp.bfloat16


def place():
    patch = lax.axis_index("patch")
    return lax.axis_index("pair"), patch // (2 * N_Z), (patch // 2) % N_Z, patch % 2


def device(x, y, z, core):
    return {"patch": (y * N_Z + z) * 2 + core, "pair": x}


def send(src, dst, send_sem, recv_sem, to):
    return pltpu.make_async_remote_copy(
        src_ref=src, dst_ref=dst, send_sem=send_sem, recv_sem=recv_sem, device_id=to, device_id_type=MESH
    )


def far_first(n):
    return sorted(range(n), key=lambda d: -min(d, n - d))


def parts(value, count):
    found = []
    for _ in range(count):
        found.append(value.astype(BF16))
        value = value - found[-1].astype(F32)
    return found


def split(value):
    return jnp.concatenate(parts(value, 2), axis=0)


def dot(a, b):
    return jnp.dot(a, b, preferred_element_type=F32)


def dot_rows(a, b):
    return lax.dot_general(a, b, (((1,), (1,)), ((), ())), preferred_element_type=F32)


def fold(value):
    return jnp.sum(value, axis=0, keepdims=True)


def total(value):
    return jnp.sum(fold(value), axis=1, keepdims=True)


def kernel(
    near_smem, right_hbm, coords_hbm, diag_hbm, near_hbm, far_hbm, rank_hbm, scale_hbm, left_hbm, factor_hbm,
    out_ref, norm_ref,
    left, right, left_t, right_t, right_ref, coords_ref, diag_ref, near_ref, far_ref, rank_ref, scale_ref,
    hc, hct, cbc, tiles, keys, hot, hot_t, weight_d, hit_t,
    quarter, picked, got, given, taken, spread, landed, span, rim, rim_in, joined,
    rows_n, shared, sums_yz,
    local_sem, once_sem, step_sem, sums_sem,
):
    x, y, z, core = place()
    patch = lax.axis_index("patch")
    n_patch = 2 * N_YZ
    first = patch * BLK_DEV
    yz = y * N_Z + z
    me = 2 * x + core
    mine = pl.ds(pl.multiple_of(yz * 4, 4), 4)
    up = {"patch": (patch + 1) % n_patch, "pair": x}
    down = {"patch": (patch + n_patch - 1) % n_patch, "pair": x}
    rims = ([(x + i) % N_X for i in range(N_X)], [x])
    twin = device(x, y, z, 1 - core)
    column = []
    for i in (4, 5, 2, 3, 6, 7, 1):
        other_x, other_core = (x + i // 2) % N_X, (core + i) % 2
        column.append((2 * other_x + other_core, other_x % 2, device(other_x, y, z, other_core)))

    joins = ([device((x + i) % N_X, y, z, core) for i in (2, 1, 3)], [to for _, _, to in column])

    barrier = pltpu.get_barrier_semaphore()

    z_peers = [((z + d) % N_Z, d) for d in far_first(N_Z)]

    def over_plane(act, begin=0, end=N_Y):
        def rows(k, _):
            other_y = (y + N_Y // 2 + ((k + 1) // 2) * (1 - 2 * (k % 2))) % N_Y
            for other_z, _ in z_peers:
                act(other_y, other_z)
            return 0

        lax.fori_loop(begin, min(end, N_Y - 1), rows, 0)
        if end == N_Y:
            for other_z, d in z_peers:
                if d:
                    act(y, other_z)

    def greet(other_y, other_z):
        pl.semaphore_signal(
            barrier, inc=1, device_id=device(x, other_y, other_z, core), device_id_type=MESH
        )

    over_plane(greet)
    for _, _, to in column:
        pl.semaphore_signal(barrier, inc=1, device_id=to, device_id_type=MESH)
    for other in rims[0]:
        for to in (up, down):
            pl.semaphore_signal(
                barrier, inc=1, device_id={"patch": to["patch"], "pair": other}, device_id_type=MESH
            )
    loads = [
        pltpu.make_async_copy(src, dst, local_sem.at[i])
        for i, (src, dst) in enumerate(
            (
                (left_hbm, left), (factor_hbm, right), (right_hbm, right_ref), (coords_hbm, coords_ref),
                (diag_hbm, diag_ref), (near_hbm, near_ref), (far_hbm, far_ref), (rank_hbm, rank_ref),
                (scale_hbm, scale_ref),
            )
        )
    ]
    for load in loads:
        load.start()
    for load in loads:
        load.wait()

    def natural(ref):
        return jnp.concatenate([ref[pl.ds(h, BLK_DEV, stride=2), :] for h in range(2)], axis=1)

    def own_quarter(value):
        found = value[:4, :128]
        for q in range(1, N_X):
            a, h = q // 2, q % 2
            found = jnp.where(x == q, value[4 * a : 4 * a + 4, 128 * h : 128 * h + 128], found)
        return found

    b_own = natural(right_ref)
    diag = natural(diag_ref)
    span[0, RIM : RIM + BLK_DEV, :] = b_own
    shared[core, 0] = b_own
    shared[core, 1] = diag
    quarter[0, mine, :] = own_quarter(b_own)
    for d in range(3):
        for b in range(BLK_DEV):
            hc[d, RIM + b : RIM + b + 1, :] = coords_ref[d : d + 1, b * BS : (b + 1) * BS]

    near_f = near_ref[...].astype(F32)
    far_f = far_ref[...].astype(F32)
    sub_key = lax.broadcasted_iota(jnp.int32, (FAR_DEV, COLUMN * FAR_DEV), 0)
    lane_key = lax.broadcasted_iota(jnp.int32, (FAR_DEV, COLUMN * FAR_DEV), 1)
    pick = (lane_key == sub_key + me * FAR_DEV).astype(F32)
    laid = jnp.dot(far_f, pick, precision=HIGH, preferred_element_type=F32)
    keys[me] = jnp.broadcast_to(laid[0:1], (8, COLUMN * FAR_DEV))

    pair_of = lax.broadcasted_iota(jnp.int32, (FAR_DEV, FACT), 1) // RMAX
    term_of = lax.broadcasted_iota(jnp.int32, (FAR_DEV, FACT), 1) % RMAX
    sub = lax.broadcasted_iota(jnp.int32, (FAR_DEV, FACT), 0)
    eye = lax.broadcasted_iota(jnp.int32, (FAR_DEV, FAR_DEV), 0) == lax.broadcasted_iota(
        jnp.int32, (FAR_DEV, FAR_DEV), 1
    )
    rank_col = jnp.sum(jnp.where(eye, rank_ref[...].astype(F32), 0.0), axis=1, keepdims=True)
    term = lax.broadcasted_iota(jnp.int32, (FAR_DEV, RMAX), 1).astype(F32)
    weights = jnp.where(term < rank_col, scale_ref[...], 0.0)
    spread_w = jnp.dot(weights, (sub == term_of).astype(F32), precision=HIGH, preferred_element_type=F32)
    weight_d[...] = jnp.where(sub == pair_of, spread_w, 0.0)
    target_row = far_ref[1:2, :] - first
    onto = (lax.broadcasted_iota(jnp.int32, (BLK_DEV, FAR_DEV), 0) == target_row).astype(F32)
    hit_t[...] = jnp.dot(onto, (sub == pair_of).astype(F32), preferred_element_type=F32)

    def wait_for(view, sem, sent):
        copy = send(view, view, sem, sem, twin)
        if sent:
            copy.wait_send()
        else:
            copy.wait_recv()

    def plane(step, sems, begin=0, end=N_Y):
        def each(other_y, other_z):
            src, dst = step(other_y * N_Z + other_z)
            send(src, dst, sems[0], sems[1], device(x, other_y, other_z, core)).start()

        over_plane(each, begin, end)

    def give(it, own_value):
        back = dot(split(own_value), left_t[...])
        back = fold(hit_t[...] * (back[:BLK_DEV] + back[BLK_DEV:]))
        to_far = dot(split(weight_d[...] * back), right[...])
        to_far = to_far[:FAR_DEV] + to_far[FAR_DEV:]
        for h in range(2):
            given[it, h] = to_far[:, 128 * h : 128 * h + 128]
        taken[it, me] = given[it, x % 2]

    def give_start(it):
        for number, half, to in column:
            send(given.at[it, half], taken.at[it, me], step_sem.at[it, 0], step_sem.at[it, 1], to).start()

    def gather_start(it, begin, end):
        own_rows = quarter.at[it, mine]
        plane(lambda there: (own_rows, own_rows), (step_sem.at[it, 2], step_sem.at[it, 3]), begin, end)

    def span_start(it):
        send(
            span.at[it, pl.ds(BLK_DEV, RIM)], span.at[it, pl.ds(0, RIM)],
            step_sem.at[it, 4], step_sem.at[it, 5], up,
        ).start()
        send(
            span.at[it, pl.ds(RIM, RIM)], span.at[it, pl.ds(RIM + BLK_DEV, RIM)],
            step_sem.at[it, 6], step_sem.at[it, 7], down,
        ).start()

    def scatter_plane(it):
        wait_for(taken.at[it, pl.ds(0, COLUMN - 1)], step_sem.at[it, 1], False)
        value = 0.0
        for part in parts(taken[it].reshape(COLUMN * FAR_DEV, 128), 2):
            value = value + dot(hot[...], part)
        spread[it] = value
        landed[it, mine, :] = spread[it, mine, :]
        plane(
            lambda there: (spread.at[it, pl.ds(pl.multiple_of(there * 4, 4), 4)], landed.at[it, mine]),
            (step_sem.at[it, 8], step_sem.at[it, 9]),
        )

    def gather_column(it, extras):
        wait_for(quarter.at[it, pl.ds(0, ROWS - 4)], step_sem.at[it, 3], False)
        value = 0.0
        for part in parts(quarter[it], 2):
            value = value + dot(hot_t[...], part)
        picked[it, :, pl.ds(0, FAR_DEV), :] = value.reshape(COLUMN, FAR_DEV, 128)
        sums = [fold(quarter[i] * quarter[j]) for i, j in extras]
        sums = jnp.concatenate(sums + [jnp.zeros((EXTRA - len(sums), 128), F32)], axis=0)
        for g in range(COLUMN):
            picked[it, g, pl.ds(FAR_DEV, EXTRA), :] = sums
        got[it, me] = picked[it, me]
        for number, half, to in column:
            send(picked.at[it, number], got.at[it, me], step_sem.at[it, 10], step_sem.at[it, 11], to).start()

    def gather_end(it):
        wait_for(got.at[it, pl.ds(0, COLUMN - 1)], step_sem.at[it, 11], False)
        halves = []
        for h in range(2):
            at = 2 * h
            halves.append((got[it, at] + got[it, at + 1]) + (got[it, at + 4] + got[it, at + 5]))
        sums = jnp.sum(halves[0][FAR_DEV:] + halves[1][FAR_DEV:], axis=1, keepdims=True)
        far_v = split(jnp.concatenate([half[:FAR_DEV] for half in halves], axis=1))
        coef = dot(far_v, right_t[...])
        coef = fold(weight_d[...] * (coef[:FAR_DEV] + coef[FAR_DEV:]))
        to_own = dot(split(hit_t[...] * coef), left[...])
        return to_own[:BLK_DEV] + to_own[BLK_DEV:], sums

    def near(it):
        wait_for(span.at[it, pl.ds(0, RIM)], step_sem.at[it, 5], False)
        wait_for(span.at[it, pl.ds(0, RIM)], step_sem.at[it, 7], False)
        vectors = []
        for way in range(2):
            rows = [
                span[it, pl.ds(jnp.clip(near_smem[way, k] - first + RIM, 0, SLOTS - 1), 1), :]
                for k in range(NEAR_DEV)
            ]
            vectors.append(split(jnp.concatenate(rows, axis=0)))
        for k in range(NEAR_DEV):
            for way, multiply in enumerate((dot_rows, dot)):
                image = multiply(vectors[way], tiles[k, 0]) + multiply(vectors[way], tiles[k, 1])
                at = way * NEAR_DEV + k
                rows_n[at : at + 1, :] = image[k : k + 1] + image[NEAR_DEV + k : NEAR_DEV + k + 1]
        slot = lax.broadcasted_iota(jnp.int32, (SLOTS, NEAR_DEV), 0)
        hits = [(slot == near_ref[way : way + 1, :] - first + RIM).astype(F32) for way in (1, 0)]
        hits = jnp.concatenate(hits, axis=1).astype(BF16)
        value = 0.0
        for part in parts(rows_n[...], 3):
            value = value + dot(hits, part)
        rim[it] = value
        for other in rims[it]:
            send(
                rim.at[it, pl.ds(0, RIM)], rim_in.at[it, x, pl.ds(RIM, RIM)],
                step_sem.at[it, 12], step_sem.at[it, 13], {"patch": down["patch"], "pair": other},
            ).start()
            send(
                rim.at[it, pl.ds(RIM + BLK_DEV, RIM)], rim_in.at[it, x, pl.ds(0, RIM)],
                step_sem.at[it, 14], step_sem.at[it, 15], {"patch": up["patch"], "pair": other},
            ).start()

    def rim_wait(it, at, sent):
        wait_for(rim.at[it, pl.ds(0, RIM * len(rims[it]))], step_sem.at[it, at], sent)

    def join(it, far_own):
        local = far_own + rim[it, RIM : RIM + BLK_DEV, :]
        if len(rims[it]) == 1:
            rim_wait(it, 13, False)
            rim_wait(it, 15, False)
            local = local + rim_in[it, x]
        wait_for(landed.at[it, pl.ds(0, ROWS - 4)], step_sem.at[it, 9], False)
        image = jnp.sum(landed[it].reshape(ROWS // 8, 8, 128), axis=0)
        image = image[:4] + image[4:]
        image = jnp.concatenate([image, image], axis=0)
        image = jnp.concatenate([image, image], axis=1)
        at_row = lax.broadcasted_iota(jnp.int32, (BLK_DEV, BS), 0) // 4
        at_half = lax.broadcasted_iota(jnp.int32, (BLK_DEV, BS), 1) // 128
        joined[it, me] = local + jnp.where(2 * at_row + at_half == x, image, 0.0)
        for to in joins[it]:
            send(joined.at[it, me], joined.at[it, me], step_sem.at[it, 16], step_sem.at[it, 17], to).start()
        wait_for(joined.at[it, pl.ds(0, len(joins[it]))], step_sem.at[it, 17], False)

    def pair_sum(it, c):
        return (joined[it, c] + joined[it, 2 + c]) + (joined[it, 4 + c] + joined[it, 6 + c])

    def sent(it):
        wait_for(taken.at[it, pl.ds(0, COLUMN - 1)], step_sem.at[it, 0], True)
        wait_for(quarter.at[it, pl.ds(0, ROWS - 4)], step_sem.at[it, 2], True)
        wait_for(span.at[it, pl.ds(0, RIM)], step_sem.at[it, 4], True)
        wait_for(span.at[it, pl.ds(0, RIM)], step_sem.at[it, 6], True)
        wait_for(landed.at[it, pl.ds(0, ROWS - 4)], step_sem.at[it, 8], True)
        wait_for(got.at[it, pl.ds(0, COLUMN - 1)], step_sem.at[it, 10], True)
        rim_wait(it, 12, True)
        rim_wait(it, 14, True)
        wait_for(joined.at[it, pl.ds(0, len(joins[it]))], step_sem.at[it, 16], True)

    def build(k, _):
        source = jnp.clip(near_smem[0, k] - first + RIM, 0, SLOTS - 1)
        target = jnp.clip(near_smem[1, k] - first, 0, BLK_DEV - 1)
        line = [hc[d, pl.ds(source, 1), :] for d in range(3)]
        for r in range(0, BS, 64):
            col = [cbc[target, d, r : r + 64, :] for d in range(3)]
            for h in range(2):
                dist = SOFT_SQ
                for d in range(3):
                    diff = col[d] - line[d][:, 128 * h : 128 * h + 128]
                    dist = dist + diff * diff
                tile = (NEAR_GAIN / BS) * lax.rsqrt(dist)
                high = tile.astype(BF16)
                tiles[k, 0, r : r + 64, 128 * h : 128 * h + 128] = high
                tiles[k, 1, r : r + 64, 128 * h : 128 * h + 128] = (tile - high.astype(F32)).astype(BF16)
        return 0

    left_t[...] = left[...].T
    right_t[...] = right[...].T
    give(0, b_own)
    for d in range(3):
        hct[pl.ds(BLK_DEV * d, BLK_DEV), :] = hc[d, RIM : RIM + BLK_DEV, :]
    turned = hct[...].T
    for b in range(BLK_DEV):
        for d in range(3):
            at = BLK_DEV * d + b
            cbc[b, d] = jnp.broadcast_to(turned[:, at : at + 1], (BS, 128))
    pl.semaphore_wait(barrier, N_YZ - 1 + COLUMN - 1 + 2 * N_X)

    gather_start(0, 0, 1)
    for number, half, to in column:
        send(keys.at[me], keys.at[me], once_sem.at[0], once_sem.at[1], to).start()
    give_start(0)
    halo_up = send(hc.at[:, pl.ds(BLK_DEV, RIM)], hc.at[:, pl.ds(0, RIM)], once_sem.at[2], once_sem.at[3], up)
    halo_down = send(
        hc.at[:, pl.ds(RIM, RIM)], hc.at[:, pl.ds(RIM + BLK_DEV, RIM)], once_sem.at[4], once_sem.at[5], down
    )
    halo_up.start()
    halo_down.start()
    gather_start(0, 1, N_Y)
    span_start(0)
    constants = shared.at[core, pl.ds(0, 2)]
    send(constants, constants, once_sem.at[6], once_sem.at[7], twin).start()
    halo_up.wait_recv()
    halo_down.wait_recv()
    lax.fori_loop(0, 8, build, 0)
    wait_for(keys.at[pl.ds(0, COLUMN - 1)], once_sem.at[1], False)
    key = keys[0]
    for g in range(1, COLUMN):
        key = key + keys[g]
    key = (key[0:1] + 0.5).astype(jnp.int32)
    row = lax.broadcasted_iota(jnp.int32, (ROWS, COLUMN * FAR_DEV), 0)
    block = (row // 4) * 16 + core * 8 + (x // 2) * 4 + row % 4
    hits = (block == key).astype(F32)
    hot[...] = hits.astype(BF16)
    hot_t[...] = hits.T.astype(BF16)
    scatter_plane(0)

    lax.fori_loop(8, 14, build, 0)
    gather_column(0, ((0, 0),))
    lax.fori_loop(14, NEAR_DEV, build, 0)
    near(0)
    far_own, sums = gather_end(0)
    beta = jnp.sqrt(sums[0:1])
    inv_beta = 1.0 / beta
    join(0, far_own)
    rim_wait(0, 13, False)
    rim_wait(0, 15, False)
    from_rims = (rim_in[0, 0] + rim_in[0, 1]) + (rim_in[0, 2] + rim_in[0, 3])
    w_own = (pair_sum(0, core) + from_rims + diag * b_own) * inv_beta

    span[1, RIM : RIM + BLK_DEV, :] = w_own
    quarter[1, mine, :] = own_quarter(w_own)
    gather_start(1, 0, 1)
    give(1, w_own)
    give_start(1)
    gather_start(1, 1, N_Y)
    span_start(1)
    shared[core, 2] = w_own
    krylov = shared.at[core, pl.ds(2, 1)]
    send(krylov, krylov, once_sem.at[8], once_sem.at[9], twin).start()
    wait_for(constants, once_sem.at[6], True)
    wait_for(keys.at[pl.ds(0, COLUMN - 1)], once_sem.at[0], True)
    halo_up.wait_send()
    halo_down.wait_send()
    sent(0)
    scatter_plane(1)
    near(1)
    gather_column(1, ((0, 1), (1, 1)))
    far_own, sums = gather_end(1)
    h00 = sums[0:1] * inv_beta
    shift = sums[1:2] - h00 * h00
    alpha = h00 * inv_beta
    wait_for(constants, once_sem.at[7], False)
    wait_for(krylov, once_sem.at[9], False)
    wait_for(krylov, once_sem.at[8], True)
    v0 = shared[:, 0] * inv_beta
    w = shared[:, 2]
    u = w - h00 * v0
    known = shared[:, 1] * w - h00 * w - shift * v0 - h00 * u
    join(1, far_own)
    rest = jnp.stack([pair_sum(1, c) for c in range(2)]) + known

    def lanes(value):
        value = fold(value.reshape(2 * BLK_DEV, BS))
        return value[:, :128] + value[:, 128:]

    sums_yz[mine, :] = jnp.concatenate(
        [lanes(rest * rest), lanes(rest * v0), lanes(rest * u), lanes(u * u)], axis=0
    )
    own_sums = sums_yz.at[mine]
    plane(lambda there: (own_sums, own_sums), (sums_sem.at[0], sums_sem.at[1]))
    sent(1)
    wait_for(sums_yz.at[pl.ds(0, ROWS - 4)], sums_sem.at[1], False)
    wait_for(sums_yz.at[pl.ds(0, ROWS - 4)], sums_sem.at[0], True)
    acc = jnp.sum(sums_yz[...].reshape(ROWS // 8, 8, 128), axis=0)
    acc = jnp.sum(acc[:4] + acc[4:], axis=1, keepdims=True)
    sq, a0, a1, uu = acc[0:1], acc[1:2], acc[2:3], acc[3:4]
    h10 = jnp.sqrt(uu)
    inv_h10 = 1.0 / h10
    a1 = a1 * inv_h10
    h01 = (shift + a0) * inv_h10
    h11 = h00 + a1 * inv_h10
    h21 = jnp.sqrt(jnp.maximum(sq - a0 * a0 - a1 * a1, 0.0)) * inv_h10

    rho0 = jnp.sqrt(h00 * h00 + h10 * h10)
    c0 = h00 / rho0
    s0 = h10 / rho0
    r01 = c0 * h01 + s0 * h11
    r11 = c0 * h11 - s0 * h01
    rho1 = jnp.sqrt(r11 * r11 + h21 * h21)
    c1 = r11 / rho1
    s1 = h21 / rho1
    g0 = c0 * beta
    g1 = -s0 * beta
    y1 = c1 * g1 / rho1
    y0 = (g0 - r01 * y1) / rho0
    norm_ref[...] = jnp.abs(s1 * g1)
    u_own = w_own - alpha * b_own
    answer = (y0 * inv_beta) * b_own + (y1 * inv_h10) * u_own
    for h in range(2):
        out_ref[pl.ds(h, BLK_DEV, stride=2), :] = answer[:, 128 * h : 128 * h + 128]


def body(
    right_side, coords, diagonal, near_pairs, far_pairs, far_rank, far_left, far_right, far_scale
):
    vmem = pl.BlockSpec(memory_space=pltpu.VMEM)
    smem = pl.BlockSpec(memory_space=pltpu.SMEM)
    hbm = pl.BlockSpec(memory_space=pltpu.HBM)
    width = COLUMN * FAR_DEV
    scratch = [
        pltpu.VMEM((FACT, BS), BF16),
        pltpu.VMEM((FACT, BS), BF16),
        pltpu.VMEM((BS, FACT), BF16),
        pltpu.VMEM((BS, FACT), BF16),
        pltpu.VMEM((16, 128), F32),
        pltpu.VMEM((3, BLK_DEV * BS), F32),
        pltpu.VMEM((16, 128), F32),
        pltpu.VMEM((2, NEAR_DEV), jnp.int32),
        pltpu.VMEM((2, FAR_DEV), jnp.int32),
        pltpu.VMEM((1, FAR_DEV), jnp.int32),
        pltpu.VMEM((FAR_DEV, RMAX), F32),
        pltpu.VMEM((3, SLOTS, BS), F32),
        pltpu.VMEM((3 * BLK_DEV, BS), F32),
        pltpu.VMEM((BLK_DEV, 3, BS, 128), F32),
        pltpu.VMEM((NEAR_DEV, 2, BS, BS), BF16),
        pltpu.VMEM((COLUMN, 8, width), F32),
        pltpu.VMEM((ROWS, width), BF16),
        pltpu.VMEM((width, ROWS), BF16),
        pltpu.VMEM((FAR_DEV, FACT), F32),
        pltpu.VMEM((BLK_DEV, FACT), F32),
        pltpu.VMEM((2, ROWS, 128), F32),
        pltpu.VMEM((2, COLUMN, FAR_DEV + EXTRA, 128), F32),
        pltpu.VMEM((2, COLUMN, FAR_DEV + EXTRA, 128), F32),
        pltpu.VMEM((2, 2, FAR_DEV, 128), F32),
        pltpu.VMEM((2, COLUMN, FAR_DEV, 128), F32),
        pltpu.VMEM((2, ROWS, 128), F32),
        pltpu.VMEM((2, ROWS, 128), F32),
        pltpu.VMEM((2, SLOTS, BS), F32),
        pltpu.VMEM((2, SLOTS, BS), F32),
        pltpu.VMEM((2, N_X, BLK_DEV, BS), F32),
        pltpu.VMEM((2, COLUMN, BLK_DEV, BS), F32),
        pltpu.VMEM((2 * NEAR_DEV, BS), F32),
        pltpu.VMEM((2, 3, BLK_DEV, BS), F32),
        pltpu.VMEM((ROWS, 128), F32),
        pltpu.SemaphoreType.DMA((9,)),
        pltpu.SemaphoreType.DMA((10,)),
        pltpu.SemaphoreType.DMA((2, 18)),
        pltpu.SemaphoreType.DMA((2,)),
    ]
    solution, norm = pl.pallas_call(
        kernel,
        out_shape=(
            jax.ShapeDtypeStruct((16, 128), F32),
            jax.ShapeDtypeStruct((1, 1), F32),
        ),
        in_specs=[smem] + [hbm] * 9,
        out_specs=(vmem, vmem),
        scratch_shapes=scratch,
        compiler_params=pltpu.CompilerParams(
            collective_id=0, has_side_effects=True, vmem_limit_bytes=60 * 1024 * 1024
        ),
        cost_estimate=pl.CostEstimate(flops=100_000_000, bytes_accessed=2_000_000, transcendentals=2_000_000),
        name="gmres",
    )(
        near_pairs, right_side.reshape(16, 128), coords, diagonal.reshape(16, 128), near_pairs,
        far_pairs, far_rank.reshape(1, FAR_DEV), far_scale, far_left.reshape(FACT, BS),
        far_right.reshape(FACT, BS),
    )
    return solution.reshape(BLK_DEV * BS), norm.reshape(())


def solution(mesh):
    placed = (
        P("patch"),
        P(None, "patch"),
        P("patch"),
        P(None, ("patch", "pair")),
        P(None, ("patch", "pair")),
        P(("patch", "pair")),
        P(("patch", "pair"), None, None),
        P(("patch", "pair"), None, None),
        P(("patch", "pair"), None),
    )
    return jax.shard_map(
        body, mesh=mesh, in_specs=placed, out_specs=(P("patch"), P()), check_vma=False
    )
```

```python
import functools

import jax
import jax.numpy as jnp
from jax import lax
from jax.experimental import pallas as pl
from jax.experimental.pallas import tpu as pltpu
from jax.sharding import PartitionSpec as P

BS = 256
BLK_DEV = 8
RIM = 4
RMAX = 32
NEAR_DEV = 16
FAR_DEV = 32
NEAR_GAIN = 2.0
SOFT_SQ = 0.25

N_Y, N_Z, N_X = 8, 8, 4
N_YZ = N_Y * N_Z
ROWS = 4 * N_YZ
COLUMN = 2 * N_X
SLOTS = BLK_DEV + 2 * RIM
FACT = FAR_DEV * RMAX
EXTRA = 8

MESH = pl.DeviceIdType.MESH
HIGH = lax.Precision.HIGHEST
F32 = jnp.float32
BF16 = jnp.bfloat16


def place():
    patch = lax.axis_index("patch")
    return lax.axis_index("pair"), patch // (2 * N_Z), (patch // 2) % N_Z, patch % 2


def device(x, y, z, core):
    return {"patch": (y * N_Z + z) * 2 + core, "pair": x}


def send(src, dst, send_sem, recv_sem, to):
    return pltpu.make_async_remote_copy(
        src_ref=src, dst_ref=dst, send_sem=send_sem, recv_sem=recv_sem, device_id=to, device_id_type=MESH
    )


def far_first(n):
    return sorted(range(n), key=lambda d: -min(d, n - d))


def parts(value, count):
    found = []
    for _ in range(count):
        found.append(value.astype(BF16))
        value = value - found[-1].astype(F32)
    return found


def split(value):
    return jnp.concatenate(parts(value, 2), axis=0)


def dot(a, b):
    return jnp.dot(a, b, preferred_element_type=F32)


def dot_rows(a, b):
    return lax.dot_general(a, b, (((1,), (1,)), ((), ())), preferred_element_type=F32)


def fold(value):
    return jnp.sum(value, axis=0, keepdims=True)


def total(value):
    return jnp.sum(fold(value), axis=1, keepdims=True)


def kernel(
    near_smem, right_hbm, coords_hbm, diag_hbm, near_hbm, far_hbm, rank_hbm, scale_hbm, left_hbm, factor_hbm,
    out_ref, norm_ref,
    left, right, left_t, right_t, right_ref, coords_ref, diag_ref, near_ref, far_ref, rank_ref, scale_ref,
    hc, hct, cbc, tiles, keys, hot, hot_t, weight_d, hit_t,
    quarter, picked, got, given, taken, spread, landed, span, rim, rim_in, joined,
    rows_n, shared, sums_yz,
    local_sem, once_sem, step_sem, sums_sem,
):
    x, y, z, core = place()
    patch = lax.axis_index("patch")
    n_patch = 2 * N_YZ
    first = patch * BLK_DEV
    yz = y * N_Z + z
    me = 2 * x + core
    mine = pl.ds(pl.multiple_of(yz * 4, 4), 4)
    up = {"patch": (patch + 1) % n_patch, "pair": x}
    down = {"patch": (patch + n_patch - 1) % n_patch, "pair": x}
    rims = ([(x + i) % N_X for i in range(N_X)], [x])
    twin = device(x, y, z, 1 - core)
    column = []
    for i in (4, 5, 2, 3, 6, 7, 1):
        other_x, other_core = (x + i // 2) % N_X, (core + i) % 2
        column.append((2 * other_x + other_core, other_x % 2, device(other_x, y, z, other_core)))

    joins = ([device((x + i) % N_X, y, z, core) for i in (2, 1, 3)], [to for _, _, to in column])

    barrier = pltpu.get_barrier_semaphore()

    z_peers = [((z + d) % N_Z, d) for d in far_first(N_Z)]

    def over_plane(act, begin=0, end=N_Y):
        def rows(k, _):
            other_y = (y + N_Y // 2 + ((k + 1) // 2) * (1 - 2 * (k % 2))) % N_Y
            for other_z, _ in z_peers:
                act(other_y, other_z)
            return 0

        lax.fori_loop(begin, min(end, N_Y - 1), rows, 0)
        if end == N_Y:
            for other_z, d in z_peers:
                if d:
                    act(y, other_z)

    def greet(other_y, other_z):
        pl.semaphore_signal(
            barrier, inc=1, device_id=device(x, other_y, other_z, core), device_id_type=MESH
        )

    over_plane(greet)
    for _, _, to in column:
        pl.semaphore_signal(barrier, inc=1, device_id=to, device_id_type=MESH)
    for other in rims[0]:
        for to in (up, down):
            pl.semaphore_signal(
                barrier, inc=1, device_id={"patch": to["patch"], "pair": other}, device_id_type=MESH
            )
    loads = [
        pltpu.make_async_copy(src, dst, local_sem.at[i])
        for i, (src, dst) in enumerate(
            (
                (left_hbm, left), (factor_hbm, right), (right_hbm, right_ref), (coords_hbm, coords_ref),
                (diag_hbm, diag_ref), (near_hbm, near_ref), (far_hbm, far_ref), (rank_hbm, rank_ref),
                (scale_hbm, scale_ref),
            )
        )
    ]
    for load in loads:
        load.start()
    for load in loads:
        load.wait()

    def natural(ref):
        return jnp.concatenate([ref[pl.ds(h, BLK_DEV, stride=2), :] for h in range(2)], axis=1)

    def own_quarter(value):
        found = value[:4, :128]
        for q in range(1, N_X):
            a, h = q // 2, q % 2
            found = jnp.where(x == q, value[4 * a : 4 * a + 4, 128 * h : 128 * h + 128], found)
        return found

    b_own = natural(right_ref)
    diag = natural(diag_ref)
    span[0, RIM : RIM + BLK_DEV, :] = b_own
    shared[core, 0] = b_own
    shared[core, 1] = diag
    quarter[0, mine, :] = own_quarter(b_own)
    for d in range(3):
        for b in range(BLK_DEV):
            hc[d, RIM + b : RIM + b + 1, :] = coords_ref[d : d + 1, b * BS : (b + 1) * BS]

    near_f = near_ref[...].astype(F32)
    far_f = far_ref[...].astype(F32)
    sub_key = lax.broadcasted_iota(jnp.int32, (FAR_DEV, COLUMN * FAR_DEV), 0)
    lane_key = lax.broadcasted_iota(jnp.int32, (FAR_DEV, COLUMN * FAR_DEV), 1)
    pick = (lane_key == sub_key + me * FAR_DEV).astype(F32)
    laid = jnp.dot(far_f, pick, precision=HIGH, preferred_element_type=F32)
    keys[me] = laid[0:1]

    pair_of = lax.broadcasted_iota(jnp.int32, (FAR_DEV, FACT), 1) // RMAX
    term_of = lax.broadcasted_iota(jnp.int32, (FAR_DEV, FACT), 1) % RMAX
    sub = lax.broadcasted_iota(jnp.int32, (FAR_DEV, FACT), 0)
    eye = lax.broadcasted_iota(jnp.int32, (FAR_DEV, FAR_DEV), 0) == lax.broadcasted_iota(
        jnp.int32, (FAR_DEV, FAR_DEV), 1
    )
    rank_col = jnp.sum(jnp.where(eye, rank_ref[...].astype(F32), 0.0), axis=1, keepdims=True)
    term = lax.broadcasted_iota(jnp.int32, (FAR_DEV, RMAX), 1).astype(F32)
    weights = jnp.where(term < rank_col, scale_ref[...], 0.0)
    spread_w = jnp.dot(weights, (sub == term_of).astype(F32), precision=HIGH, preferred_element_type=F32)
    weight_d[...] = jnp.where(sub == pair_of, spread_w, 0.0)
    target_row = far_ref[1:2, :] - first
    onto = (lax.broadcasted_iota(jnp.int32, (BLK_DEV, FAR_DEV), 0) == target_row).astype(F32)
    hit_t[...] = jnp.dot(onto, (sub == pair_of).astype(F32), preferred_element_type=F32)

    def wait_for(view, sem, sent):
        copy = send(view, view, sem, sem, twin)
        if sent:
            copy.wait_send()
        else:
            copy.wait_recv()

    def plane(step, sems, begin=0, end=N_Y):
        def each(other_y, other_z):
            src, dst = step(other_y * N_Z + other_z)
            send(src, dst, sems[0], sems[1], device(x, other_y, other_z, core)).start()

        over_plane(each, begin, end)

    def give(it, own_value):
        back = dot(split(own_value), left_t[...])
        back = fold(hit_t[...] * (back[:BLK_DEV] + back[BLK_DEV:]))
        to_far = dot(split(weight_d[...] * back), right[...])
        to_far = to_far[:FAR_DEV] + to_far[FAR_DEV:]
        for h in range(2):
            given[it, h] = to_far[:, 128 * h : 128 * h + 128]
        taken[it, me] = given[it, x % 2]

    def give_start(it):
        for number, half, to in column:
            send(given.at[it, half], taken.at[it, me], step_sem.at[it, 0], step_sem.at[it, 1], to).start()

    def gather_start(it, begin, end):
        own_rows = quarter.at[it, mine]
        plane(lambda there: (own_rows, own_rows), (step_sem.at[it, 2], step_sem.at[it, 3]), begin, end)

    def span_start(it):
        send(
            span.at[it, pl.ds(BLK_DEV, RIM)], span.at[it, pl.ds(0, RIM)],
            step_sem.at[it, 4], step_sem.at[it, 5], up,
        ).start()
        send(
            span.at[it, pl.ds(RIM, RIM)], span.at[it, pl.ds(RIM + BLK_DEV, RIM)],
            step_sem.at[it, 6], step_sem.at[it, 7], down,
        ).start()

    def scatter_plane(it):
        wait_for(taken.at[it, pl.ds(0, COLUMN - 1)], step_sem.at[it, 1], False)
        value = 0.0
        for part in parts(taken[it].reshape(COLUMN * FAR_DEV, 128), 2):
            value = value + dot(hot[...], part)
        spread[it] = value
        landed[it, mine, :] = spread[it, mine, :]
        plane(
            lambda there: (spread.at[it, pl.ds(pl.multiple_of(there * 4, 4), 4)], landed.at[it, mine]),
            (step_sem.at[it, 8], step_sem.at[it, 9]),
        )

    def gather_column(it, extras):
        wait_for(quarter.at[it, pl.ds(0, ROWS - 4)], step_sem.at[it, 3], False)
        value = 0.0
        for part in parts(quarter[it], 2):
            value = value + dot(hot_t[...], part)
        picked[it, :, pl.ds(0, FAR_DEV), :] = value.reshape(COLUMN, FAR_DEV, 128)
        sums = [fold(quarter[i] * quarter[j]) for i, j in extras]
        sums = jnp.concatenate(sums + [jnp.zeros((EXTRA - len(sums), 128), F32)], axis=0)
        for g in range(COLUMN):
            picked[it, g, pl.ds(FAR_DEV, EXTRA), :] = sums
        got[it, me] = picked[it, me]
        for number, half, to in column:
            send(picked.at[it, number], got.at[it, me], step_sem.at[it, 10], step_sem.at[it, 11], to).start()

    def gather_end(it):
        wait_for(got.at[it, pl.ds(0, COLUMN - 1)], step_sem.at[it, 11], False)
        halves = []
        for h in range(2):
            at = 2 * h
            halves.append((got[it, at] + got[it, at + 1]) + (got[it, at + 4] + got[it, at + 5]))
        sums = jnp.sum(halves[0][FAR_DEV:] + halves[1][FAR_DEV:], axis=1, keepdims=True)
        far_v = split(jnp.concatenate([half[:FAR_DEV] for half in halves], axis=1))
        coef = dot(far_v, right_t[...])
        coef = fold(weight_d[...] * (coef[:FAR_DEV] + coef[FAR_DEV:]))
        to_own = dot(split(hit_t[...] * coef), left[...])
        return to_own[:BLK_DEV] + to_own[BLK_DEV:], sums

    def near(it):
        wait_for(span.at[it, pl.ds(0, RIM)], step_sem.at[it, 5], False)
        wait_for(span.at[it, pl.ds(0, RIM)], step_sem.at[it, 7], False)
        vectors = []
        for way in range(2):
            rows = [
                span[it, pl.ds(jnp.clip(near_smem[way, k] - first + RIM, 0, SLOTS - 1), 1), :]
                for k in range(NEAR_DEV)
            ]
            vectors.append(split(jnp.concatenate(rows, axis=0)))
        for k in range(NEAR_DEV):
            for way, multiply in enumerate((dot_rows, dot)):
                image = multiply(vectors[way], tiles[k, 0]) + multiply(vectors[way], tiles[k, 1])
                at = way * NEAR_DEV + k
                rows_n[at : at + 1, :] = image[k : k + 1] + image[NEAR_DEV + k : NEAR_DEV + k + 1]
        slot = lax.broadcasted_iota(jnp.int32, (SLOTS, NEAR_DEV), 0)
        hits = [(slot == near_ref[way : way + 1, :] - first + RIM).astype(F32) for way in (1, 0)]
        hits = jnp.concatenate(hits, axis=1).astype(BF16)
        value = 0.0
        for part in parts(rows_n[...], 3):
            value = value + dot(hits, part)
        rim[it] = value
        for other in rims[it]:
            send(
                rim.at[it, pl.ds(0, RIM)], rim_in.at[it, x, pl.ds(RIM, RIM)],
                step_sem.at[it, 12], step_sem.at[it, 13], {"patch": down["patch"], "pair": other},
            ).start()
            send(
                rim.at[it, pl.ds(RIM + BLK_DEV, RIM)], rim_in.at[it, x, pl.ds(0, RIM)],
                step_sem.at[it, 14], step_sem.at[it, 15], {"patch": up["patch"], "pair": other},
            ).start()

    def rim_wait(it, at, sent):
        wait_for(rim.at[it, pl.ds(0, RIM * len(rims[it]))], step_sem.at[it, at], sent)

    def join(it, far_own):
        local = far_own + rim[it, RIM : RIM + BLK_DEV, :]
        if len(rims[it]) == 1:
            rim_wait(it, 13, False)
            rim_wait(it, 15, False)
            local = local + rim_in[it, x]
        wait_for(landed.at[it, pl.ds(0, ROWS - 4)], step_sem.at[it, 9], False)
        image = jnp.sum(landed[it].reshape(ROWS // 8, 8, 128), axis=0)
        image = image[:4] + image[4:]
        image = jnp.concatenate([image, image], axis=0)
        image = jnp.concatenate([image, image], axis=1)
        at_row = lax.broadcasted_iota(jnp.int32, (BLK_DEV, BS), 0) // 4
        at_half = lax.broadcasted_iota(jnp.int32, (BLK_DEV, BS), 1) // 128
        joined[it, me] = local + jnp.where(2 * at_row + at_half == x, image, 0.0)
        for to in joins[it]:
            send(joined.at[it, me], joined.at[it, me], step_sem.at[it, 16], step_sem.at[it, 17], to).start()
        wait_for(joined.at[it, pl.ds(0, len(joins[it]))], step_sem.at[it, 17], False)

    def pair_sum(it, c):
        return (joined[it, c] + joined[it, 2 + c]) + (joined[it, 4 + c] + joined[it, 6 + c])

    def sent(it):
        wait_for(taken.at[it, pl.ds(0, COLUMN - 1)], step_sem.at[it, 0], True)
        wait_for(quarter.at[it, pl.ds(0, ROWS - 4)], step_sem.at[it, 2], True)
        wait_for(span.at[it, pl.ds(0, RIM)], step_sem.at[it, 4], True)
        wait_for(span.at[it, pl.ds(0, RIM)], step_sem.at[it, 6], True)
        wait_for(landed.at[it, pl.ds(0, ROWS - 4)], step_sem.at[it, 8], True)
        wait_for(got.at[it, pl.ds(0, COLUMN - 1)], step_sem.at[it, 10], True)
        rim_wait(it, 12, True)
        rim_wait(it, 14, True)
        wait_for(joined.at[it, pl.ds(0, len(joins[it]))], step_sem.at[it, 16], True)

    def build(k, _):
        source = jnp.clip(near_smem[0, k] - first + RIM, 0, SLOTS - 1)
        target = jnp.clip(near_smem[1, k] - first, 0, BLK_DEV - 1)
        line = [hc[d, pl.ds(source, 1), :] for d in range(3)]
        for r in range(0, BS, 64):
            col = [cbc[target, d, r : r + 64, :] for d in range(3)]
            for h in range(2):
                dist = SOFT_SQ
                for d in range(3):
                    diff = col[d] - line[d][:, 128 * h : 128 * h + 128]
                    dist = dist + diff * diff
                tile = (NEAR_GAIN / BS) * lax.rsqrt(dist)
                high = tile.astype(BF16)
                tiles[k, 0, r : r + 64, 128 * h : 128 * h + 128] = high
                tiles[k, 1, r : r + 64, 128 * h : 128 * h + 128] = (tile - high.astype(F32)).astype(BF16)
        return 0

    left_t[...] = left[...].T
    right_t[...] = right[...].T
    give(0, b_own)
    for d in range(3):
        hct[pl.ds(BLK_DEV * d, BLK_DEV), :] = hc[d, RIM : RIM + BLK_DEV, :]
    turned = hct[...].T
    for b in range(BLK_DEV):
        for d in range(3):
            at = BLK_DEV * d + b
            cbc[b, d] = jnp.broadcast_to(turned[:, at : at + 1], (BS, 128))
    pl.semaphore_wait(barrier, N_YZ - 1 + COLUMN - 1 + 2 * N_X)

    gather_start(0, 0, 1)
    for number, half, to in column:
        send(keys.at[me], keys.at[me], once_sem.at[0], once_sem.at[1], to).start()
    give_start(0)
    halo_up = send(hc.at[:, pl.ds(BLK_DEV, RIM)], hc.at[:, pl.ds(0, RIM)], once_sem.at[2], once_sem.at[3], up)
    halo_down = send(
        hc.at[:, pl.ds(RIM, RIM)], hc.at[:, pl.ds(RIM + BLK_DEV, RIM)], once_sem.at[4], once_sem.at[5], down
    )
    halo_up.start()
    halo_down.start()
    gather_start(0, 1, N_Y)
    span_start(0)
    constants = shared.at[core, pl.ds(0, 2)]
    send(constants, constants, once_sem.at[6], once_sem.at[7], twin).start()
    halo_up.wait_recv()
    halo_down.wait_recv()
    lax.fori_loop(0, 8, build, 0)
    wait_for(keys.at[pl.ds(0, COLUMN - 1)], once_sem.at[1], False)
    key = keys[0]
    for g in range(1, COLUMN):
        key = key + keys[g]
    key = (key + 0.5).astype(jnp.int32)
    row = lax.broadcasted_iota(jnp.int32, (ROWS, COLUMN * FAR_DEV), 0)
    block = (row // 4) * 16 + core * 8 + (x // 2) * 4 + row % 4
    hits = (block == key).astype(F32)
    hot[...] = hits.astype(BF16)
    scatter_plane(0)
    hot_t[...] = hits.T.astype(BF16)

    lax.fori_loop(8, 14, build, 0)
    gather_column(0, ((0, 0),))
    lax.fori_loop(14, NEAR_DEV, build, 0)
    near(0)
    far_own, sums = gather_end(0)
    beta = jnp.sqrt(sums[0:1])
    inv_beta = 1.0 / beta
    join(0, far_own)
    rim_wait(0, 13, False)
    rim_wait(0, 15, False)
    from_rims = (rim_in[0, 0] + rim_in[0, 1]) + (rim_in[0, 2] + rim_in[0, 3])
    w_own = (pair_sum(0, core) + from_rims + diag * b_own) * inv_beta

    span[1, RIM : RIM + BLK_DEV, :] = w_own
    quarter[1, mine, :] = own_quarter(w_own)
    gather_start(1, 0, 1)
    give(1, w_own)
    give_start(1)
    gather_start(1, 1, N_Y)
    span_start(1)
    shared[core, 2] = w_own
    krylov = shared.at[core, pl.ds(2, 1)]
    send(krylov, krylov, once_sem.at[8], once_sem.at[9], twin).start()
    wait_for(constants, once_sem.at[6], True)
    wait_for(keys.at[pl.ds(0, COLUMN - 1)], once_sem.at[0], True)
    halo_up.wait_send()
    halo_down.wait_send()
    sent(0)
    scatter_plane(1)
    near(1)
    gather_column(1, ((0, 1), (1, 1)))
    far_own, sums = gather_end(1)
    h00 = sums[0:1] * inv_beta
    shift = sums[1:2] - h00 * h00
    alpha = h00 * inv_beta
    wait_for(constants, once_sem.at[7], False)
    wait_for(krylov, once_sem.at[9], False)
    wait_for(krylov, once_sem.at[8], True)
    v0 = shared[:, 0] * inv_beta
    w = shared[:, 2]
    u = w - h00 * v0
    known = shared[:, 1] * w - h00 * w - shift * v0 - h00 * u
    join(1, far_own)
    rest = jnp.stack([pair_sum(1, c) for c in range(2)]) + known

    def lanes(value):
        value = fold(value.reshape(2 * BLK_DEV, BS))
        return value[:, :128] + value[:, 128:]

    sums_yz[mine, :] = jnp.concatenate(
        [lanes(rest * rest), lanes(rest * v0), lanes(rest * u), lanes(u * u)], axis=0
    )
    own_sums = sums_yz.at[mine]
    plane(lambda there: (own_sums, own_sums), (sums_sem.at[0], sums_sem.at[1]))
    sent(1)
    wait_for(sums_yz.at[pl.ds(0, ROWS - 4)], sums_sem.at[1], False)
    wait_for(sums_yz.at[pl.ds(0, ROWS - 4)], sums_sem.at[0], True)
    acc = jnp.sum(sums_yz[...].reshape(ROWS // 8, 8, 128), axis=0)
    acc = jnp.sum(acc[:4] + acc[4:], axis=1, keepdims=True)
    sq, a0, a1, uu = acc[0:1], acc[1:2], acc[2:3], acc[3:4]
    h10 = jnp.sqrt(uu)
    inv_h10 = 1.0 / h10
    a1 = a1 * inv_h10
    h01 = (shift + a0) * inv_h10
    h11 = h00 + a1 * inv_h10
    h21 = jnp.sqrt(jnp.maximum(sq - a0 * a0 - a1 * a1, 0.0)) * inv_h10

    rho0 = jnp.sqrt(h00 * h00 + h10 * h10)
    c0 = h00 / rho0
    s0 = h10 / rho0
    r01 = c0 * h01 + s0 * h11
    r11 = c0 * h11 - s0 * h01
    rho1 = jnp.sqrt(r11 * r11 + h21 * h21)
    c1 = r11 / rho1
    s1 = h21 / rho1
    g0 = c0 * beta
    g1 = -s0 * beta
    y1 = c1 * g1 / rho1
    y0 = (g0 - r01 * y1) / rho0
    norm_ref[...] = jnp.abs(s1 * g1)
    u_own = w_own - alpha * b_own
    answer = (y0 * inv_beta) * b_own + (y1 * inv_h10) * u_own
    for h in range(2):
        out_ref[pl.ds(h, BLK_DEV, stride=2), :] = answer[:, 128 * h : 128 * h + 128]


def body(
    right_side, coords, diagonal, near_pairs, far_pairs, far_rank, far_left, far_right, far_scale
):
    vmem = pl.BlockSpec(memory_space=pltpu.VMEM)
    smem = pl.BlockSpec(memory_space=pltpu.SMEM)
    hbm = pl.BlockSpec(memory_space=pltpu.HBM)
    width = COLUMN * FAR_DEV
    scratch = [
        pltpu.VMEM((FACT, BS), BF16),
        pltpu.VMEM((FACT, BS), BF16),
        pltpu.VMEM((BS, FACT), BF16),
        pltpu.VMEM((BS, FACT), BF16),
        pltpu.VMEM((16, 128), F32),
        pltpu.VMEM((3, BLK_DEV * BS), F32),
        pltpu.VMEM((16, 128), F32),
        pltpu.VMEM((2, NEAR_DEV), jnp.int32),
        pltpu.VMEM((2, FAR_DEV), jnp.int32),
        pltpu.VMEM((1, FAR_DEV), jnp.int32),
        pltpu.VMEM((FAR_DEV, RMAX), F32),
        pltpu.VMEM((3, SLOTS, BS), F32),
        pltpu.VMEM((3 * BLK_DEV, BS), F32),
        pltpu.VMEM((BLK_DEV, 3, BS, 128), F32),
        pltpu.VMEM((NEAR_DEV, 2, BS, BS), BF16),
        pltpu.VMEM((COLUMN, 1, width), F32),
        pltpu.VMEM((ROWS, width), BF16),
        pltpu.VMEM((width, ROWS), BF16),
        pltpu.VMEM((FAR_DEV, FACT), F32),
        pltpu.VMEM((BLK_DEV, FACT), F32),
        pltpu.VMEM((2, ROWS, 128), F32),
        pltpu.VMEM((2, COLUMN, FAR_DEV + EXTRA, 128), F32),
        pltpu.VMEM((2, COLUMN, FAR_DEV + EXTRA, 128), F32),
        pltpu.VMEM((2, 2, FAR_DEV, 128), F32),
        pltpu.VMEM((2, COLUMN, FAR_DEV, 128), F32),
        pltpu.VMEM((2, ROWS, 128), F32),
        pltpu.VMEM((2, ROWS, 128), F32),
        pltpu.VMEM((2, SLOTS, BS), F32),
        pltpu.VMEM((2, SLOTS, BS), F32),
        pltpu.VMEM((2, N_X, BLK_DEV, BS), F32),
        pltpu.VMEM((2, COLUMN, BLK_DEV, BS), F32),
        pltpu.VMEM((2 * NEAR_DEV, BS), F32),
        pltpu.VMEM((2, 3, BLK_DEV, BS), F32),
        pltpu.VMEM((ROWS, 128), F32),
        pltpu.SemaphoreType.DMA((9,)),
        pltpu.SemaphoreType.DMA((10,)),
        pltpu.SemaphoreType.DMA((2, 18)),
        pltpu.SemaphoreType.DMA((2,)),
    ]
    solution, norm = pl.pallas_call(
        kernel,
        out_shape=(
            jax.ShapeDtypeStruct((16, 128), F32),
            jax.ShapeDtypeStruct((1, 1), F32),
        ),
        in_specs=[smem] + [hbm] * 9,
        out_specs=(vmem, vmem),
        scratch_shapes=scratch,
        compiler_params=pltpu.CompilerParams(
            collective_id=0, has_side_effects=True, vmem_limit_bytes=60 * 1024 * 1024
        ),
        cost_estimate=pl.CostEstimate(flops=100_000_000, bytes_accessed=2_000_000, transcendentals=2_000_000),
        name="gmres",
    )(
        near_pairs, right_side.reshape(16, 128), coords, diagonal.reshape(16, 128), near_pairs,
        far_pairs, far_rank.reshape(1, FAR_DEV), far_scale, far_left.reshape(FACT, BS),
        far_right.reshape(FACT, BS),
    )
    return solution.reshape(BLK_DEV * BS), norm.reshape(())


def solution(mesh):
    placed = (
        P("patch"),
        P(None, "patch"),
        P("patch"),
        P(None, ("patch", "pair")),
        P(None, ("patch", "pair")),
        P(("patch", "pair")),
        P(("patch", "pair"), None, None),
        P(("patch", "pair"), None, None),
        P(("patch", "pair"), None),
    )
    return jax.shard_map(
        body, mesh=mesh, in_specs=placed, out_specs=(P("patch"), P()), check_vma=False
    )
```
